32 devices in a mesh: group: 2 (over y), row: 4 (over z), col: 4 (over x, core).
Axes of the slice: x: 2, y: 2, z: 4, core: 2. Of those that a mesh axis runs over, the one named last changes fastest.
Arguments:
- atom_acts: bfloat16 [65536, 128], P(('group', 'row', 'col')), parts along dimension 0, may hold values from -6 to 6
- first_gain: float32 [128], replicated, may hold values from 0.25 to 1.75
- first_qkv: bfloat16 [128, 384], replicated, may hold values from -0.5 to 0.5
- first_out: bfloat16 [128, 128], replicated, may hold values from -0.5 to 0.5
- second_gain: float32 [128], replicated, may hold values from 0.25 to 1.75
- second_qkv: bfloat16 [128, 384], replicated, may hold values from -0.5 to 0.5
- second_out: bfloat16 [128, 128], replicated, may hold values from -0.5 to 0.5
- atom_bias: bfloat16 [4, 65536, 128], P(None, ('group', 'row', 'col')), parts along dimension 1, may hold values from -4 to 320
- window_start: int32 [2048], P(('group', 'row', 'col')), parts along dimension 0, may hold values from 0 to 32640, as said below
- atom_token: int32 [65536], P(('group', 'row', 'col')), parts along dimension 0, may hold values from 0 to 1023, as said below
- up_weight: bfloat16 [128, 768], replicated, may hold values from -0.5 to 0.5
- token_gain: float32 [768], replicated, may hold values from 0.25 to 1.75
- token_weight: bfloat16 [768, 3072], replicated, may hold values from -0.21875 to 0.21875
- token_out: bfloat16 [768, 768], replicated, may hold values from -0.21875 to 0.21875
- down_weight: bfloat16 [768, 128], replicated, may hold values from -0.21875 to 0.21875
- pair_bias: bfloat16 [16, 2048, 1024], P(None, ('group', 'row'), 'col'), parts along dimension 1, may hold values from -4 to 320
Outputs:
- atom_result: bfloat16 [65536, 128], P(('group', 'row', 'col')), parts along dimension 0
The draws below stay inside these ranges and needn't reach their ends.
There are 2 independent parts, one for each index of `group`. The reference program is written for one: setup_inputs(seed, part) draws one part's arguments, and reference() takes and returns one part's arrays. A program takes and returns all parts, laid end to end along the dimension named above; an argument that names none is the same for every part. Nothing has to cross between parts.
Inputs may be any that keep to these rules, and one draw needn't show every extreme that they name: `atom_token`: nondecreasing along the atoms; every token has one atom or more; the tokens r * 256 to (r + 1) * 256 - 1 own exactly the atoms r * 8192 to (r + 1) * 8192 - 1; in each such block the first 128 tokens hold one atom each, the others share the rest unevenly. `window_start`: entry b is max(0, min(32640, b * 32 + d)) with d from -64 to 32 - 64; both ends of that range occur.
All inputs are finite; a program needn't handle non-finite values.
Results may differ from the reference program's by a relative error of at most 0.011.
Values may be sent and summed in bfloat16 or wider, within the bound.
No kernel may reach another device: no remote copies, remote signals or barrier semaphores. Data moves between devices by JAX's collectives and lax.ppermute only.
A program may use at most 128 MiB of HBM per device.

```python
import math
import jax
import jax.numpy as jnp
from jax import lax

CA = 128
HA = 4
CT = 768
HT = 16
QB = 32
KW = 128
TOK_ROW = 256
ATOMS = 32768
TOKENS = 1024
RIM = 64
N_ROW = 4
N_COL = 4


def spiked(key, shape):
    base_key = jax.random.fold_in(key, 0)
    return jax.random.truncated_normal(base_key, -4.0, 4.0, shape, jnp.float32)


def draw_atom_bias(key, part):
    return spiked(jax.random.fold_in(key, 11), (HA, ATOMS, KW)).astype(jnp.bfloat16)


def draw_pair_bias(key, part):
    return spiked(jax.random.fold_in(key, 23), (HT, TOKENS, TOKENS)).astype(jnp.bfloat16)


def draw_window_start(key, part):
    windows = ATOMS // QB
    jitter_key, place_key = jax.random.split(jax.random.fold_in(key, 37))
    jitter = jax.random.randint(jitter_key, (windows,), -RIM, QB - KW + RIM + 1)
    extreme_at = jax.random.randint(place_key, (), 2, windows - 3)
    jitter = jitter.at[extreme_at].set(-RIM)
    jitter = jitter.at[extreme_at + 1].set(QB - KW + RIM)
    placed = jnp.arange(windows, dtype=jnp.int32) * QB + jitter
    return jnp.clip(placed, 0, ATOMS - KW).astype(jnp.int32)


def draw_atom_token(key, part):
    row_blocks = TOKENS // TOK_ROW
    block_atoms = ATOMS // row_blocks
    single_tokens = TOK_ROW // 2
    base_key = jax.random.fold_in(key, 53)

    def one_block(block_index):
        block_key = jax.random.fold_in(base_key, block_index)
        single_cuts = jnp.arange(1, single_tokens + 1, dtype=jnp.int32)
        later_cuts = jax.random.permutation(block_key, block_atoms - single_tokens - 1)[:TOK_ROW - single_tokens - 1] + single_tokens + 1
        boundary = jnp.zeros((block_atoms,), jnp.int32).at[single_cuts].add(1).at[later_cuts].add(1)
        return jnp.cumsum(boundary).astype(jnp.int32) + block_index * TOK_ROW
    return jax.vmap(one_block)(jnp.arange(row_blocks, dtype=jnp.int32)).reshape(ATOMS).astype(jnp.int32)


def level_of(stream_key, extent, pieces, least, high):
    def one(axis_at, parts):
        heights = jax.random.uniform(jax.random.fold_in(jax.random.fold_in(stream_key, 6), axis_at), (parts,), jnp.float32, least / len(pieces), high / len(pieces))
        return jnp.repeat(jnp.exp(heights), extent[axis_at] // parts).reshape((-1,) + (1,) * (len(extent) - axis_at - 1))

    factor_of = one(*pieces[0])
    for cut in pieces[1:]:
        factor_of = factor_of * one(*cut)
    return factor_of


def scatter_about(own_key, shape, scale, limit, cuts=(), kind=jnp.bfloat16):
    array = scale * jax.random.normal(own_key, shape, jnp.float32)
    if cuts:
        array = array * level_of(own_key, shape, cuts, -0.22, 0.18)
    return jnp.clip(array, -limit, limit).astype(kind)


def setup_inputs(seed: int = 0, part: int = 0) -> dict:
    keys = jax.random.split(jax.random.key(seed), 17)
    part_keys = jax.random.split(jax.random.fold_in(keys[16], part), 17)
    return {
        "atom_acts": scatter_about(part_keys[0], (ATOMS, CA), 1.0, 6.0, ((0, 16),)),
        "first_gain": jnp.clip(1.0 + 0.15 * jax.random.normal(keys[1], (CA,), jnp.float32), 0.25, 1.75),
        "first_qkv": scatter_about(keys[2], (CA, 3 * CA), CA ** -0.5, 0.5),
        "first_out": scatter_about(keys[3], (CA, CA), CA ** -0.5, 0.5),
        "second_gain": jnp.clip(1.0 + 0.15 * jax.random.normal(keys[4], (CA,), jnp.float32), 0.25, 1.75),
        "second_qkv": scatter_about(keys[5], (CA, 3 * CA), CA ** -0.5, 0.5),
        "second_out": scatter_about(keys[6], (CA, CA), CA ** -0.5, 0.5),
        "atom_bias": draw_atom_bias(jax.random.fold_in(jax.random.fold_in(keys[16], part), 71), part),
        "window_start": draw_window_start(jax.random.fold_in(jax.random.fold_in(keys[16], part), 71), part),
        "atom_token": draw_atom_token(jax.random.fold_in(jax.random.fold_in(keys[16], part), 71), part),
        "up_weight": scatter_about(keys[10], (CA, CT), CA ** -0.5, 0.5),
        "token_gain": jnp.clip(1.0 + 0.15 * jax.random.normal(keys[11], (CT,), jnp.float32), 0.25, 1.75),
        "token_weight": scatter_about(keys[12], (CT, 4 * CT), CT ** -0.5, 0.21875),
        "token_out": scatter_about(keys[13], (CT, CT), CT ** -0.5, 0.21875),
        "down_weight": scatter_about(keys[14], (CT, CA), CT ** -0.5, 0.21875),
        "pair_bias": draw_pair_bias(jax.random.fold_in(jax.random.fold_in(keys[16], part), 71), part),
    }


def layer_norm(values, gain_vec):
    values = values.astype(jnp.float32)
    center = values - lax.optimization_barrier(jnp.mean(values, axis=-1, keepdims=True))
    spread = lax.optimization_barrier(jnp.mean(center * center, axis=-1, keepdims=True))
    return center * lax.rsqrt(spread + 1e-05) * gain_vec.astype(jnp.float32)

def window_block(atom_acts, gain_vec, qkv_weight, out_weight, atom_bias, window_start):
    channels = atom_acts.shape[1]
    head_size = channels // HA
    score_scale = 1.0 / math.sqrt(head_size)
    normed = layer_norm(atom_acts, gain_vec).astype(jnp.bfloat16)
    packed = jnp.dot(normed, qkv_weight, preferred_element_type=jnp.float32).astype(jnp.bfloat16)

    def one_window(window):
        anchor = (window * QB).astype(jnp.int32)
        begin_key = window_start[window].astype(jnp.int32)
        queries = lax.dynamic_slice_in_dim(packed, anchor, QB, 0)[:, :channels]
        beside_all = lax.dynamic_slice_in_dim(packed, begin_key, KW, 0)
        key_heads = beside_all[:, channels:2 * channels].astype(jnp.float32).reshape(KW, HA, head_size)
        value_heads = beside_all[:, 2 * channels:].astype(jnp.float32).reshape(KW, HA, head_size)
        query_heads = queries.astype(jnp.float32).reshape(QB, HA, head_size)
        bias_tile = lax.dynamic_slice_in_dim(atom_bias, anchor, QB, 1).astype(jnp.float32)
        scores = jnp.einsum('qhd,khd->hqk', query_heads, key_heads) * score_scale + bias_tile
        weights = jax.nn.softmax(scores, axis=-1).astype(jnp.bfloat16)
        mixed = jnp.einsum('hqk,khd->qhd', weights.astype(jnp.float32), value_heads).astype(jnp.bfloat16)
        return mixed.reshape(QB, channels)
    mixed = lax.map(one_window, jnp.arange(ATOMS // QB, dtype=jnp.int32)).reshape(ATOMS, channels)
    return (atom_acts.astype(jnp.float32) + jnp.dot(mixed, out_weight, preferred_element_type=jnp.float32)).astype(jnp.bfloat16)

def reference(atom_acts, first_gain, first_qkv, first_out, second_gain, second_qkv, second_out, atom_bias, window_start, atom_token, up_weight, token_gain, token_weight, token_out, down_weight, pair_bias):
    atoms1 = window_block(atom_acts, first_gain, first_qkv, first_out, atom_bias, window_start)
    atom_feat = jax.nn.relu(jnp.dot(atoms1, up_weight, preferred_element_type=jnp.float32)).astype(jnp.bfloat16)
    token_sum = jax.ops.segment_sum(atom_feat.astype(jnp.float32), atom_token, num_segments=TOKENS)
    atom_count = jax.ops.segment_sum(jnp.ones((ATOMS,), jnp.float32), atom_token, num_segments=TOKENS)
    token_act = (token_sum / atom_count[:, None]).astype(jnp.bfloat16)
    tok_normed = layer_norm(token_act, token_gain).astype(jnp.bfloat16)
    tok_proj = jnp.dot(tok_normed, token_weight, preferred_element_type=jnp.float32).astype(jnp.bfloat16)
    queries = tok_proj[:, :CT]
    gate_raw = tok_proj[:, 3 * CT:]
    share_rows = TOK_ROW // N_COL
    ordered = tok_proj[:, CT:3 * CT].reshape(N_ROW, N_COL, share_rows, 2 * CT).transpose(1, 0, 2, 3).reshape(TOKENS, 2 * CT)
    head_size = CT // HT
    score_scale = 1.0 / math.sqrt(head_size)
    query_heads = queries.reshape(TOKENS, HT, head_size).transpose(1, 0, 2)
    key_heads = ordered[:, :CT].reshape(TOKENS, HT, head_size).transpose(1, 0, 2)
    value_heads = ordered[:, CT:].reshape(TOKENS, HT, head_size).transpose(1, 0, 2)

    def one_head(head_items):
        query_one, key_one, value_one, bias_one = head_items
        scores = jnp.dot(query_one, key_one.T, preferred_element_type=jnp.float32) * score_scale + bias_one.astype(jnp.float32)
        row_top = lax.optimization_barrier(jnp.max(scores, axis=-1, keepdims=True))
        exp_scores = jnp.exp(scores - row_top)
        tok_denom = lax.optimization_barrier(jnp.sum(exp_scores, axis=-1))
        tok_weights = exp_scores.astype(jnp.bfloat16)
        return jnp.dot(tok_weights, value_one, preferred_element_type=jnp.float32) / tok_denom[:, None]
    tok_mixed = lax.map(one_head, (query_heads, key_heads, value_heads, pair_bias))
    tok_mixed = tok_mixed.transpose(1, 0, 2).reshape(TOKENS, CT)
    gated = (tok_mixed * jax.nn.sigmoid(gate_raw.astype(jnp.float32))).astype(jnp.bfloat16)
    tok_result = (token_act.astype(jnp.float32) + jnp.dot(gated, token_out, preferred_element_type=jnp.float32)).astype(jnp.bfloat16)
    back_proj = jnp.dot(tok_result, down_weight, preferred_element_type=jnp.float32).astype(jnp.bfloat16)
    atoms2 = (atoms1.astype(jnp.float32) + back_proj[atom_token].astype(jnp.float32)).astype(jnp.bfloat16)
    return window_block(atoms2, second_gain, second_qkv, second_out, atom_bias, window_start)
```

```python
import functools
import math

import jax
import jax.numpy as jnp
from jax import lax
from jax.experimental import pallas as pl
from jax.experimental.pallas import tpu as pltpu
from jax.sharding import PartitionSpec as P

BF = jnp.bfloat16
F32 = jnp.float32
RIM = 64
LANES = 128
VMEM = pl.BlockSpec(memory_space=pltpu.VMEM)
SMEM = pl.BlockSpec(memory_space=pltpu.SMEM)


def dot(a, b):
    return jnp.dot(a, b, preferred_element_type=F32)


def dot_nt(a, b):
    return lax.dot_general(a, b, (((1,), (1,)), ((), ())), preferred_element_type=F32)


def dot_tn(a, b):
    return lax.dot_general(a, b, (((0,), (0,)), ((), ())), preferred_element_type=F32)


def norm_rows(values, gain):
    center = values - jnp.mean(values, axis=-1, keepdims=True)
    spread = jnp.mean(center * center, axis=-1, keepdims=True)
    return center * lax.rsqrt(spread + 1e-05) * gain


def token_of(count, share, first_parity):
    half = count // 2
    row = lax.broadcasted_iota(jnp.int32, (count, 1), 0)
    second = (row >= half).astype(jnp.int32)
    inner = row - second * half
    shift = share.bit_length() - 1
    share_pair = inner >> shift
    inside = inner & (share - 1)
    parity = first_parity + second - 2 * first_parity * second
    return (2 * share_pair + parity) * share + inside


def one_hot(table_ids, atom_ids):
    return jnp.where(table_ids == atom_ids, 1.0, 0.0).astype(BF)


def project(rows, gain, qkv, q, k, v, at):
    channels = rows.shape[1]
    packed = dot(norm_rows(rows.astype(F32), gain).astype(BF), qkv).astype(BF)
    place = slice(RIM + at, RIM + at + rows.shape[0])
    q[at : at + rows.shape[0], :] = packed[:, :channels]
    k[place, :] = packed[:, channels : 2 * channels].astype(F32)
    v[place, :] = packed[:, 2 * channels :].astype(F32)


def project_rim(rows, gain, qkv, k, v, at):
    channels = rows.shape[1]
    normed = norm_rows(rows.astype(F32), gain).astype(BF)
    packed = dot(normed, qkv[:, channels:]).astype(BF).astype(F32)
    place = pl.ds(pl.multiple_of(at, RIM), RIM)
    k[place, :] = packed[:, :channels]
    v[place, :] = packed[:, channels:]


def attend_windows(offsets, bias, q, k, v, mixed):
    heads, atom_rows, span = bias.shape
    windows = offsets.shape[0]
    block = atom_rows // windows
    channels = q.shape[1]
    size = channels // heads
    scale = 1.0 / math.sqrt(size)
    stacked = heads * block
    head_row = lax.broadcasted_iota(jnp.int32, (heads, block, channels), 0).reshape(stacked, channels)
    head_lane = lax.broadcasted_iota(jnp.int32, (stacked, channels), 1) // size
    own_head = jnp.where(head_row == head_lane, 1.0, 0.0).astype(BF)
    lane_head = lax.broadcasted_iota(jnp.int32, (block, channels), 1) // size

    def one_window(window, carry):
        begin = offsets[window]
        anchor = pl.multiple_of(window * block, block)
        keys = k[pl.ds(begin, span), :].astype(BF)
        values = v[pl.ds(begin, span), :].astype(BF)
        query = q[pl.ds(anchor, block), :]
        spread = jnp.concatenate([query] * heads, axis=0) * own_head
        tile = bias[:, pl.ds(anchor, block), :].reshape(stacked, span).astype(F32)
        scores = dot_nt(spread, keys) * scale + tile
        top = jnp.max(scores, axis=-1, keepdims=True)
        raised = jnp.exp(scores - top)
        weights = (raised / jnp.sum(raised, axis=-1, keepdims=True)).astype(BF)
        out = dot(weights, values)
        picked = out[:block]
        for head in range(1, heads):
            picked = jnp.where(lane_head == head, out[head * block : (head + 1) * block], picked)
        mixed[pl.ds(anchor, block), :] = picked.astype(BF)
        return carry

    lax.fori_loop(0, windows, one_window, 0, unroll=4)


def first_block(
    info, offsets, ids, acts, near, far, gain, qkv, out_weight, bias, up, atoms, send, keep, q, k, v, mixed, *, share
):
    side = info[0]
    rows, channels = acts.shape
    gain_row = gain[...]
    weight = qkv[...]
    end = RIM + rows
    project_rim(near[:RIM, :], gain_row, weight, k, v, jnp.where(side == 0, end, 0))
    project_rim(far[:RIM, :], gain_row, weight, k, v, jnp.where(side == 0, 0, end))
    step = 256
    for at in range(0, rows, step):
        project(acts[at : at + step, :], gain_row, weight, q, k, v, at)
    attend_windows(offsets, bias, q, k, v, mixed)
    for at in range(0, rows, step):
        part = acts[at : at + step, :].astype(F32) + dot(mixed[at : at + step, :], out_weight[...])
        atoms[at : at + step, :] = part.astype(BF)
    tokens = 2 * send.shape[0]
    half = tokens // 2
    member = one_hot(token_of(tokens, share, 1 - side), ids[...])
    wide = up.shape[1]
    atom_rows = atoms[...]
    for at in range(0, wide, step):
        feat = jnp.maximum(dot(atom_rows, up[:, at : at + step]), 0.0).astype(BF)
        sums = dot(member, feat).astype(BF)
        send[:, at : at + step] = sums[:half]
        keep[:, at : at + step] = sums[half:]
    count = dot(member, jnp.ones((rows, LANES), BF))
    high = jnp.floor(count * (1.0 / 64.0))
    low = count - 64.0 * high
    lane = lax.broadcasted_iota(jnp.int32, (tokens, LANES), 1)
    pieces = jnp.where(lane == 0, high, jnp.where(lane == 1, low, 0.0)).astype(BF)
    send[:, wide:] = pieces[:half]
    keep[:, wide:] = pieces[half:]


def mean_tokens(*refs, count):
    parts, gain, act, normed = refs[:count], refs[count], refs[count + 1], refs[count + 2]
    total = parts[0][...].astype(F32)
    for part in parts[1:]:
        total = total + part[...].astype(F32)
    wide = act.shape[1]
    atoms = total[:, wide : wide + 1] * 64.0 + total[:, wide + 1 : wide + 2]
    rounded = (total[:, :wide] / atoms).astype(BF)
    act[...] = rounded
    normed[...] = norm_rows(rounded.astype(F32), gain[...]).astype(BF)


def query_tokens(info, weight, gain, own_act, *refs, others):
    other_acts, act, queries, gates = refs[:others], refs[others], refs[others + 1], refs[others + 2]
    share, wide = own_act.shape
    pairs = others + 1
    place = info[2]
    act[pl.ds(pl.multiple_of(place * share, share), share), :] = own_act[...]
    for step in range(1, pairs):
        at = lax.rem(place - step + pairs, pairs) * share
        act[pl.ds(pl.multiple_of(at, share), share), :] = other_acts[step - 1][...]
    normed = norm_rows(act[...].astype(F32), gain[...]).astype(BF)
    queries[...] = dot(normed, weight[:, :wide]).astype(BF)
    raw = dot(normed, weight[:, 3 * wide :]).astype(BF).astype(F32)
    gates[...] = jax.nn.sigmoid(raw)


def attend_tokens(info, weight, queries, bias_own, bias_near, *refs, rows_count):
    own, near = refs[:rows_count], refs[rows_count : 2 * rows_count]
    out, tokens, keys_values = refs[2 * rows_count], refs[2 * rows_count + 1], refs[2 * rows_count + 2]
    share, wide = own[0].shape
    side, row = info[0], info[1]
    keys = rows_count * share
    for step in range(rows_count):
        at = lax.rem(row - step + rows_count, rows_count) * share
        tokens[pl.ds(pl.multiple_of(at, share), share), :] = own[step][...]
        tokens[pl.ds(pl.multiple_of(at + keys, share), share), :] = near[step][...]
    keys_values[...] = dot(tokens[...], weight[:, wide : 3 * wide]).astype(BF)
    count = queries.shape[0]
    pairs = count // share
    heads = bias_own.shape[0]
    size = wide // heads
    scale = 1.0 / math.sqrt(size)
    lane = lax.broadcasted_iota(jnp.int32, (count, LANES), 1)
    blocks = [None] * (wide // LANES)
    logs = jnp.zeros((count, LANES), F32)
    for head in range(heads):
        first, last = head * size, (head + 1) * size
        low, high = first // LANES, -(-last // LANES)
        chunk = slice(low * LANES, high * LANES)
        chunk_lane = lax.broadcasted_iota(jnp.int32, (count, (high - low) * LANES), 1) + low * LANES
        inside = (chunk_lane >= first) & (chunk_lane < last)
        query = jnp.where(inside, queries[:, chunk].astype(F32), 0.0).astype(BF)
        own_rows = [
            bias_own[head, pl.ds(pl.multiple_of((2 * pair + side) * share, share), share), :] for pair in range(pairs)
        ]
        own_tile = jnp.concatenate(own_rows, axis=0).astype(F32)
        scores_own = dot_nt(query, keys_values[:keys, chunk]) * scale + own_tile
        scores_near = dot_nt(query, keys_values[keys:, chunk]) * scale + bias_near[head].astype(F32)
        top = jnp.maximum(
            jnp.max(scores_own, axis=-1, keepdims=True), jnp.max(scores_near, axis=-1, keepdims=True)
        )
        raised_own = jnp.exp(scores_own - top)
        raised_near = jnp.exp(scores_near - top)
        total = jnp.sum(raised_own, axis=-1, keepdims=True) + jnp.sum(raised_near, axis=-1, keepdims=True)
        values = slice(wide + chunk.start, wide + chunk.stop)
        mixed = dot(raised_own.astype(BF), keys_values[:keys, values]) + dot(
            raised_near.astype(BF), keys_values[keys:, values]
        )
        mixed = mixed / total
        logs = jnp.where(lane == head, top + jnp.log(total), logs)
        for block in range(low, high):
            piece = mixed[:, (block - low) * LANES : (block - low + 1) * LANES]
            if blocks[block] is None:
                blocks[block] = piece
            else:
                blocks[block] = jnp.where(lane + block * LANES >= first, piece, blocks[block])
    for block, piece in enumerate(blocks):
        out[:, block * LANES : (block + 1) * LANES] = piece.astype(BF)
    top_piece = logs.astype(BF).astype(F32)
    rest = logs - top_piece
    middle = rest.astype(BF).astype(F32)
    rest = rest - middle
    out[:, wide:] = (top_piece + pltpu.roll(middle, heads, 1) + pltpu.roll(rest, 2 * heads, 1)).astype(BF)


def finish_tokens(act, gates, token_out, down, *refs, parts_count):
    parts, back = refs[:parts_count], refs[parts_count]
    count, wide = act.shape
    heads = 16
    size = wide // heads
    logs = []
    for part in parts:
        packed = part[:, wide:].astype(F32)
        logs.append(
            packed + pltpu.roll(packed, LANES - heads, 1) + pltpu.roll(packed, LANES - 2 * heads, 1)
        )
    top = functools.reduce(jnp.maximum, logs)
    weights = [jnp.exp(log - top) for log in logs]
    total = functools.reduce(jnp.add, weights)
    head = lax.broadcasted_iota(jnp.int32, (LANES, wide), 0)
    feature = lax.broadcasted_iota(jnp.int32, (LANES, wide), 1)
    expand = jnp.where((feature >= head * size) & (feature < (head + 1) * size), 1.0, 0.0).astype(BF)
    mixed = jnp.zeros((count, wide), F32)
    for part, weight in zip(parts, weights):
        factor = weight / total
        coarse = factor.astype(BF)
        fine = (factor - coarse.astype(F32)).astype(BF)
        mixed = mixed + (dot(coarse, expand) + dot(fine, expand)) * part[:, :wide].astype(F32)
    gated = (mixed * gates[...]).astype(BF)
    result = (act[...].astype(F32) + dot(gated, token_out[...])).astype(BF)
    back[...] = dot(result, down[...]).astype(BF)


def second_block(
    info, offsets, ids, atoms1, near, far, near_ids, far_ids, own_back, near_back, far_back,
    gain, qkv, out_weight, bias, result, q, k, v, mixed, table, atoms2, *, share, columns
):
    side, column = info[0], info[3]
    rows, channels = atoms1.shape
    gain_row = gain[...]
    weight = qkv[...]
    half = own_back.shape[0]
    tokens = 2 * half
    table[:half, :] = own_back[...]
    table[half:, :] = near_back[...]
    table_ids = token_of(tokens, share, side)
    end = RIM + rows
    first_token = (info[1] * tokens).astype(F32)

    def rim_ids(message):
        packed = message[RIM : RIM + 16, :].astype(F32)
        return (packed[0:1, :RIM] * 64.0 + packed[1:2, :RIM] - first_token).astype(jnp.int32)

    near_rows = near[...].astype(F32) + dot_tn(one_hot(table_ids, rim_ids(near_ids)), table[...])
    project_rim(near_rows.astype(BF), gain_row, weight, k, v, jnp.where(side == 0, end, 0))
    far_token = rim_ids(far_ids)
    beyond = lax.broadcasted_iota(jnp.int32, (RIM, 1), 0) + jnp.where(
        column == 0, -RIM, jnp.where(column == columns - 1, tokens, 4 * tokens)
    )
    far_rows = (
        far[...].astype(F32)
        + dot_tn(one_hot(table_ids, far_token), table[...])
        + dot_tn(one_hot(beyond, far_token), far_back[...])
    )
    project_rim(far_rows.astype(BF), gain_row, weight, k, v, jnp.where(side == 0, 0, end))
    step = 256
    for at in range(0, rows, step):
        member = one_hot(table_ids, ids[:, at : at + step])
        moved = (atoms1[at : at + step, :].astype(F32) + dot_tn(member, table[...])).astype(BF)
        atoms2[at : at + step, :] = moved
        project(moved, gain_row, weight, q, k, v, at)
    attend_windows(offsets, bias, q, k, v, mixed)
    for at in range(0, rows, step):
        part = atoms2[at : at + step, :].astype(F32) + dot(mixed[at : at + step, :], out_weight[...])
        result[at : at + step, :] = part.astype(BF)


def call(kernel, outs, scratch, specs, flops, limit=40):
    return pl.pallas_call(
        kernel,
        out_shape=outs,
        in_specs=specs,
        out_specs=jax.tree.map(lambda _: VMEM, outs),
        scratch_shapes=scratch,
        compiler_params=pltpu.CompilerParams(vmem_limit_bytes=limit * 1024 * 1024),
        cost_estimate=pl.CostEstimate(flops=flops, bytes_accessed=4_000_000, transcendentals=1_000_000),
    )


def body(
    atom_acts, first_gain, first_qkv, first_out, second_gain, second_qkv, second_out, atom_bias, window_start,
    atom_token, up_weight, token_gain, token_weight, token_out, down_weight, pair_bias,
):
    rows, channels = atom_acts.shape
    heads, tok_rows, slots = pair_bias.shape
    wide = token_weight.shape[0]
    row_count, col_count = lax.axis_size("row"), lax.axis_size("col")
    pairs = col_count // 2
    share = tok_rows // col_count
    half = tok_rows // 2
    row, col = lax.axis_index("row"), lax.axis_index("col")
    side, pair = col % 2, col // 2
    info = jnp.stack([side, row, pair, col]).astype(jnp.int32)
    devices = row_count * col_count

    def to_near(x):
        return lax.ppermute(x, "col", [(i, i ^ 1) for i in range(col_count)])

    def to_far(x):
        swap = [(i, (i + 1) % devices if i % 2 else (i - 1) % devices) for i in range(devices)]
        return lax.ppermute(x, ("row", "col"), swap)

    def along_pairs(x, step):
        return lax.ppermute(
            x, "col", [(2 * i + k, 2 * ((i + step) % pairs) + k) for i in range(pairs) for k in range(2)]
        )

    def along_rows(x, step):
        return lax.ppermute(x, "row", [(i, (i + step) % row_count) for i in range(row_count)])

    def rim_of(x, last):
        return lax.dynamic_slice_in_dim(x, jnp.where(last, rows - RIM, 0), RIM, axis=0)

    def message(last):
        acts = rim_of(atom_acts, last)
        ids = rim_of(atom_token, last)
        coded = jnp.stack([ids >> 6, ids & 63]).astype(BF)
        coded = jnp.pad(coded, ((0, 14), (0, channels - RIM)))
        return jnp.concatenate([acts, coded], axis=0)

    near_acts = to_near(message(side == 0))
    far_acts = to_far(message(side == 1))
    split_bias = pair_bias.reshape(heads, pairs, 2, share, slots)
    bias_near = to_near(lax.dynamic_index_in_dim(split_bias, 1 - side, 2, False).reshape(heads, half, slots))

    offsets = window_start - (row * col_count + col) * rows + RIM
    ids = (atom_token - row * tok_rows).reshape(1, rows)
    window_scratch = [
        pltpu.VMEM((rows, channels), BF),
        pltpu.VMEM((rows + 2 * RIM, channels), F32),
        pltpu.VMEM((rows + 2 * RIM, channels), F32),
        pltpu.VMEM((rows, channels), BF),
    ]
    packed_shape = jax.ShapeDtypeStruct((half, wide + LANES), BF)
    atoms1, send, keep = call(
        functools.partial(first_block, share=share),
        [jax.ShapeDtypeStruct((rows, channels), BF), packed_shape, packed_shape],
        window_scratch,
        [SMEM, SMEM] + [VMEM] * 9,
        3_000_000_000,
    )(
        info, offsets, ids, atom_acts, near_acts, far_acts, first_gain.reshape(1, -1), first_qkv, first_out,
        atom_bias, up_weight,
    )

    chip_sum = (keep.astype(F32) + to_near(send).astype(F32)).astype(BF)
    sums = [lax.dynamic_slice_in_dim(chip_sum, pair * share, share, axis=0)]
    for step in range(1, pairs):
        piece = lax.dynamic_slice_in_dim(chip_sum, (pair + step) % pairs * share, share, axis=0)
        sums.append(along_pairs(piece, step))
    share_shape = jax.ShapeDtypeStruct((share, wide), BF)
    gain_row = token_gain.reshape(1, -1)
    act, normed = call(
        functools.partial(mean_tokens, count=len(sums)), [share_shape] * 2, [], [VMEM] * (len(sums) + 1), 1_000_000
    )(*sums, gain_row)

    own_keys = [normed] + [along_rows(normed, step) for step in range(1, row_count)]
    near_keys = [to_near(x) for x in own_keys]
    other_acts = [along_pairs(act, step) for step in range(1, pairs)]
    half_shape = jax.ShapeDtypeStruct((half, wide), BF)
    act_rows, queries, gates = call(
        functools.partial(query_tokens, others=len(other_acts)),
        [half_shape, half_shape, jax.ShapeDtypeStruct((half, wide), F32)],
        [],
        [SMEM] + [VMEM] * (3 + len(other_acts)),
        300_000_000,
    )(info, token_weight, gain_row, act, *other_acts)

    near_atoms = to_near(rim_of(atoms1, side == 0))
    far_atoms = to_far(rim_of(atoms1, side == 1))

    part = call(
        functools.partial(attend_tokens, rows_count=row_count),
        packed_shape,
        [pltpu.VMEM((2 * slots, wide), BF), pltpu.VMEM((2 * slots, 2 * wide), BF)],
        [SMEM] + [VMEM] * (4 + 2 * row_count),
        2_000_000_000,
    )(info, token_weight, queries, pair_bias, bias_near, *own_keys, *near_keys)

    parts = [part] + [along_pairs(part, step) for step in range(1, pairs)]
    own_back = call(
        functools.partial(finish_tokens, parts_count=pairs),
        jax.ShapeDtypeStruct((half, channels), BF),
        [],
        [VMEM] * (4 + pairs),
        200_000_000,
    )(act_rows, gates, token_out, down_weight, *parts)

    near_back = to_near(own_back)
    if share >= RIM:
        last_rows = own_back[half - RIM :]
        first_rows = own_back[:RIM]
    else:
        both = jnp.where(side == 0, jnp.stack([own_back, near_back]), jnp.stack([near_back, own_back]))
        both = both.reshape(2, pairs, share, channels).transpose(1, 0, 2, 3).reshape(tok_rows, channels)
        last_rows = both[tok_rows - RIM :]
        first_rows = both[:RIM]
    far_back = to_far(jnp.where(side == 1, last_rows, first_rows))

    return call(
        functools.partial(second_block, share=share, columns=col_count),
        jax.ShapeDtypeStruct((rows, channels), BF),
        window_scratch + [pltpu.VMEM((tok_rows, channels), BF), pltpu.VMEM((rows, channels), BF)],
        [SMEM, SMEM] + [VMEM] * 13,
        1_500_000_000,
    )(
        info, offsets, ids, atoms1, near_atoms, far_atoms, near_acts, far_acts, own_back, near_back, far_back,
        second_gain.reshape(1, -1), second_qkv, second_out, atom_bias,
    )


def solution(mesh):
    atoms = P(("group", "row", "col"))
    in_specs = (
        P(("group", "row", "col"), None),
        P(), P(), P(), P(), P(), P(),
        P(None, ("group", "row", "col"), None),
        atoms,
        atoms,
        P(), P(), P(), P(), P(),
        P(None, ("group", "row"), "col"),
    )
    out_specs = P(("group", "row", "col"), None)
    return jax.shard_map(body, mesh=mesh, in_specs=in_specs, out_specs=out_specs, check_vma=False)
```

```python
import functools
import math

import jax
import jax.numpy as jnp
from jax import lax
from jax.experimental import pallas as pl
from jax.experimental.pallas import tpu as pltpu
from jax.sharding import PartitionSpec as P

BF = jnp.bfloat16
F32 = jnp.float32
RIM = 64
LANES = 128
VMEM = pl.BlockSpec(memory_space=pltpu.VMEM)
SMEM = pl.BlockSpec(memory_space=pltpu.SMEM)


def dot(a, b):
    return jnp.dot(a, b, preferred_element_type=F32)


def dot_nt(a, b):
    return lax.dot_general(a, b, (((1,), (1,)), ((), ())), preferred_element_type=F32)


def dot_tn(a, b):
    return lax.dot_general(a, b, (((0,), (0,)), ((), ())), preferred_element_type=F32)


def norm_rows(values, gain):
    center = values - jnp.mean(values, axis=-1, keepdims=True)
    spread = jnp.mean(center * center, axis=-1, keepdims=True)
    return center * lax.rsqrt(spread + 1e-05) * gain


def token_of(count, share, first_parity):
    half = count // 2
    row = lax.broadcasted_iota(jnp.int32, (count, 1), 0)
    second = (row >= half).astype(jnp.int32)
    inner = row - second * half
    shift = share.bit_length() - 1
    share_pair = inner >> shift
    inside = inner & (share - 1)
    parity = first_parity + second - 2 * first_parity * second
    return (2 * share_pair + parity) * share + inside


def one_hot(table_ids, atom_ids):
    return jnp.where(table_ids == atom_ids, 1.0, 0.0).astype(BF)


def project(rows, gain, qkv, q, k, v, at):
    channels = rows.shape[1]
    packed = dot(norm_rows(rows.astype(F32), gain).astype(BF), qkv).astype(BF)
    place = slice(at, at + rows.shape[0])
    q[place, :] = packed[:, :channels]
    k[place, :] = packed[:, channels : 2 * channels].astype(F32)
    v[place, :] = packed[:, 2 * channels :].astype(F32)


def attend_windows(places, bias, q, k, v, mixed):
    heads, _, span = bias.shape
    channels = q.shape[1]
    block = span - 3 * RIM // 2
    size = channels // heads
    scale = 1.0 / math.sqrt(size)
    stacked = heads * block
    head_row = lax.broadcasted_iota(jnp.int32, (heads, block, channels), 0).reshape(stacked, channels)
    head_lane = lax.broadcasted_iota(jnp.int32, (stacked, channels), 1) // size
    own_head = jnp.where(head_row == head_lane, 1.0, 0.0).astype(BF)
    lane_head = lax.broadcasted_iota(jnp.int32, (block, channels), 1) // size
    ones = jnp.ones((span, channels), BF)

    def picked(stack):
        out = stack[:block]
        for head in range(1, heads):
            out = jnp.where(lane_head == head, stack[head * block : (head + 1) * block], out)
        return out

    scores = []
    for query_at, _, key_at in places:
        spread = jnp.concatenate([q[pl.ds(query_at, block), :]] * heads, axis=0) * own_head
        scores.append(dot_nt(spread, k[pl.ds(key_at, span), :].astype(BF)))
    raised = []
    for (_, bias_at, _), score in zip(places, scores):
        tile = bias[:, pl.ds(bias_at, block), :].reshape(stacked, span).astype(F32)
        score = score * scale + tile
        raised.append(jnp.exp(score - jnp.max(score, axis=-1, keepdims=True)).astype(BF))
    for (query_at, _, key_at), weights in zip(places, raised):
        values = jnp.concatenate([v[pl.ds(key_at, span), :].astype(BF), ones], axis=1)
        out = dot(weights, values)
        mixed[pl.ds(query_at, block), :] = (picked(out[:, :channels]) / picked(out[:, channels:])).astype(BF)


def inner_windows(offsets, bias, q, k, v, mixed, edge_q, edge_k, edge_v):
    windows = offsets.shape[0]
    rows = q.shape[0]
    block = rows // windows
    edge = RIM // block
    group = next(size for size in (15, 12, 10, 6, 5, 4, 3, 2, 1) if (windows - 2 * edge) % size == 0)

    def one_group(step, carry):
        places = []
        for member in range(group):
            window = edge + step * group + member
            at = pl.multiple_of(window * block, block)
            places.append((at, at, offsets[window] - RIM))
        attend_windows(places, bias, q, k, v, mixed)
        return carry

    lax.fori_loop(0, (windows - 2 * edge) // group, one_group, 0)
    edge_q[:RIM, :] = q[:RIM, :]
    edge_q[RIM:, :] = q[rows - RIM :, :]
    for source, target in ((k, edge_k), (v, edge_v)):
        target[: 2 * RIM, :] = source[: 2 * RIM, :]
        target[2 * RIM :, :] = source[rows - 2 * RIM :, :]


def edge_windows(offsets, bias, gain, qkv, near, far, side, edge_q, edge_k, edge_v, k, v, mixed):
    windows = offsets.shape[0]
    rows = bias.shape[1]
    channels = edge_q.shape[1]
    block = rows // windows
    edge = RIM // block
    for source, target in ((edge_k, k), (edge_v, v)):
        target[RIM : 3 * RIM, :] = source[: 2 * RIM, :]
        target[3 * RIM : 5 * RIM, :] = source[2 * RIM :, :]
    normed = norm_rows(jnp.concatenate([near, far], axis=0), gain).astype(BF)
    packed = dot(normed, qkv[:, channels:]).astype(BF).astype(F32)
    near_at = pl.multiple_of(jnp.where(side == 0, 5 * RIM, 0), RIM)
    far_at = pl.multiple_of(5 * RIM - near_at, RIM)
    for at, part in ((near_at, packed[:RIM]), (far_at, packed[RIM:])):
        k[pl.ds(at, RIM), :] = part[:, :channels]
        v[pl.ds(at, RIM), :] = part[:, channels:]
    places = []
    for member in range(edge):
        places.append((member * block, member * block, offsets[member]))
    for member in range(edge):
        window = windows - edge + member
        places.append((RIM + member * block, window * block, offsets[window] - (rows - 4 * RIM)))
    attend_windows(places, bias, edge_q, k, v, mixed)


def first_inner(offsets, acts, gain, qkv, bias, mixed, edge_q, edge_k, edge_v, q, k, v):
    step = 256
    for at in range(0, acts.shape[0], step):
        project(acts[at : at + step, :], gain[...], qkv[...], q, k, v, at)
    inner_windows(offsets, bias, q, k, v, mixed, edge_q, edge_k, edge_v)


def first_edge(
    info, offsets, ids, acts, near, far, gain, qkv, out_weight, bias, up, mixed, edge_q, edge_k, edge_v,
    atoms, send, keep, k, v, edge_mixed, *, share
):
    side = info[0]
    rows = acts.shape[0]
    edge_windows(
        offsets, bias, gain[...], qkv[...], near[:RIM, :].astype(F32), far[:RIM, :].astype(F32), side,
        edge_q, edge_k, edge_v, k, v, edge_mixed,
    )
    close_rows(acts, mixed, edge_mixed, out_weight, atoms)
    step = 256
    tokens = 2 * send.shape[0]
    half = tokens // 2
    member = one_hot(token_of(tokens, share, 1 - side), ids[...])
    wide = up.shape[1]
    atom_rows = atoms[...]
    for at in range(0, wide, step):
        feat = jnp.maximum(dot(atom_rows, up[:, at : at + step]), 0.0).astype(BF)
        sums = dot(member, feat).astype(BF)
        send[:, at : at + step] = sums[:half]
        keep[:, at : at + step] = sums[half:]
    count = dot(member, jnp.ones((rows, LANES), BF))
    high = jnp.floor(count * (1.0 / 64.0))
    low = count - 64.0 * high
    lane = lax.broadcasted_iota(jnp.int32, (tokens, LANES), 1)
    pieces = jnp.where(lane == 0, high, jnp.where(lane == 1, low, 0.0)).astype(BF)
    send[:, wide:] = pieces[:half]
    keep[:, wide:] = pieces[half:]


def close_rows(acts, mixed, edge_mixed, out_weight, out):
    rows = acts.shape[0]
    weight = out_weight[...]
    step = 256
    for at in range(0, rows, step):
        first, last = at, at + step
        pieces = [mixed[max(first, RIM) : min(last, rows - RIM), :]]
        if first == 0:
            pieces.insert(0, edge_mixed[:RIM, :])
        if last == rows:
            pieces.append(edge_mixed[RIM:, :])
        block = jnp.concatenate(pieces, axis=0)
        out[first:last, :] = (acts[first:last, :].astype(F32) + dot(block, weight)).astype(BF)


def mean_tokens(*refs, count):
    parts, gain, act, normed = refs[:count], refs[count], refs[count + 1], refs[count + 2]
    total = parts[0][...].astype(F32)
    for part in parts[1:]:
        total = total + part[...].astype(F32)
    wide = act.shape[1]
    atoms = total[:, wide : wide + 1] * 64.0 + total[:, wide + 1 : wide + 2]
    rounded = (total[:, :wide] / atoms).astype(BF)
    act[...] = rounded
    normed[...] = norm_rows(rounded.astype(F32), gain[...]).astype(BF)


def query_tokens(info, weight, gain, own_act, *refs, others):
    other_acts, act, queries, gates = refs[:others], refs[others], refs[others + 1], refs[others + 2]
    share, wide = own_act.shape
    pairs = others + 1
    place = info[2]
    act[pl.ds(pl.multiple_of(place * share, share), share), :] = own_act[...]
    for step in range(1, pairs):
        at = lax.rem(place - step + pairs, pairs) * share
        act[pl.ds(pl.multiple_of(at, share), share), :] = other_acts[step - 1][...]
    normed = norm_rows(act[...].astype(F32), gain[...]).astype(BF)
    queries[...] = dot(normed, weight[:, :wide]).astype(BF)
    raw = dot(normed, weight[:, 3 * wide :]).astype(BF).astype(F32)
    gates[...] = jax.nn.sigmoid(raw)


def attend_tokens(info, weight, queries, bias_own, bias_near, *refs, rows_count):
    own, near = refs[:rows_count], refs[rows_count : 2 * rows_count]
    out, tokens, keys_values = refs[2 * rows_count], refs[2 * rows_count + 1], refs[2 * rows_count + 2]
    share, wide = own[0].shape
    side, row = info[0], info[1]
    keys = rows_count * share
    for step in range(rows_count):
        at = lax.rem(row - step + rows_count, rows_count) * share
        tokens[pl.ds(pl.multiple_of(at, share), share), :] = own[step][...]
        tokens[pl.ds(pl.multiple_of(at + keys, share), share), :] = near[step][...]
    keys_values[...] = dot(tokens[...], weight[:, wide : 3 * wide]).astype(BF)
    count = queries.shape[0]
    pairs = count // share
    heads = bias_own.shape[0]
    size = wide // heads
    scale = 1.0 / math.sqrt(size)
    lane = lax.broadcasted_iota(jnp.int32, (count, LANES), 1)
    blocks = [None] * (wide // LANES)
    logs = jnp.zeros((count, LANES), F32)
    for head in range(heads):
        first, last = head * size, (head + 1) * size
        low, high = first // LANES, -(-last // LANES)
        chunk = slice(low * LANES, high * LANES)
        chunk_lane = lax.broadcasted_iota(jnp.int32, (count, (high - low) * LANES), 1) + low * LANES
        inside = (chunk_lane >= first) & (chunk_lane < last)
        query = jnp.where(inside, queries[:, chunk].astype(F32), 0.0).astype(BF)
        own_rows = [
            bias_own[head, pl.ds(pl.multiple_of((2 * pair + side) * share, share), share), :] for pair in range(pairs)
        ]
        own_tile = jnp.concatenate(own_rows, axis=0).astype(F32)
        scores_own = dot_nt(query, keys_values[:keys, chunk]) * scale + own_tile
        scores_near = dot_nt(query, keys_values[keys:, chunk]) * scale + bias_near[head].astype(F32)
        top = jnp.maximum(
            jnp.max(scores_own, axis=-1, keepdims=True), jnp.max(scores_near, axis=-1, keepdims=True)
        )
        raised_own = jnp.exp(scores_own - top)
        raised_near = jnp.exp(scores_near - top)
        total = jnp.sum(raised_own, axis=-1, keepdims=True) + jnp.sum(raised_near, axis=-1, keepdims=True)
        values = slice(wide + chunk.start, wide + chunk.stop)
        mixed = dot(raised_own.astype(BF), keys_values[:keys, values]) + dot(
            raised_near.astype(BF), keys_values[keys:, values]
        )
        mixed = mixed / total
        logs = jnp.where(lane == head, top + jnp.log(total), logs)
        for block in range(low, high):
            piece = mixed[:, (block - low) * LANES : (block - low + 1) * LANES]
            if blocks[block] is None:
                blocks[block] = piece
            else:
                blocks[block] = jnp.where(lane + block * LANES >= first, piece, blocks[block])
    for block, piece in enumerate(blocks):
        out[:, block * LANES : (block + 1) * LANES] = piece.astype(BF)
    top_piece = logs.astype(BF).astype(F32)
    rest = logs - top_piece
    middle = rest.astype(BF).astype(F32)
    rest = rest - middle
    out[:, wide:] = (top_piece + pltpu.roll(middle, heads, 1) + pltpu.roll(rest, 2 * heads, 1)).astype(BF)


def finish_tokens(act, gates, token_out, down, *refs, parts_count):
    parts, back = refs[:parts_count], refs[parts_count]
    count, wide = act.shape
    heads = 16
    size = wide // heads
    logs = []
    for part in parts:
        packed = part[:, wide:].astype(F32)
        logs.append(
            packed + pltpu.roll(packed, LANES - heads, 1) + pltpu.roll(packed, LANES - 2 * heads, 1)
        )
    top = functools.reduce(jnp.maximum, logs)
    weights = [jnp.exp(log - top) for log in logs]
    total = functools.reduce(jnp.add, weights)
    head = lax.broadcasted_iota(jnp.int32, (LANES, wide), 0)
    feature = lax.broadcasted_iota(jnp.int32, (LANES, wide), 1)
    expand = jnp.where((feature >= head * size) & (feature < (head + 1) * size), 1.0, 0.0).astype(BF)
    mixed = jnp.zeros((count, wide), F32)
    for part, weight in zip(parts, weights):
        factor = weight / total
        coarse = factor.astype(BF)
        fine = (factor - coarse.astype(F32)).astype(BF)
        mixed = mixed + (dot(coarse, expand) + dot(fine, expand)) * part[:, :wide].astype(F32)
    gated = (mixed * gates[...]).astype(BF)
    result = (act[...].astype(F32) + dot(gated, token_out[...])).astype(BF)
    back[...] = dot(result, down[...]).astype(BF)


def second_inner(
    info, offsets, ids, atoms1, own_back, near_back, gain, qkv, bias,
    atoms2, mixed, edge_q, edge_k, edge_v, q, k, v, *, share
):
    tokens = 2 * own_back.shape[0]
    table = jnp.concatenate([own_back[...], near_back[...]], axis=0)
    table_ids = token_of(tokens, share, info[0])
    step = 256
    for at in range(0, atoms1.shape[0], step):
        member = one_hot(table_ids, ids[:, at : at + step])
        moved = (atoms1[at : at + step, :].astype(F32) + dot_tn(member, table)).astype(BF)
        atoms2[at : at + step, :] = moved
        project(moved, gain[...], qkv[...], q, k, v, at)
    inner_windows(offsets, bias, q, k, v, mixed, edge_q, edge_k, edge_v)


def second_edge(
    info, offsets, atoms2, near, far, near_ids, far_ids, own_back, near_back, far_back, gain, qkv, out_weight, bias,
    mixed, edge_q, edge_k, edge_v, result, k, v, edge_mixed, *, share, columns
):
    side, column = info[0], info[3]
    tokens = 2 * own_back.shape[0]
    table = jnp.concatenate([own_back[...], near_back[...]], axis=0)
    table_ids = token_of(tokens, share, side)
    first_token = (info[1] * tokens).astype(F32)

    def rim_ids(message):
        packed = message[RIM : RIM + 16, :].astype(F32)
        return (packed[0:1, :RIM] * 64.0 + packed[1:2, :RIM] - first_token).astype(jnp.int32)

    near_rows = near[...].astype(F32) + dot_tn(one_hot(table_ids, rim_ids(near_ids)), table)
    far_token = rim_ids(far_ids)
    beyond = lax.broadcasted_iota(jnp.int32, (RIM, 1), 0) + jnp.where(
        column == 0, -RIM, jnp.where(column == columns - 1, tokens, 4 * tokens)
    )
    far_rows = (
        far[...].astype(F32)
        + dot_tn(one_hot(table_ids, far_token), table)
        + dot_tn(one_hot(beyond, far_token), far_back[...])
    )
    edge_windows(
        offsets, bias, gain[...], qkv[...], near_rows.astype(BF).astype(F32), far_rows.astype(BF).astype(F32), side,
        edge_q, edge_k, edge_v, k, v, edge_mixed,
    )
    close_rows(atoms2, mixed, edge_mixed, out_weight, result)


def call(kernel, outs, scratch, specs, flops, limit=28):
    return pl.pallas_call(
        kernel,
        out_shape=outs,
        in_specs=specs,
        out_specs=jax.tree.map(lambda _: VMEM, outs),
        scratch_shapes=scratch,
        compiler_params=pltpu.CompilerParams(vmem_limit_bytes=limit * 1024 * 1024),
        cost_estimate=pl.CostEstimate(flops=flops, bytes_accessed=4_000_000, transcendentals=1_000_000),
    )


def body(
    atom_acts, first_gain, first_qkv, first_out, second_gain, second_qkv, second_out, atom_bias, window_start,
    atom_token, up_weight, token_gain, token_weight, token_out, down_weight, pair_bias,
):
    rows, channels = atom_acts.shape
    heads, tok_rows, slots = pair_bias.shape
    wide = token_weight.shape[0]
    row_count, col_count = lax.axis_size("row"), lax.axis_size("col")
    pairs = col_count // 2
    share = tok_rows // col_count
    half = tok_rows // 2
    row, col = lax.axis_index("row"), lax.axis_index("col")
    side, pair = col % 2, col // 2
    info = jnp.stack([side, row, pair, col]).astype(jnp.int32)
    devices = row_count * col_count

    def to_near(x):
        return lax.ppermute(x, "col", [(i, i ^ 1) for i in range(col_count)])

    def to_far(x):
        swap = [(i, i + 1 if i % 2 else i - 1) for i in range(1, devices - 1)]
        swap = [(0, 0)] + swap + [(devices - 1, devices - 1)]
        return lax.ppermute(x, ("row", "col"), swap)

    def along_pairs(x, step):
        return lax.ppermute(
            x, "col", [(2 * i + k, 2 * ((i + step) % pairs) + k) for i in range(pairs) for k in range(2)]
        )

    def along_rows(x, step):
        return lax.ppermute(x, "row", [(i, (i + step) % row_count) for i in range(row_count)])

    def rim_of(x, last):
        return lax.dynamic_slice_in_dim(x, jnp.where(last, rows - RIM, 0), RIM, axis=0)

    def message(last):
        acts = rim_of(atom_acts, last)
        ids = rim_of(atom_token, last)
        coded = jnp.stack([ids >> 6, ids & 63]).astype(BF)
        coded = jnp.pad(coded, ((0, 14), (0, channels - RIM)))
        return jnp.concatenate([acts, coded], axis=0)

    near_acts = to_near(message(side == 0))
    far_acts = to_far(message(side == 1))
    split_bias = pair_bias.reshape(heads, pairs, 2, share, slots)
    bias_near = to_near(lax.dynamic_index_in_dim(split_bias, 1 - side, 2, False).reshape(heads, half, slots))

    offsets = window_start - (row * col_count + col) * rows + RIM
    ids = (atom_token - row * tok_rows).reshape(1, rows)
    inner_scratch = [
        pltpu.VMEM((rows, channels), BF),
        pltpu.VMEM((rows, channels), F32),
        pltpu.VMEM((rows, channels), F32),
    ]
    edge_scratch = [
        pltpu.VMEM((6 * RIM, channels), F32),
        pltpu.VMEM((6 * RIM, channels), F32),
        pltpu.VMEM((2 * RIM, channels), BF),
    ]
    atom_shape = jax.ShapeDtypeStruct((rows, channels), BF)
    edge_shapes = [
        jax.ShapeDtypeStruct((2 * RIM, channels), BF),
        jax.ShapeDtypeStruct((4 * RIM, channels), F32),
        jax.ShapeDtypeStruct((4 * RIM, channels), F32),
    ]
    packed_shape = jax.ShapeDtypeStruct((half, wide + LANES), BF)
    first_gain, second_gain = first_gain.reshape(1, -1), second_gain.reshape(1, -1)
    mixed1 = call(
        first_inner, [atom_shape] + edge_shapes, inner_scratch, [SMEM] + [VMEM] * 4, 1_500_000_000, 24
    )(offsets, atom_acts, first_gain, first_qkv, atom_bias)
    atoms1, send, keep = call(
        functools.partial(first_edge, share=share),
        [atom_shape, packed_shape, packed_shape],
        edge_scratch,
        [SMEM, SMEM] + [VMEM] * 13,
        2_000_000_000,
        24,
    )(
        info, offsets, ids, atom_acts, near_acts, far_acts, first_gain, first_qkv, first_out,
        atom_bias, up_weight, *mixed1,
    )

    chip_sum = (keep.astype(F32) + to_near(send).astype(F32)).astype(BF)
    sums = [lax.dynamic_slice_in_dim(chip_sum, pair * share, share, axis=0)]
    for step in range(1, pairs):
        piece = lax.dynamic_slice_in_dim(chip_sum, (pair + step) % pairs * share, share, axis=0)
        sums.append(along_pairs(piece, step))
    share_shape = jax.ShapeDtypeStruct((share, wide), BF)
    gain_row = token_gain.reshape(1, -1)
    act, normed = call(
        functools.partial(mean_tokens, count=len(sums)), [share_shape] * 2, [], [VMEM] * (len(sums) + 1), 1_000_000
    )(*sums, gain_row)

    own_keys = [normed] + [along_rows(normed, step) for step in range(1, row_count)]
    near_keys = [to_near(x) for x in own_keys]
    other_acts = [along_pairs(act, step) for step in range(1, pairs)]
    half_shape = jax.ShapeDtypeStruct((half, wide), BF)
    act_rows, queries, gates = call(
        functools.partial(query_tokens, others=len(other_acts)),
        [half_shape, half_shape, jax.ShapeDtypeStruct((half, wide), F32)],
        [],
        [SMEM] + [VMEM] * (3 + len(other_acts)),
        300_000_000,
    )(info, token_weight, gain_row, act, *other_acts)

    near_atoms = to_near(rim_of(atoms1, side == 0))
    far_atoms = to_far(rim_of(atoms1, side == 1))

    part = call(
        functools.partial(attend_tokens, rows_count=row_count),
        packed_shape,
        [pltpu.VMEM((2 * slots, wide), BF), pltpu.VMEM((2 * slots, 2 * wide), BF)],
        [SMEM] + [VMEM] * (4 + 2 * row_count),
        2_000_000_000,
    )(info, token_weight, queries, pair_bias, bias_near, *own_keys, *near_keys)

    parts = [part] + [along_pairs(part, step) for step in range(1, pairs)]
    own_back = call(
        functools.partial(finish_tokens, parts_count=pairs),
        jax.ShapeDtypeStruct((half, channels), BF),
        [],
        [VMEM] * (4 + pairs),
        200_000_000,
    )(act_rows, gates, token_out, down_weight, *parts)

    near_back = to_near(own_back)
    if share >= RIM:
        last_rows = own_back[half - RIM :]
        first_rows = own_back[:RIM]
    else:
        both = jnp.where(side == 0, jnp.stack([own_back, near_back]), jnp.stack([near_back, own_back]))
        both = both.reshape(2, pairs, share, channels).transpose(1, 0, 2, 3).reshape(tok_rows, channels)
        last_rows = both[tok_rows - RIM :]
        first_rows = both[:RIM]
    far_back = to_far(jnp.where(side == 1, last_rows, first_rows))

    atoms2, *mixed2 = call(
        functools.partial(second_inner, share=share),
        [atom_shape, atom_shape] + edge_shapes,
        inner_scratch,
        [SMEM, SMEM] + [VMEM] * 7,
        1_500_000_000,
        24,
    )(info, offsets, ids, atoms1, own_back, near_back, second_gain, second_qkv, atom_bias)
    return call(
        functools.partial(second_edge, share=share, columns=col_count),
        atom_shape,
        edge_scratch,
        [SMEM, SMEM] + [VMEM] * 16,
        300_000_000,
        24,
    )(
        info, offsets, atoms2, near_atoms, far_atoms, near_acts, far_acts, own_back, near_back, far_back,
        second_gain, second_qkv, second_out, atom_bias, *mixed2,
    )


def solution(mesh):
    atoms = P(("group", "row", "col"))
    in_specs = (
        P(("group", "row", "col"), None),
        P(), P(), P(), P(), P(), P(),
        P(None, ("group", "row", "col"), None),
        atoms,
        atoms,
        P(), P(), P(), P(), P(),
        P(None, ("group", "row"), "col"),
    )
    out_specs = P(("group", "row", "col"), None)
    return jax.shard_map(body, mesh=mesh, in_specs=in_specs, out_specs=out_specs, check_vma=False)
```

```python
import functools
import math

import jax
import jax.numpy as jnp
from jax import lax
from jax.experimental import pallas as pl
from jax.experimental.pallas import tpu as pltpu
from jax.sharding import PartitionSpec as P

BF = jnp.bfloat16
F32 = jnp.float32
RIM = 64
LANES = 128
VMEM = pl.BlockSpec(memory_space=pltpu.VMEM)
SMEM = pl.BlockSpec(memory_space=pltpu.SMEM)
HBM = pl.BlockSpec(memory_space=pltpu.HBM)


def dot(a, b):
    return jnp.dot(a, b, preferred_element_type=F32)


def dot_nt(a, b):
    return lax.dot_general(a, b, (((1,), (1,)), ((), ())), preferred_element_type=F32)


def dot_tn(a, b):
    return lax.dot_general(a, b, (((0,), (0,)), ((), ())), preferred_element_type=F32)


def norm_rows(values, gain):
    center = values - jnp.mean(values, axis=-1, keepdims=True)
    spread = jnp.mean(center * center, axis=-1, keepdims=True)
    return center * lax.rsqrt(spread + 1e-05) * gain


def token_of(count, share, first_parity, dim=0):
    half = count // 2
    row = lax.broadcasted_iota(jnp.int32, (count, 1) if dim == 0 else (1, count), dim)
    second = (row >= half).astype(jnp.int32)
    inner = row - second * half
    shift = share.bit_length() - 1
    share_pair = inner >> shift
    inside = inner & (share - 1)
    parity = first_parity + second - 2 * first_parity * second
    return (2 * share_pair + parity) * share + inside


def one_hot(table_ids, atom_ids):
    return jnp.where(table_ids == atom_ids, 1.0, 0.0).astype(BF)


def project(rows, gain, qkv, q, k, v, at):
    channels = rows.shape[1]
    packed = dot(norm_rows(rows.astype(F32), gain).astype(BF), qkv).astype(BF)
    place = slice(at, at + rows.shape[0])
    q[place, :] = packed[:, :channels]
    k[place, :] = packed[:, channels : 2 * channels].astype(F32)
    v[place, :] = packed[:, 2 * channels :].astype(F32)


def attend_windows(places, bias, q, k, v, mixed):
    heads, _, span = bias.shape
    channels = q.shape[1]
    block = span - 3 * RIM // 2
    size = channels // heads
    scale = 1.0 / math.sqrt(size)
    stacked = heads * block
    head_row = lax.broadcasted_iota(jnp.int32, (heads, block, channels), 0).reshape(stacked, channels)
    head_lane = lax.broadcasted_iota(jnp.int32, (stacked, channels), 1) // size
    own_head = jnp.where(head_row == head_lane, 1.0, 0.0).astype(BF)
    lane_head = lax.broadcasted_iota(jnp.int32, (block, channels), 1) // size
    ones = jnp.ones((span, channels), BF)

    def picked(stack):
        out = stack[:block]
        for head in range(1, heads):
            out = jnp.where(lane_head == head, stack[head * block : (head + 1) * block], out)
        return out

    scores = []
    for query_at, _, key_at in places:
        spread = jnp.concatenate([q[pl.ds(query_at, block), :]] * heads, axis=0) * own_head
        scores.append(dot_nt(spread, k[pl.ds(key_at, span), :].astype(BF)))
    raised = []
    for (_, bias_at, _), score in zip(places, scores):
        tile = bias[:, pl.ds(bias_at, block), :].reshape(stacked, span).astype(F32)
        score = score * scale + tile
        raised.append(jnp.exp(score - jnp.max(score, axis=-1, keepdims=True)).astype(BF))
    for (query_at, _, key_at), weights in zip(places, raised):
        values = jnp.concatenate([v[pl.ds(key_at, span), :].astype(BF), ones], axis=1)
        out = dot(weights, values)
        mixed[pl.ds(query_at, block), :] = (picked(out[:, :channels]) / picked(out[:, channels:])).astype(BF)


class starts_from:
    def __init__(self, starts, base):
        self.starts, self.base, self.shape = starts, base, starts.shape

    def __getitem__(self, window):
        return self.starts[window] - self.base


def inner_windows(offsets, bias, q, k, v, mixed, edge_q, edge_k, edge_v):
    windows = offsets.shape[0]
    rows = q.shape[0]
    block = rows // windows
    edge = RIM // block
    group = next(size for size in (15, 12, 10, 6, 5, 4, 3, 2, 1) if (windows - 2 * edge) % size == 0)

    def one_group(step, carry):
        places = []
        for member in range(group):
            window = edge + step * group + member
            at = pl.multiple_of(window * block, block)
            places.append((at, at, offsets[window]))
        attend_windows(places, bias, q, k, v, mixed)
        return carry

    lax.fori_loop(0, (windows - 2 * edge) // group, one_group, 0)
    edge_q[:RIM, :] = q[:RIM, :]
    edge_q[RIM:, :] = q[rows - RIM :, :]
    for source, target in ((k, edge_k), (v, edge_v)):
        target[: 2 * RIM, :] = source[: 2 * RIM, :]
        target[2 * RIM :, :] = source[rows - 2 * RIM :, :]


def edge_windows(offsets, bias, gain, qkv, near, far, side, edge_q, edge_k, edge_v, k, v, mixed):
    windows = offsets.shape[0]
    rows = bias.shape[1]
    channels = edge_q.shape[1]
    block = rows // windows
    edge = RIM // block
    for source, target in ((edge_k, k), (edge_v, v)):
        target[RIM : 3 * RIM, :] = source[: 2 * RIM, :]
        target[3 * RIM : 5 * RIM, :] = source[2 * RIM :, :]
    normed = norm_rows(jnp.concatenate([near, far], axis=0), gain).astype(BF)
    packed = dot(normed, qkv[:, channels:]).astype(BF).astype(F32)
    near_at = pl.multiple_of(jnp.where(side == 0, 5 * RIM, 0), RIM)
    far_at = pl.multiple_of(5 * RIM - near_at, RIM)
    for at, part in ((near_at, packed[:RIM]), (far_at, packed[RIM:])):
        k[pl.ds(at, RIM), :] = part[:, :channels]
        v[pl.ds(at, RIM), :] = part[:, channels:]
    places = []
    for member in range(edge):
        places.append((member * block, member * block, offsets[member]))
    for member in range(edge):
        window = windows - edge + member
        places.append((RIM + member * block, window * block, offsets[window] - (rows - 4 * RIM)))
    attend_windows(places, bias, edge_q, k, v, mixed)


def fetches(sources, targets, sems, first=0):
    return [
        pltpu.make_async_copy(source, target, sems.at[first + index])
        for index, (source, target) in enumerate(zip(sources, targets))
    ]


def first_inner(
    info, acts_far, gain_far, qkv_far, bias_far, starts_far, mixed, edge_q, edge_k, edge_v,
    q, k, v, acts, gain, qkv, bias, starts, sems, *, pieces
):
    rows = acts.shape[0]
    part = rows // pieces
    cuts = [pl.ds(index * part, part) for index in range(pieces)]
    small = fetches([gain_far, qkv_far], [gain, qkv], sems)
    moving = fetches([acts_far.at[cut, :] for cut in cuts], [acts.at[cut, :] for cut in cuts], sems, 2)
    late = fetches([starts_far, bias_far], [starts, bias], sems, 2 + pieces)
    for copy in moving[:1] + small + moving[1:] + late:
        copy.start()
    for copy in small:
        copy.wait()
    step = 256
    for at in range(0, rows, step):
        if at % part == 0:
            moving[at // part].wait()
        project(acts[at : at + step, :], gain[...], qkv[...], q, k, v, at)
    for copy in late:
        copy.wait()
    inner_windows(starts_from(starts, info[4]), bias, q, k, v, mixed, edge_q, edge_k, edge_v)


def first_edge(
    info, offsets, ids, acts, near, far, gain, qkv, out_weight, bias, up, mixed, edge_q, edge_k, edge_v,
    atoms, send, keep, near_message, far_message, k, v, edge_mixed, *, share
):
    side = info[0]
    rows = acts.shape[0]
    edge_windows(
        starts_from(offsets, info[4] - RIM), bias, gain[...], qkv[...], near[...].astype(F32), far[...].astype(F32), side,
        edge_q, edge_k, edge_v, k, v, edge_mixed,
    )
    close_rows(acts, mixed, edge_mixed, out_weight, atoms)
    step = 256
    tokens = 2 * send.shape[0]
    half = tokens // 2
    head_ids = ids[:, :RIM]
    tail_ids = ids[:, rows - RIM :]
    for message, last in ((near_message, 1 - side), (far_message, side)):
        at = pl.multiple_of(last * (rows - RIM), RIM)
        message[:RIM, :] = atoms[pl.ds(at, RIM), :]
        sent = head_ids + last * (tail_ids - head_ids)
        coded = jnp.concatenate([sent >> 6, sent & 63], axis=1).astype(F32)
        message[RIM:, :] = jnp.broadcast_to(coded, (16, 2 * RIM)).astype(BF)
    member = one_hot(token_of(tokens, share, 1 - side) + info[1] * tokens, ids[...])
    wide = up.shape[1]
    atom_rows = atoms[...]
    for at in range(0, wide, step):
        feat = jnp.maximum(dot(atom_rows, up[:, at : at + step]), 0.0).astype(BF)
        sums = dot(member, feat).astype(BF)
        send[:, at : at + step] = sums[:half]
        keep[:, at : at + step] = sums[half:]
    count = dot(member, jnp.ones((rows, LANES), BF))
    high = jnp.floor(count * (1.0 / 64.0))
    low = count - 64.0 * high
    lane = lax.broadcasted_iota(jnp.int32, (tokens, LANES), 1)
    pieces = jnp.where(lane == 0, high, jnp.where(lane == 1, low, 0.0)).astype(BF)
    send[:, wide:] = pieces[:half]
    keep[:, wide:] = pieces[half:]


def close_rows(acts, mixed, edge_mixed, out_weight, out):
    rows = acts.shape[0]
    weight = out_weight[...]
    step = 256
    for at in range(0, rows, step):
        first, last = at, at + step
        pieces = [mixed[max(first, RIM) : min(last, rows - RIM), :]]
        if first == 0:
            pieces.insert(0, edge_mixed[:RIM, :])
        if last == rows:
            pieces.append(edge_mixed[RIM:, :])
        block = jnp.concatenate(pieces, axis=0)
        out[first:last, :] = (acts[first:last, :].astype(F32) + dot(block, weight)).astype(BF)


def mean_tokens(*refs, count):
    parts, gain, act, normed = refs[:count], refs[count], refs[count + 1], refs[count + 2]
    total = parts[0][...].astype(F32)
    for part in parts[1:]:
        total = total + part[...].astype(F32)
    wide = act.shape[1]
    atoms = total[:, wide : wide + 1] * 64.0 + total[:, wide + 1 : wide + 2]
    rounded = (total[:, :wide] / atoms).astype(BF)
    act[...] = rounded
    normed[...] = norm_rows(rounded.astype(F32), gain[...]).astype(BF)


def query_tokens(info, weight_far, gain, own_act, *refs, others):
    other_acts = refs[:others]
    act, queries, gates, query_weight, gate_weight, sems = refs[others:]
    share, wide = own_act.shape
    copies = fetches(
        [weight_far.at[:, pl.ds(0, wide)], weight_far.at[:, pl.ds(3 * wide, wide)]], [query_weight, gate_weight], sems
    )
    for copy in copies:
        copy.start()
    pairs = others + 1
    place = info[2]
    act[pl.ds(pl.multiple_of(place * share, share), share), :] = own_act[...]
    for step in range(1, pairs):
        at = lax.rem(place - step + pairs, pairs) * share
        act[pl.ds(pl.multiple_of(at, share), share), :] = other_acts[step - 1][...]
    normed = norm_rows(act[...].astype(F32), gain[...]).astype(BF)
    copies[0].wait()
    queries[...] = dot(normed, query_weight[...]).astype(BF)
    copies[1].wait()
    raw = dot(normed, gate_weight[...]).astype(BF).astype(F32)
    gates[...] = jax.nn.sigmoid(raw)


def place_keys(info, own, near, tokens):
    share = own[0].shape[0]
    group = LANES // share
    place = info[1] & (group - 1)
    for index, (own_rows, near_rows) in enumerate(zip(own, near)):
        at = index // group * 2 * LANES + (place ^ (index % group)) * share
        tokens[pl.ds(pl.multiple_of(at, share), share), :] = own_rows[...]
        tokens[pl.ds(pl.multiple_of(at + LANES, share), share), :] = near_rows[...]


def bias_pieces(info, biases_far, first, tile, share):
    count, blocks = tile.shape[1], tile.shape[2] // (2 * LANES)
    group = LANES // share
    side, row = info[0], info[1]
    sources, targets = [], []
    for block in range(blocks):
        slot = pl.multiple_of(((row // group) ^ (first + block)) * LANES, LANES)
        for half, bias_far in enumerate(biases_far):
            for pair in range(count // share):
                at = pl.multiple_of((2 * pair + side) * share, share)
                sources.append(bias_far.at[:, pl.ds(at, share), pl.ds(slot, LANES)])
                targets.append(tile.at[:, pl.ds(pair * share, share), pl.ds((2 * block + half) * LANES, LANES)])
    return sources, targets


def attend_heads(queries, bias, keys, values, previous, keep):
    count, wide = queries.shape
    heads = bias.shape[0]
    size = wide // heads
    scale = 1.0 / math.sqrt(size)
    span = keys.shape[0] // LANES
    lane = lax.broadcasted_iota(jnp.int32, (count, LANES), 1)
    out = [None] * (wide // LANES)
    together = 4
    for start in range(0, heads, together):
        members = []
        for head in range(start, start + together):
            first, last = head * size, (head + 1) * size
            low, high = first // LANES, -(-last // LANES)
            chunk = slice(low * LANES, high * LANES)
            chunk_lane = lax.broadcasted_iota(jnp.int32, (count, (high - low) * LANES), 1) + low * LANES
            inside = (chunk_lane >= first) & (chunk_lane < last)
            query = jnp.where(inside, queries[:, chunk].astype(F32), 0.0).astype(BF)
            members.append((head, first, low, high, dot_nt(query, keys[:, chunk])))
        raised = []
        for head, first, low, high, score in members:
            score = score * scale + bias[head].astype(F32)
            top = jnp.broadcast_to(jnp.max(score, axis=-1, keepdims=True), (count, LANES))
            if previous is not None:
                former = previous[1][head]
                top = jnp.maximum(top, former)
            weights = jnp.exp(score - jnp.concatenate([top] * span, axis=1))
            total = jnp.broadcast_to(jnp.sum(weights, axis=-1, keepdims=True), (count, LANES))
            fade = None
            if previous is not None:
                fade = jnp.exp(former - top)
                total = total + fade * previous[2][head]
            keep(head, top, total)
            raised.append((weights.astype(BF), fade, total))
        for (head, first, low, high, _), (weights, fade, total) in zip(members, raised):
            mixed = dot(weights, values[:, low * LANES : high * LANES])
            if previous is not None:
                inverse = 1.0 / total
            for block in range(low, high):
                piece = mixed[:, (block - low) * LANES : (block - low + 1) * LANES]
                if previous is not None:
                    piece = (piece + fade * previous[0][:, block * LANES : (block + 1) * LANES]) * inverse
                if out[block] is not None:
                    piece = jnp.where(lane + block * LANES >= first, piece, out[block])
                out[block] = piece
    return out


def attend_first(info, weight_far, queries, own_far, near_far, *refs, rows_count):
    own, near = refs[:rows_count], refs[rows_count : 2 * rows_count]
    key_weight, value_weight, rest_bias, mixed, tops, totals, tokens, keys, values, bias, sems = refs[2 * rows_count :]
    share, wide = own[0].shape
    weights = fetches(
        [weight_far.at[:, pl.ds(wide, wide)], weight_far.at[:, pl.ds(2 * wide, wide)]], [key_weight, value_weight], sems
    )
    now = fetches(*bias_pieces(info, (own_far, near_far), 0, bias, share), sems, 2)
    later = fetches(*bias_pieces(info, (own_far, near_far), 1, rest_bias, share), sems, 2 + len(now))
    for copy in weights + now + later:
        copy.start()
    place_keys(info, own, near, tokens)
    weights[0].wait()
    keys[...] = dot(tokens[...], key_weight[...]).astype(BF)
    weights[1].wait()
    values[...] = dot(tokens[...], value_weight[...]).astype(BF)
    for copy in now:
        copy.wait()

    def keep(head, top, total):
        tops[head] = top
        totals[head] = total

    out = attend_heads(queries, bias, keys, values, None, keep)
    for block, piece in enumerate(out):
        mixed[:, block * LANES : (block + 1) * LANES] = piece
    for copy in later:
        copy.wait()


def attend_rest(queries, key_weight, value_weight, bias, info, former, former_top, former_total, *refs, rows_count):
    own, near = refs[:rows_count], refs[rows_count : 2 * rows_count]
    packed, tokens, keys, values = refs[2 * rows_count :]
    heads = bias.shape[0]
    count, wide = queries.shape
    place_keys(info, own, near, tokens)
    keys[...] = dot(tokens[...], key_weight[...]).astype(BF)
    values[...] = dot(tokens[...], value_weight[...]).astype(BF)
    lane = lax.broadcasted_iota(jnp.int32, (count, LANES), 1)
    ends = [jnp.zeros((count, LANES), F32), jnp.ones((count, LANES), F32)]

    def keep(head, top, total):
        ends[0] = jnp.where(lane == head, top, ends[0])
        ends[1] = jnp.where(lane == head, total, ends[1])

    out = attend_heads(queries, bias, keys, values, (former, former_top, former_total), keep)
    for block, piece in enumerate(out):
        packed[:, block * LANES : (block + 1) * LANES] = piece.astype(BF)
    logs = ends[0] + jnp.log(ends[1])
    first = logs.astype(BF).astype(F32)
    rest = logs - first
    second = rest.astype(BF).astype(F32)
    rest = rest - second
    packed[:, wide:] = (first + pltpu.roll(second, heads, 1) + pltpu.roll(rest, 2 * heads, 1)).astype(BF)


def finish_tokens(act, gates, token_out, down, *refs, parts_count):
    parts, back = refs[:parts_count], refs[parts_count]
    count, wide = act.shape
    heads = 16
    size = wide // heads
    logs = []
    for part in parts:
        packed = part[:, wide:].astype(F32)
        logs.append(
            packed + pltpu.roll(packed, LANES - heads, 1) + pltpu.roll(packed, LANES - 2 * heads, 1)
        )
    top = functools.reduce(jnp.maximum, logs)
    weights = [jnp.exp(log - top) for log in logs]
    total = functools.reduce(jnp.add, weights)
    head = lax.broadcasted_iota(jnp.int32, (LANES, wide), 0)
    feature = lax.broadcasted_iota(jnp.int32, (LANES, wide), 1)
    expand = jnp.where((feature >= head * size) & (feature < (head + 1) * size), 1.0, 0.0).astype(BF)
    mixed = jnp.zeros((count, wide), F32)
    for part, weight in zip(parts, weights):
        factor = weight / total
        coarse = factor.astype(BF)
        fine = (factor - coarse.astype(F32)).astype(BF)
        mixed = mixed + (dot(coarse, expand) + dot(fine, expand)) * part[:, :wide].astype(F32)
    gated = (mixed * gates[...]).astype(BF)
    result = (act[...].astype(F32) + dot(gated, token_out[...])).astype(BF)
    back[...] = dot(result, down[...]).astype(BF)


def second_inner(
    info, offsets, ids, atoms1, own_back, near_back, gain, qkv, bias,
    atoms2, mixed, edge_q, edge_k, edge_v, q, k, v, *, share
):
    tokens = 2 * own_back.shape[0]
    table = jnp.concatenate([own_back[...], near_back[...]], axis=0)
    table_ids = (token_of(tokens, share, info[0], 1) + info[1] * tokens).astype(F32)
    step = 256
    for at in range(0, atoms1.shape[0], step):
        members = []
        for first in range(at, at + step, LANES):
            atom_ids = jnp.broadcast_to(ids[:, first : first + LANES].astype(F32), (LANES, LANES)).T
            members.append(
                jnp.concatenate(
                    [one_hot(table_ids[:, t : t + LANES], atom_ids) for t in range(0, tokens, LANES)], axis=1
                )
            )
        member = jnp.concatenate(members, axis=0)
        moved = (atoms1[at : at + step, :].astype(F32) + dot(member, table)).astype(BF)
        atoms2[at : at + step, :] = moved
        project(moved, gain[...], qkv[...], q, k, v, at)
    inner_windows(starts_from(offsets, info[4]), bias, q, k, v, mixed, edge_q, edge_k, edge_v)


def second_edge(
    info, offsets, atoms2, near, far, own_back, near_back, far_back, gain, qkv, out_weight, bias,
    mixed, edge_q, edge_k, edge_v, result, k, v, edge_mixed, *, share, columns
):
    side, column = info[0], info[3]
    tokens = 2 * own_back.shape[0]
    table = jnp.concatenate([own_back[...], near_back[...]], axis=0)
    table_ids = token_of(tokens, share, side)
    first_token = (info[1] * tokens).astype(F32)

    def rim_ids(message):
        packed = message[RIM:, :].astype(F32)
        return (packed[0:1, :RIM] * 64.0 + packed[0:1, RIM:] - first_token).astype(jnp.int32)

    near_rows = near[:RIM, :].astype(F32) + dot_tn(one_hot(table_ids, rim_ids(near)), table)
    far_token = rim_ids(far)
    beyond = lax.broadcasted_iota(jnp.int32, (RIM, 1), 0) + jnp.where(
        column == 0, -RIM, jnp.where(column == columns - 1, tokens, 4 * tokens)
    )
    far_rows = (
        far[:RIM, :].astype(F32)
        + dot_tn(one_hot(table_ids, far_token), table)
        + dot_tn(one_hot(beyond, far_token), far_back[...])
    )
    edge_windows(
        starts_from(offsets, info[4] - RIM), bias, gain[...], qkv[...], near_rows.astype(BF).astype(F32), far_rows.astype(BF).astype(F32), side,
        edge_q, edge_k, edge_v, k, v, edge_mixed,
    )
    close_rows(atoms2, mixed, edge_mixed, out_weight, result)


def stay(x):
    return pltpu.with_memory_space_constraint(x, pltpu.HBM)


def call(kernel, outs, scratch, specs, flops, limit=20):
    return pl.pallas_call(
        kernel,
        out_shape=outs,
        in_specs=specs,
        out_specs=jax.tree.map(lambda _: VMEM, outs),
        scratch_shapes=scratch,
        compiler_params=pltpu.CompilerParams(vmem_limit_bytes=limit * 1024 * 1024),
        cost_estimate=pl.CostEstimate(flops=flops, bytes_accessed=1_000, transcendentals=1_000),
    )


def body(
    atom_acts, first_gain, first_qkv, first_out, second_gain, second_qkv, second_out, atom_bias, window_start,
    atom_token, up_weight, token_gain, token_weight, token_out, down_weight, pair_bias,
):
    rows, channels = atom_acts.shape
    heads, tok_rows, slots = pair_bias.shape
    wide = token_weight.shape[0]
    row_count, col_count = lax.axis_size("row"), lax.axis_size("col")
    pairs = col_count // 2
    share = tok_rows // col_count
    half = tok_rows // 2
    row, col = lax.axis_index("row"), lax.axis_index("col")
    side, pair = col % 2, col // 2
    info = jnp.stack([side, row, pair, col, (row * col_count + col) * rows]).astype(jnp.int32)
    devices = row_count * col_count

    def to_near(x):
        return lax.ppermute(x, "col", [(i, i ^ 1) for i in range(col_count)])

    def to_far(x):
        swap = [(i, i + 1 if i % 2 else i - 1) for i in range(1, devices - 1)]
        swap = [(0, 0)] + swap + [(devices - 1, devices - 1)]
        return lax.ppermute(x, ("row", "col"), swap)

    def along_pairs(x, step):
        return lax.ppermute(
            x, "col", [(2 * i + k, 2 * ((i + step) % pairs) + k) for i in range(pairs) for k in range(2)]
        )

    def along_rows(x, step):
        return lax.ppermute(x, "row", [(i, i ^ step) for i in range(row_count)])

    def rim_of(x, last):
        return lax.dynamic_slice_in_dim(x, jnp.where(last, rows - RIM, 0), RIM, axis=0)

    near_acts = to_near(rim_of(atom_acts, side == 0))
    far_acts = to_far(rim_of(atom_acts, side == 1))

    ids = atom_token.reshape(1, rows)
    inner_scratch = [
        pltpu.VMEM((rows, channels), BF),
        pltpu.VMEM((rows, channels), F32),
        pltpu.VMEM((rows, channels), F32),
    ]
    edge_scratch = [
        pltpu.VMEM((6 * RIM, channels), F32),
        pltpu.VMEM((6 * RIM, channels), F32),
        pltpu.VMEM((2 * RIM, channels), BF),
    ]
    atom_shape = jax.ShapeDtypeStruct((rows, channels), BF)
    edge_shapes = [
        jax.ShapeDtypeStruct((2 * RIM, channels), BF),
        jax.ShapeDtypeStruct((4 * RIM, channels), F32),
        jax.ShapeDtypeStruct((4 * RIM, channels), F32),
    ]
    packed_shape = jax.ShapeDtypeStruct((half, wide + LANES), BF)
    first_gain, second_gain = first_gain.reshape(1, -1), second_gain.reshape(1, -1)
    pieces = 4
    first_args = [atom_acts, first_gain, first_qkv, atom_bias]
    mixed1 = call(
        functools.partial(first_inner, pieces=pieces),
        [atom_shape] + edge_shapes,
        inner_scratch
        + [pltpu.VMEM(x.shape, x.dtype) for x in first_args]
        + [pltpu.SMEM(window_start.shape, jnp.int32), pltpu.SemaphoreType.DMA((4 + pieces,))],
        [SMEM] + [HBM] * 5,
        1_500_000_000,
        16,
    )(info, *map(stay, first_args), stay(window_start))
    message_shape = jax.ShapeDtypeStruct((RIM + 16, channels), BF)
    atoms1, send, keep, near_message, far_message = call(
        functools.partial(first_edge, share=share),
        [atom_shape, packed_shape, packed_shape, message_shape, message_shape],
        edge_scratch,
        [SMEM, SMEM] + [VMEM] * 13,
        2_000_000_000,
        16,
    )(
        info, window_start, ids, atom_acts, near_acts, far_acts, first_gain, first_qkv, first_out,
        atom_bias, up_weight, *mixed1,
    )

    chip_sum = (keep.astype(F32) + to_near(send).astype(F32)).astype(BF)
    chip_sum, near_bias = lax.optimization_barrier((chip_sum, pair_bias))
    bias_near = to_near(near_bias)
    sums = [lax.dynamic_slice_in_dim(chip_sum, pair * share, share, axis=0)]
    for step in range(1, pairs):
        piece = lax.dynamic_slice_in_dim(chip_sum, (pair + step) % pairs * share, share, axis=0)
        sums.append(along_pairs(piece, step))
    share_shape = jax.ShapeDtypeStruct((share, wide), BF)
    gain_row = token_gain.reshape(1, -1)
    act, normed = call(
        functools.partial(mean_tokens, count=len(sums)), [share_shape] * 2, [], [VMEM] * (len(sums) + 1), 1_000_000
    )(*sums, gain_row)

    group = LANES // share
    own_keys = [normed] + [along_rows(normed, step) for step in range(1, row_count)]
    near_keys = [to_near(x) for x in own_keys[:group]]
    other_acts = [along_pairs(act, step) for step in range(1, pairs)]
    half_shape = jax.ShapeDtypeStruct((half, wide), BF)
    wide_shape = jax.ShapeDtypeStruct((half, wide), F32)
    act_rows, queries, gates = call(
        functools.partial(query_tokens, others=len(other_acts)),
        [half_shape, half_shape, wide_shape],
        [pltpu.VMEM((wide, wide), BF)] * 2 + [pltpu.SemaphoreType.DMA((2,))],
        [SMEM, HBM] + [VMEM] * (2 + len(other_acts)),
        1_000,
    )(info, stay(token_weight), gain_row, act, *other_acts)

    rest = row_count - group

    def key_scratch(count):
        keys = 2 * count * share
        return [pltpu.VMEM((keys, wide), BF)] * 3

    head_shape = jax.ShapeDtypeStruct((heads, half, LANES), F32)
    weight_shape = jax.ShapeDtypeStruct((wide, wide), BF)
    pieces = 2 * pairs * (row_count // group)
    *held, mixed, tops, totals = call(
        functools.partial(attend_first, rows_count=group),
        [weight_shape, weight_shape, jax.ShapeDtypeStruct((heads, half, 2 * rest * share), BF)]
        + [wide_shape, head_shape, head_shape],
        key_scratch(group) + [pltpu.VMEM((heads, half, 2 * LANES), BF), pltpu.SemaphoreType.DMA((2 + pieces,))],
        [SMEM, HBM, VMEM, HBM, HBM] + [VMEM] * (2 * group),
        1_000,
    )(info, stay(token_weight), queries, stay(pair_bias), stay(bias_near), *own_keys[:group], *near_keys)
    rest_keys, mixed = lax.optimization_barrier((own_keys[group:], mixed))
    rest_near = [to_near(x) for x in rest_keys]
    part = call(
        functools.partial(attend_rest, rows_count=rest),
        packed_shape,
        key_scratch(rest),
        [VMEM] * 4 + [SMEM] + [VMEM] * (3 + 2 * rest),
        2_000_000_000,
    )(queries, *held, info, mixed, tops, totals, *rest_keys, *rest_near)

    near_message, far_message, part = lax.optimization_barrier((near_message, far_message, part))
    parts = [along_pairs(part, step) for step in range(1, pairs)]
    near_message, far_message, parts = lax.optimization_barrier(
        (to_near(near_message), to_far(far_message), parts)
    )
    parts = [part] + parts
    own_back = call(
        functools.partial(finish_tokens, parts_count=pairs),
        jax.ShapeDtypeStruct((half, channels), BF),
        [],
        [VMEM] * (4 + pairs),
        200_000_000,
    )(act_rows, gates, token_out, down_weight, *parts)

    near_back = to_near(own_back)
    if share >= RIM:
        last_rows = own_back[half - RIM :]
        first_rows = own_back[:RIM]
    else:
        both = jnp.where(side == 0, jnp.stack([own_back, near_back]), jnp.stack([near_back, own_back]))
        both = both.reshape(2, pairs, share, channels).transpose(1, 0, 2, 3).reshape(tok_rows, channels)
        last_rows = both[tok_rows - RIM :]
        first_rows = both[:RIM]
    far_back = to_far(jnp.where(side == 1, last_rows, first_rows))

    atoms2, *mixed2 = call(
        functools.partial(second_inner, share=share),
        [atom_shape, atom_shape] + edge_shapes,
        inner_scratch,
        [SMEM, SMEM] + [VMEM] * 7,
        1_500_000_000,
        16,
    )(info, window_start, ids, atoms1, own_back, near_back, second_gain, second_qkv, atom_bias)
    return call(
        functools.partial(second_edge, share=share, columns=col_count),
        atom_shape,
        edge_scratch,
        [SMEM, SMEM] + [VMEM] * 14,
        300_000_000,
        16,
    )(
        info, window_start, atoms2, near_message, far_message, own_back, near_back, far_back,
        second_gain, second_qkv, second_out, atom_bias, *mixed2,
    )


def solution(mesh):
    atoms = P(("group", "row", "col"))
    in_specs = (
        P(("group", "row", "col"), None),
        P(), P(), P(), P(), P(), P(),
        P(None, ("group", "row", "col"), None),
        atoms,
        atoms,
        P(), P(), P(), P(), P(),
        P(None, ("group", "row"), "col"),
    )
    out_specs = P(("group", "row", "col"), None)
    return jax.shard_map(body, mesh=mesh, in_specs=in_specs, out_specs=out_specs, check_vma=False)
```

```python
import functools
import math

import jax
import jax.numpy as jnp
from jax import lax
from jax.experimental import pallas as pl
from jax.experimental.pallas import tpu as pltpu
from jax.sharding import PartitionSpec as P

BF = jnp.bfloat16
F32 = jnp.float32
RIM = 64
LANES = 128
VMEM = pl.BlockSpec(memory_space=pltpu.VMEM)
SMEM = pl.BlockSpec(memory_space=pltpu.SMEM)
HBM = pl.BlockSpec(memory_space=pltpu.HBM)


def dot(a, b):
    return jnp.dot(a, b, preferred_element_type=F32)


def dot_nt(a, b):
    return lax.dot_general(a, b, (((1,), (1,)), ((), ())), preferred_element_type=F32)


def dot_tn(a, b):
    return lax.dot_general(a, b, (((0,), (0,)), ((), ())), preferred_element_type=F32)


def norm_rows(values, gain):
    center = values - jnp.mean(values, axis=-1, keepdims=True)
    spread = jnp.mean(center * center, axis=-1, keepdims=True)
    return center * lax.rsqrt(spread + 1e-05) * gain


def token_of(count, share, first_parity, dim=0):
    half = count // 2
    row = lax.broadcasted_iota(jnp.int32, (count, 1) if dim == 0 else (1, count), dim)
    second = (row >= half).astype(jnp.int32)
    inner = row - second * half
    shift = share.bit_length() - 1
    share_pair = inner >> shift
    inside = inner & (share - 1)
    parity = first_parity + second - 2 * first_parity * second
    return (2 * share_pair + parity) * share + inside


def one_hot(table_ids, atom_ids):
    return jnp.where(table_ids == atom_ids, 1.0, 0.0).astype(BF)


def project(rows, gain, qkv, q, k, v, at):
    channels = rows.shape[1]
    packed = dot(norm_rows(rows.astype(F32), gain).astype(BF), qkv).astype(BF)
    place = slice(at, at + rows.shape[0])
    q[place, :] = packed[:, :channels]
    k[place, :] = packed[:, channels : 2 * channels].astype(F32)
    v[place, :] = packed[:, 2 * channels :].astype(F32)


def attend_windows(places, bias, q, k, v, mixed):
    heads, _, span = bias.shape
    channels = q.shape[1]
    block = span - 3 * RIM // 2
    size = channels // heads
    scale = 1.0 / math.sqrt(size)
    stacked = heads * block
    head_row = lax.broadcasted_iota(jnp.int32, (heads, block, channels), 0).reshape(stacked, channels)
    head_lane = lax.broadcasted_iota(jnp.int32, (stacked, channels), 1) // size
    own_head = jnp.where(head_row == head_lane, 1.0, 0.0).astype(BF)
    lane_head = lax.broadcasted_iota(jnp.int32, (block, channels), 1) // size
    ones = jnp.ones((span, channels), BF)

    def picked(stack):
        out = stack[:block]
        for head in range(1, heads):
            out = jnp.where(lane_head == head, stack[head * block : (head + 1) * block], out)
        return out

    scores = []
    for query_at, _, key_at in places:
        spread = jnp.concatenate([q[pl.ds(query_at, block), :]] * heads, axis=0) * own_head
        scores.append(dot_nt(spread, k[pl.ds(key_at, span), :].astype(BF)))
    raised = []
    for (_, bias_at, _), score in zip(places, scores):
        tile = bias[:, pl.ds(bias_at, block), :].reshape(stacked, span).astype(F32)
        score = score * scale + tile
        raised.append(jnp.exp(score - jnp.max(score, axis=-1, keepdims=True)).astype(BF))
    for (query_at, _, key_at), weights in zip(places, raised):
        values = jnp.concatenate([v[pl.ds(key_at, span), :].astype(BF), ones], axis=1)
        out = dot(weights, values)
        mixed[pl.ds(query_at, block), :] = (picked(out[:, :channels]) / picked(out[:, channels:])).astype(BF)


class starts_from:
    def __init__(self, starts, base):
        self.starts, self.base, self.shape = starts, base, starts.shape

    def __getitem__(self, window):
        return self.starts[window] - self.base


def window_group(windows, edge):
    return next(size for size in (15, 12, 10, 6, 5, 4, 3, 2, 1) if (windows - 2 * edge) % size == 0)


def inner_windows(offsets, bias, q, k, v, mixed, edge_q, edge_k, edge_v, ready=None):
    windows = offsets.shape[0]
    rows = q.shape[0]
    block = rows // windows
    edge = RIM // block
    group = window_group(windows, edge)

    def one_group(step, carry):
        if ready is not None:
            ready(step)
        places = []
        for member in range(group):
            window = edge + step * group + member
            at = pl.multiple_of(window * block, block)
            places.append((at, at, offsets[window]))
        attend_windows(places, bias, q, k, v, mixed)
        return carry

    lax.fori_loop(0, (windows - 2 * edge) // group, one_group, 0)
    edge_q[:RIM, :] = q[:RIM, :]
    edge_q[RIM:, :] = q[rows - RIM :, :]
    for source, target in ((k, edge_k), (v, edge_v)):
        target[: 2 * RIM, :] = source[: 2 * RIM, :]
        target[2 * RIM :, :] = source[rows - 2 * RIM :, :]


def edge_windows(offsets, bias, gain, qkv, near, far, side, edge_q, edge_k, edge_v, k, v, mixed):
    windows = offsets.shape[0]
    channels = edge_q.shape[1]
    block = bias.shape[2] - 3 * RIM // 2
    rows = windows * block
    edge = RIM // block
    for source, target in ((edge_k, k), (edge_v, v)):
        target[RIM : 3 * RIM, :] = source[: 2 * RIM, :]
        target[3 * RIM : 5 * RIM, :] = source[2 * RIM :, :]
    normed = norm_rows(jnp.concatenate([near, far], axis=0), gain).astype(BF)
    packed = dot(normed, qkv[:, channels:]).astype(BF).astype(F32)
    near_at = pl.multiple_of(jnp.where(side == 0, 5 * RIM, 0), RIM)
    far_at = pl.multiple_of(5 * RIM - near_at, RIM)
    for at, part in ((near_at, packed[:RIM]), (far_at, packed[RIM:])):
        k[pl.ds(at, RIM), :] = part[:, :channels]
        v[pl.ds(at, RIM), :] = part[:, channels:]
    places = []
    for member in range(edge):
        places.append((member * block, member * block, offsets[member]))
    for member in range(edge):
        window = windows - edge + member
        at = RIM + member * block
        places.append((at, at, offsets[window] - (rows - 4 * RIM)))
    attend_windows(places, bias, edge_q, k, v, mixed)


def fetches(sources, targets, sems, first=0):
    return [
        pltpu.make_async_copy(source, target, sems.at[first + index])
        for index, (source, target) in enumerate(zip(sources, targets))
    ]


def first_inner(
    info, acts_far, gain_far, qkv_far, starts_far, bias_far, mixed, edge_q, edge_k, edge_v, edge_bias,
    q, k, v, acts, gain, qkv, starts, bias, sems, bias_sems, *, pieces
):
    rows = acts.shape[0]
    windows = starts.shape[0]
    block = rows // windows
    span = window_group(windows, RIM // block) * block
    part = rows // pieces
    cuts = [pl.ds(index * part, part) for index in range(pieces)]
    small = fetches([gain_far, qkv_far, starts_far], [gain, qkv, starts], sems)
    moving = fetches([acts_far.at[cut, :] for cut in cuts], [acts.at[cut, :] for cut in cuts], sems, 3)
    ends = fetches(
        [bias_far.at[:, pl.ds(at, RIM), :] for at in (0, rows - RIM)],
        [edge_bias.at[:, pl.ds(at, RIM), :] for at in (0, RIM)],
        sems,
        3 + pieces,
    )

    def tile(step):
        place = pl.ds(pl.multiple_of(RIM + step * span, block), span)
        return pltpu.make_async_copy(bias_far.at[:, place, :], bias.at[:, place, :], bias_sems.at[step])

    for copy in moving[:1] + small + moving[1:]:
        copy.start()
    for copy in small:
        copy.wait()
    step = 256
    for index, copy in enumerate(moving):
        copy.wait()
        if index == 0:
            for group in range(bias_sems.shape[0]):
                tile(group).start()
            for end in ends:
                end.start()
        for at in range(index * part, (index + 1) * part, step):
            project(acts[at : at + step, :], gain[...], qkv[...], q, k, v, at)
    inner_windows(
        starts_from(starts, info[4]), bias, q, k, v, mixed, edge_q, edge_k, edge_v, lambda index: tile(index).wait()
    )
    for end in ends:
        end.wait()


def first_edge(
    info, offsets, ids, acts, near, far, gain, qkv, out_weight, up, mixed, edge_q, edge_k, edge_v, bias,
    atoms, send, keep, near_message, far_message, k, v, edge_mixed, *, share
):
    side = info[0]
    rows = acts.shape[0]
    close_inner(acts, mixed, out_weight, atoms)
    edge_windows(
        starts_from(offsets, info[4] - RIM), bias, gain[...], qkv[...], near[...].astype(F32), far[...].astype(F32), side,
        edge_q, edge_k, edge_v, k, v, edge_mixed,
    )
    close_edge(acts, edge_mixed, out_weight, atoms)
    step = 256
    tokens = 2 * send.shape[0]
    half = tokens // 2
    head_ids = ids[:, :RIM]
    tail_ids = ids[:, rows - RIM :]
    for message, last in ((near_message, 1 - side), (far_message, side)):
        at = pl.multiple_of(last * (rows - RIM), RIM)
        message[:RIM, :] = atoms[pl.ds(at, RIM), :]
        sent = head_ids + last * (tail_ids - head_ids)
        coded = jnp.concatenate([sent >> 6, sent & 63], axis=1).astype(F32)
        message[RIM:, :] = jnp.broadcast_to(coded, (16, 2 * RIM)).astype(BF)
    member = one_hot(token_of(tokens, share, 1 - side) + info[1] * tokens, ids[...])
    wide = up.shape[1]
    atom_rows = atoms[...]
    for at in range(0, wide, step):
        feat = jnp.maximum(dot(atom_rows, up[:, at : at + step]), 0.0).astype(BF)
        sums = dot(member, feat).astype(BF)
        send[:, at : at + step] = sums[:half]
        keep[:, at : at + step] = sums[half:]
    count = dot(member, jnp.ones((rows, LANES), BF))
    high = jnp.floor(count * (1.0 / 64.0))
    low = count - 64.0 * high
    lane = lax.broadcasted_iota(jnp.int32, (tokens, LANES), 1)
    pieces = jnp.where(lane == 0, high, jnp.where(lane == 1, low, 0.0)).astype(BF)
    send[:, wide:] = pieces[:half]
    keep[:, wide:] = pieces[half:]


def close_inner(acts, mixed, out_weight, out):
    rows = acts.shape[0]
    step = 256
    for at in range(0, rows, step):
        first, last = max(at, RIM), min(at + step, rows - RIM)
        part = acts[first:last, :].astype(F32) + dot(mixed[first:last, :], out_weight[...])
        out[first:last, :] = part.astype(BF)


def close_edge(acts, mixed, out_weight, out):
    rows = acts.shape[0]
    moved = dot(mixed[...], out_weight[...])
    out[:RIM, :] = (acts[:RIM, :].astype(F32) + moved[:RIM]).astype(BF)
    out[rows - RIM :, :] = (acts[rows - RIM :, :].astype(F32) + moved[RIM:]).astype(BF)


def mean_tokens(*refs, count):
    parts, gain, act, normed = refs[:count], refs[count], refs[count + 1], refs[count + 2]
    total = parts[0][...].astype(F32)
    for part in parts[1:]:
        total = total + part[...].astype(F32)
    wide = act.shape[1]
    atoms = total[:, wide : wide + 1] * 64.0 + total[:, wide + 1 : wide + 2]
    rounded = (total[:, :wide] / atoms).astype(BF)
    act[...] = rounded
    normed[...] = norm_rows(rounded.astype(F32), gain[...]).astype(BF)


def query_tokens(info, weight_far, gain, own_act, *refs, others):
    other_acts = refs[:others]
    act, queries, gates, query_weight, gate_weight, sems = refs[others:]
    share, wide = own_act.shape
    copies = fetches(
        [weight_far.at[:, pl.ds(0, wide)], weight_far.at[:, pl.ds(3 * wide, wide)]], [query_weight, gate_weight], sems
    )
    for copy in copies:
        copy.start()
    pairs = others + 1
    place = info[2]
    act[pl.ds(pl.multiple_of(place * share, share), share), :] = own_act[...]
    for step in range(1, pairs):
        at = lax.rem(place - step + pairs, pairs) * share
        act[pl.ds(pl.multiple_of(at, share), share), :] = other_acts[step - 1][...]
    normed = norm_rows(act[...].astype(F32), gain[...]).astype(BF)
    copies[0].wait()
    queries[...] = dot(normed, query_weight[...]).astype(BF)
    copies[1].wait()
    raw = dot(normed, gate_weight[...]).astype(BF).astype(F32)
    gates[...] = jax.nn.sigmoid(raw)


def place_keys(info, own, near, tokens, steps, solo):
    share = own[0].shape[0]
    group = LANES // share
    place = info[1] & (group - 1)
    lead = 2 * share if solo else 0
    for own_rows, near_rows, step in zip(own, near, steps):
        if solo and step < group:
            places = (0, share)
        else:
            at = lead + (step // group - (steps[0] + solo) // group) * 2 * LANES + (place ^ (step % group)) * share
            places = (at, at + LANES)
        for rows, at in zip((own_rows, near_rows), places):
            tokens[pl.ds(pl.multiple_of(at, share), share), :] = rows[...]


def bias_pieces(info, biases_far, block, targets, share):
    count = targets[0].shape[1]
    group = LANES // share
    side, row = info[0], info[1]
    slot = pl.multiple_of(((row // group) ^ block) * LANES, LANES)
    sources, places = [], []
    for bias_far, target in zip(biases_far, targets):
        for pair in range(count // share):
            at = pl.multiple_of((2 * pair + side) * share, share)
            sources.append(bias_far.at[:, pl.ds(at, share), pl.ds(slot, LANES)])
            places.append(target.at[:, pl.ds(pair * share, share), :])
    return sources, places


def split_bias(info, slots, bias, rest):
    heads, count = bias.shape[0], bias.shape[1]
    lane = lax.broadcasted_iota(jnp.int32, (count, LANES), 1)
    lower = lane < LANES // 2
    first = info[1] & 1
    for head in range(heads):
        own, near = slots[0, head].astype(F32), slots[1, head].astype(F32)
        low = jnp.where(lower, own, pltpu.roll(near, LANES // 2, 1))
        high = jnp.where(lower, pltpu.roll(own, LANES // 2, 1), near)
        bias[head] = jnp.where(first == 0, low, high).astype(BF)
        rest[head, :, :LANES] = jnp.where(first == 0, high, low).astype(BF)


def attend_heads(queries, bias, keys, values, previous, keep):
    count, wide = queries.shape
    heads = bias.shape[0]
    size = wide // heads
    scale = 1.0 / math.sqrt(size)
    span = keys.shape[0] // LANES
    lane = lax.broadcasted_iota(jnp.int32, (count, LANES), 1)
    out = [None] * (wide // LANES)
    together = 4
    for start in range(0, heads, together):
        members = []
        for head in range(start, start + together):
            first, last = head * size, (head + 1) * size
            low, high = first // LANES, -(-last // LANES)
            chunk = slice(low * LANES, high * LANES)
            chunk_lane = lax.broadcasted_iota(jnp.int32, (count, (high - low) * LANES), 1) + low * LANES
            inside = (chunk_lane >= first) & (chunk_lane < last)
            query = jnp.where(inside, queries[:, chunk].astype(F32), 0.0).astype(BF)
            members.append((head, first, low, high, dot_nt(query, keys[:, chunk])))
        raised = []
        for head, first, low, high, score in members:
            score = score * scale + bias[head].astype(F32)
            top = jnp.broadcast_to(jnp.max(score, axis=-1, keepdims=True), (count, LANES))
            if previous is not None:
                former = previous[1][head]
                top = jnp.maximum(top, former)
            weights = jnp.exp(score - jnp.concatenate([top] * span, axis=1))
            total = jnp.broadcast_to(jnp.sum(weights, axis=-1, keepdims=True), (count, LANES))
            fade = None
            if previous is not None:
                fade = jnp.exp(former - top)
                total = total + fade * previous[2][head]
            keep(head, top, total)
            raised.append((weights.astype(BF), fade, total))
        for (head, first, low, high, _), (weights, fade, total) in zip(members, raised):
            mixed = dot(weights, values[:, low * LANES : high * LANES])
            if previous is not None:
                inverse = 1.0 / total
            for block in range(low, high):
                piece = mixed[:, (block - low) * LANES : (block - low + 1) * LANES]
                if previous is not None:
                    piece = (piece + fade * previous[0][:, block * LANES : (block + 1) * LANES]) * inverse
                if out[block] is not None:
                    piece = jnp.where(lane + block * LANES >= first, piece, out[block])
                out[block] = piece
    return out


def attend_first(info, weight_far, queries, own_far, near_far, *refs, steps, solo):
    rows_count = len(steps)
    own, near = refs[:rows_count], refs[rows_count : 2 * rows_count]
    key_weight, value_weight, rest_bias, mixed, tops, totals, tokens, keys, values, bias, slots, sems = refs[
        2 * rows_count :
    ]
    share, wide = own[0].shape
    weights = fetches(
        [weight_far.at[:, pl.ds(wide, wide)], weight_far.at[:, pl.ds(2 * wide, wide)]], [key_weight, value_weight], sems
    )
    biases_far = (own_far, near_far)
    targets = (slots.at[0], slots.at[1]) if solo else [bias.at[:, :, pl.ds(at, LANES)] for at in (0, LANES)]
    now = fetches(*bias_pieces(info, biases_far, 0, targets, share), sems, 2)
    later = []
    lead = LANES if solo else 0
    for block in range((rest_bias.shape[2] - lead) // (2 * LANES)):
        first = lead + block * 2 * LANES
        targets = [rest_bias.at[:, :, pl.ds(at, LANES)] for at in (first, first + LANES)]
        sources, places = bias_pieces(info, biases_far, block + 1, targets, share)
        later += fetches(sources, places, sems, 2 + len(now) + len(later))
    for copy in weights + now + later:
        copy.start()
    place_keys(info, own, near, tokens, steps, solo)
    weights[0].wait()
    keys[...] = dot(tokens[...], key_weight[...]).astype(BF)
    weights[1].wait()
    values[...] = dot(tokens[...], value_weight[...]).astype(BF)
    for copy in now:
        copy.wait()
    if solo:
        split_bias(info, slots, bias, rest_bias)

    def keep(head, top, total):
        tops[head] = top
        totals[head] = total

    out = attend_heads(queries, bias, keys, values, None, keep)
    for block, piece in enumerate(out):
        mixed[:, block * LANES : (block + 1) * LANES] = piece
    for copy in later:
        copy.wait()


def attend_rest(queries, key_weight, value_weight, bias, info, former, former_top, former_total, *refs, steps, solo):
    rows_count = len(steps)
    own, near = refs[:rows_count], refs[rows_count : 2 * rows_count]
    packed, tokens, keys, values = refs[2 * rows_count :]
    heads = bias.shape[0]
    count, wide = queries.shape
    place_keys(info, own, near, tokens, steps, solo)
    keys[...] = dot(tokens[...], key_weight[...]).astype(BF)
    values[...] = dot(tokens[...], value_weight[...]).astype(BF)
    lane = lax.broadcasted_iota(jnp.int32, (count, LANES), 1)
    ends = [jnp.zeros((count, LANES), F32), jnp.ones((count, LANES), F32)]

    def keep(head, top, total):
        ends[0] = jnp.where(lane == head, top, ends[0])
        ends[1] = jnp.where(lane == head, total, ends[1])

    out = attend_heads(queries, bias, keys, values, (former, former_top, former_total), keep)
    for block, piece in enumerate(out):
        packed[:, block * LANES : (block + 1) * LANES] = piece.astype(BF)
    logs = ends[0] + jnp.log(ends[1])
    first = logs.astype(BF).astype(F32)
    rest = logs - first
    second = rest.astype(BF).astype(F32)
    rest = rest - second
    packed[:, wide:] = (first + pltpu.roll(second, heads, 1) + pltpu.roll(rest, 2 * heads, 1)).astype(BF)


def finish_tokens(act, gates, token_out, down, *refs, parts_count):
    parts, back = refs[:parts_count], refs[parts_count]
    count, wide = act.shape
    heads = 16
    size = wide // heads
    logs = []
    for part in parts:
        packed = part[:, wide:].astype(F32)
        logs.append(
            packed + pltpu.roll(packed, LANES - heads, 1) + pltpu.roll(packed, LANES - 2 * heads, 1)
        )
    top = functools.reduce(jnp.maximum, logs)
    weights = [jnp.exp(log - top) for log in logs]
    total = functools.reduce(jnp.add, weights)
    head = lax.broadcasted_iota(jnp.int32, (LANES, wide), 0)
    feature = lax.broadcasted_iota(jnp.int32, (LANES, wide), 1)
    expand = jnp.where((feature >= head * size) & (feature < (head + 1) * size), 1.0, 0.0).astype(BF)
    mixed = jnp.zeros((count, wide), F32)
    for part, weight in zip(parts, weights):
        factor = weight / total
        coarse = factor.astype(BF)
        fine = (factor - coarse.astype(F32)).astype(BF)
        mixed = mixed + (dot(coarse, expand) + dot(fine, expand)) * part[:, :wide].astype(F32)
    gated = (mixed * gates[...]).astype(BF)
    result = (act[...].astype(F32) + dot(gated, token_out[...])).astype(BF)
    back[...] = dot(result, down[...]).astype(BF)


def second_inner(
    info, offsets, ids, atoms1, own_back, near_back, gain, qkv, bias,
    atoms2, mixed, edge_q, edge_k, edge_v, q, k, v, *, share
):
    tokens = 2 * own_back.shape[0]
    table = jnp.concatenate([own_back[...], near_back[...]], axis=0)
    table_ids = (token_of(tokens, share, info[0], 1) + info[1] * tokens).astype(F32)
    step = 256
    for at in range(0, atoms1.shape[0], step):
        members = []
        for first in range(at, at + step, LANES):
            atom_ids = jnp.broadcast_to(ids[:, first : first + LANES].astype(F32), (LANES, LANES)).T
            members.append(
                jnp.concatenate(
                    [one_hot(table_ids[:, t : t + LANES], atom_ids) for t in range(0, tokens, LANES)], axis=1
                )
            )
        member = jnp.concatenate(members, axis=0)
        atoms2[at : at + step, :] = (atoms1[at : at + step, :].astype(F32) + dot(member, table)).astype(BF)
    for at in range(0, atoms1.shape[0], step):
        project(atoms2[at : at + step, :], gain[...], qkv[...], q, k, v, at)
    inner_windows(starts_from(offsets, info[4]), bias, q, k, v, mixed, edge_q, edge_k, edge_v)


def second_edge(
    info, offsets, atoms2, near, far, own_back, near_back, far_back, gain, qkv, out_weight, bias,
    mixed, edge_q, edge_k, edge_v, result, k, v, edge_mixed, ends, *, share, columns
):
    side, column = info[0], info[3]
    close_inner(atoms2, mixed, out_weight, result)
    ends[:, :RIM, :] = bias[:, :RIM, :]
    ends[:, RIM:, :] = bias[:, bias.shape[1] - RIM :, :]
    tokens = 2 * own_back.shape[0]
    table = jnp.concatenate([own_back[...], near_back[...]], axis=0)
    table_ids = token_of(tokens, share, side)
    first_token = (info[1] * tokens).astype(F32)

    def rim_ids(message):
        packed = message[RIM:, :].astype(F32)
        return (packed[0:1, :RIM] * 64.0 + packed[0:1, RIM:] - first_token).astype(jnp.int32)

    near_rows = near[:RIM, :].astype(F32) + dot_tn(one_hot(table_ids, rim_ids(near)), table)
    far_token = rim_ids(far)
    beyond = lax.broadcasted_iota(jnp.int32, (RIM, 1), 0) + jnp.where(
        column == 0, -RIM, jnp.where(column == columns - 1, tokens, 4 * tokens)
    )
    far_rows = (
        far[:RIM, :].astype(F32)
        + dot_tn(one_hot(table_ids, far_token), table)
        + dot_tn(one_hot(beyond, far_token), far_back[...])
    )
    edge_windows(
        starts_from(offsets, info[4] - RIM), ends, gain[...], qkv[...], near_rows.astype(BF).astype(F32), far_rows.astype(BF).astype(F32), side,
        edge_q, edge_k, edge_v, k, v, edge_mixed,
    )
    close_edge(atoms2, edge_mixed, out_weight, result)


def stay(x):
    return pltpu.with_memory_space_constraint(x, pltpu.HBM)


def call(kernel, outs, scratch, specs, flops, limit=20):
    return pl.pallas_call(
        kernel,
        out_shape=outs,
        in_specs=specs,
        out_specs=jax.tree.map(lambda _: VMEM, outs),
        scratch_shapes=scratch,
        compiler_params=pltpu.CompilerParams(vmem_limit_bytes=limit * 1024 * 1024),
        cost_estimate=pl.CostEstimate(flops=flops, bytes_accessed=1_000, transcendentals=1_000),
    )


def body(
    atom_acts, first_gain, first_qkv, first_out, second_gain, second_qkv, second_out, atom_bias, window_start,
    atom_token, up_weight, token_gain, token_weight, token_out, down_weight, pair_bias,
):
    rows, channels = atom_acts.shape
    heads, tok_rows, slots = pair_bias.shape
    wide = token_weight.shape[0]
    row_count, col_count = lax.axis_size("row"), lax.axis_size("col")
    pairs = col_count // 2
    share = tok_rows // col_count
    half = tok_rows // 2
    row, col = lax.axis_index("row"), lax.axis_index("col")
    side, pair = col % 2, col // 2
    info = jnp.stack([side, row, pair, col, (row * col_count + col) * rows]).astype(jnp.int32)
    devices = row_count * col_count

    def to_near(x):
        return lax.ppermute(x, "col", [(i, i ^ 1) for i in range(col_count)])

    def to_far(x):
        swap = [(i, i + 1 if i % 2 else i - 1) for i in range(1, devices - 1)]
        swap = [(0, 0)] + swap + [(devices - 1, devices - 1)]
        return lax.ppermute(x, ("row", "col"), swap)

    def to_beyond(x):
        swap = {i: i for i in range(devices)}
        for i in range(1, row_count):
            first, last = i * col_count, i * col_count - 1
            for one, other in ((first, first - col_count + 1), (last, last + col_count - 1)):
                swap[one], swap[other] = other, one
        return lax.ppermute(x, ("row", "col"), sorted(swap.items()))

    def along_pairs(x, step):
        return lax.ppermute(
            x, "col", [(2 * i + k, 2 * ((i + step) % pairs) + k) for i in range(pairs) for k in range(2)]
        )

    def along_rows(x, step):
        return lax.ppermute(x, "row", [(i, i ^ step) for i in range(row_count)])

    def rim_of(x, last):
        return lax.dynamic_slice_in_dim(x, jnp.where(last, rows - RIM, 0), RIM, axis=0)

    near_acts = to_near(rim_of(atom_acts, side == 0))
    far_acts = to_far(rim_of(atom_acts, side == 1))

    ids = atom_token.reshape(1, rows)
    inner_scratch = [
        pltpu.VMEM((rows, channels), BF),
        pltpu.VMEM((rows, channels), F32),
        pltpu.VMEM((rows, channels), F32),
    ]
    edge_scratch = [
        pltpu.VMEM((6 * RIM, channels), F32),
        pltpu.VMEM((6 * RIM, channels), F32),
        pltpu.VMEM((2 * RIM, channels), BF),
    ]
    atom_shape = jax.ShapeDtypeStruct((rows, channels), BF)
    edge_shapes = [
        jax.ShapeDtypeStruct((2 * RIM, channels), BF),
        jax.ShapeDtypeStruct((4 * RIM, channels), F32),
        jax.ShapeDtypeStruct((4 * RIM, channels), F32),
    ]
    packed_shape = jax.ShapeDtypeStruct((half, wide + LANES), BF)
    first_gain, second_gain = first_gain.reshape(1, -1), second_gain.reshape(1, -1)
    pieces = 2
    windows = window_start.shape[0]
    edge = RIM * windows // rows
    groups = (windows - 2 * edge) // window_group(windows, edge)
    first_args = [atom_acts, first_gain, first_qkv]
    mixed1 = call(
        functools.partial(first_inner, pieces=pieces),
        [atom_shape] + edge_shapes + [jax.ShapeDtypeStruct((atom_bias.shape[0], 2 * RIM, atom_bias.shape[2]), BF)],
        inner_scratch
        + [pltpu.VMEM(x.shape, x.dtype) for x in first_args]
        + [pltpu.SMEM(window_start.shape, jnp.int32), pltpu.VMEM(atom_bias.shape, BF)]
        + [pltpu.SemaphoreType.DMA((5 + pieces,)), pltpu.SemaphoreType.DMA((groups,))],
        [SMEM] + [HBM] * 5,
        1_500_000_000,
        16,
    )(info, *map(stay, first_args), stay(window_start), stay(atom_bias))
    message_shape = jax.ShapeDtypeStruct((RIM + 16, channels), BF)
    atoms1, send, keep, near_message, far_message = call(
        functools.partial(first_edge, share=share),
        [atom_shape, packed_shape, packed_shape, message_shape, message_shape],
        edge_scratch,
        [SMEM, SMEM] + [VMEM] * 13,
        2_000_000_000,
        16,
    )(
        info, window_start, ids, atom_acts, near_acts, far_acts, first_gain, first_qkv, first_out,
        up_weight, *mixed1,
    )

    chip_sum = (keep.astype(F32) + to_near(send).astype(F32)).astype(BF)
    chip_sum, near_bias = lax.optimization_barrier((chip_sum, pair_bias))
    bias_near = to_near(near_bias)
    sums = [lax.dynamic_slice_in_dim(chip_sum, pair * share, share, axis=0)]
    for step in range(1, pairs):
        piece = lax.dynamic_slice_in_dim(chip_sum, (pair + step) % pairs * share, share, axis=0)
        sums.append(along_pairs(piece, step))
    share_shape = jax.ShapeDtypeStruct((share, wide), BF)
    gain_row = token_gain.reshape(1, -1)
    act, normed = call(
        functools.partial(mean_tokens, count=len(sums)), [share_shape] * 2, [], [VMEM] * (len(sums) + 1), 1_000_000
    )(*sums, gain_row)

    group = LANES // share
    solo = group == 2
    split = 1 if solo else group
    own_keys = [normed] + [along_rows(normed, step) for step in range(1, row_count)]
    near_keys = [to_near(x) for x in own_keys[:split]]
    other_acts = [along_pairs(act, step) for step in range(1, pairs)]
    half_shape = jax.ShapeDtypeStruct((half, wide), BF)
    wide_shape = jax.ShapeDtypeStruct((half, wide), F32)
    act_rows, queries, gates = call(
        functools.partial(query_tokens, others=len(other_acts)),
        [half_shape, half_shape, wide_shape],
        [pltpu.VMEM((wide, wide), BF)] * 2 + [pltpu.SemaphoreType.DMA((2,))],
        [SMEM, HBM] + [VMEM] * (2 + len(other_acts)),
        1_000,
    )(info, stay(token_weight), gain_row, act, *other_acts)

    rest = row_count - split

    def key_scratch(count):
        return [pltpu.VMEM((2 * count * share, wide), BF)] * 3

    def bias_shape(count):
        return jax.ShapeDtypeStruct((heads, half, 2 * count * share), BF)

    head_shape = jax.ShapeDtypeStruct((heads, half, LANES), F32)
    weight_shape = jax.ShapeDtypeStruct((wide, wide), BF)
    copies = 2 + 2 * pairs * (row_count // group)
    bias_scratch = [
        pltpu.VMEM((heads, half, 2 * split * share), BF),
        pltpu.VMEM((2, heads, half, LANES), BF),
        pltpu.SemaphoreType.DMA((copies,)),
    ]
    *held, mixed, tops, totals = call(
        functools.partial(attend_first, steps=list(range(split)), solo=solo),
        [weight_shape, weight_shape, bias_shape(rest), wide_shape, head_shape, head_shape],
        key_scratch(split) + bias_scratch,
        [SMEM, HBM, VMEM, HBM, HBM] + [VMEM] * (2 * split),
        1_000,
    )(info, stay(token_weight), queries, stay(pair_bias), stay(bias_near), *own_keys[:split], *near_keys)
    rest_keys, mixed = lax.optimization_barrier((own_keys[split:], mixed))
    rest_near = [to_near(x) for x in rest_keys]
    part = call(
        functools.partial(attend_rest, steps=list(range(split, row_count)), solo=solo),
        packed_shape,
        key_scratch(rest),
        [VMEM] * 4 + [SMEM] + [VMEM] * (3 + 2 * rest),
        2_000_000_000,
    )(queries, *held, info, mixed, tops, totals, *rest_keys, *rest_near)

    near_message, far_message, part = lax.optimization_barrier((near_message, far_message, part))
    parts = [along_pairs(part, step) for step in range(1, pairs)]
    near_message, far_message, parts = lax.optimization_barrier(
        (to_near(near_message), to_far(far_message), parts)
    )
    parts = [part] + parts
    own_back = call(
        functools.partial(finish_tokens, parts_count=pairs),
        jax.ShapeDtypeStruct((half, channels), BF),
        [],
        [VMEM] * (4 + pairs),
        200_000_000,
    )(act_rows, gates, token_out, down_weight, *parts)

    near_back = to_near(own_back)
    if share >= RIM:
        last_rows = own_back[half - RIM :]
        first_rows = own_back[:RIM]
    else:
        both = jnp.where(side == 0, jnp.stack([own_back, near_back]), jnp.stack([near_back, own_back]))
        both = both.reshape(2, pairs, share, channels).transpose(1, 0, 2, 3).reshape(tok_rows, channels)
        last_rows = both[tok_rows - RIM :]
        first_rows = both[:RIM]
    far_back = to_beyond(jnp.where(side == 1, last_rows, first_rows))

    atoms2, *mixed2 = call(
        functools.partial(second_inner, share=share),
        [atom_shape, atom_shape] + edge_shapes,
        inner_scratch,
        [SMEM, SMEM] + [VMEM] * 7,
        1_500_000_000,
        16,
    )(info, window_start, ids, atoms1, own_back, near_back, second_gain, second_qkv, atom_bias)
    return call(
        functools.partial(second_edge, share=share, columns=col_count),
        atom_shape,
        edge_scratch + [pltpu.VMEM((atom_bias.shape[0], 2 * RIM, atom_bias.shape[2]), BF)],
        [SMEM, SMEM] + [VMEM] * 14,
        300_000_000,
        16,
    )(
        info, window_start, atoms2, near_message, far_message, own_back, near_back, far_back,
        second_gain, second_qkv, second_out, atom_bias, *mixed2,
    )


def solution(mesh):
    atoms = P(("group", "row", "col"))
    in_specs = (
        P(("group", "row", "col"), None),
        P(), P(), P(), P(), P(), P(),
        P(None, ("group", "row", "col"), None),
        atoms,
        atoms,
        P(), P(), P(), P(), P(),
        P(None, ("group", "row"), "col"),
    )
    out_specs = P(("group", "row", "col"), None)
    return jax.shard_map(body, mesh=mesh, in_specs=in_specs, out_specs=out_specs, check_vma=False)
```

```python
import functools
import math

import jax
import jax.numpy as jnp
from jax import lax
from jax.experimental import pallas as pl
from jax.experimental.pallas import tpu as pltpu
from jax.sharding import PartitionSpec as P

BF = jnp.bfloat16
F32 = jnp.float32
RIM = 64
LANES = 128
VMEM = pl.BlockSpec(memory_space=pltpu.VMEM)
SMEM = pl.BlockSpec(memory_space=pltpu.SMEM)
HBM = pl.BlockSpec(memory_space=pltpu.HBM)


def dot(a, b):
    return jnp.dot(a, b, preferred_element_type=F32)


def dot_nt(a, b):
    return lax.dot_general(a, b, (((1,), (1,)), ((), ())), preferred_element_type=F32)


def dot_tn(a, b):
    return lax.dot_general(a, b, (((0,), (0,)), ((), ())), preferred_element_type=F32)


def norm_rows(values, gain):
    center = values - jnp.mean(values, axis=-1, keepdims=True)
    spread = jnp.mean(center * center, axis=-1, keepdims=True)
    return center * lax.rsqrt(spread + 1e-05) * gain


def token_of(count, share, first_parity, dim=0):
    half = count // 2
    row = lax.broadcasted_iota(jnp.int32, (count, 1) if dim == 0 else (1, count), dim)
    second = (row >= half).astype(jnp.int32)
    inner = row - second * half
    shift = share.bit_length() - 1
    share_pair = inner >> shift
    inside = inner & (share - 1)
    parity = first_parity + second - 2 * first_parity * second
    return (2 * share_pair + parity) * share + inside


def one_hot(table_ids, atom_ids):
    return jnp.where(table_ids == atom_ids, 1.0, 0.0).astype(BF)


def project(rows, gain, qkv, q, k, v, at):
    channels = rows.shape[1]
    packed = dot(norm_rows(rows.astype(F32), gain).astype(BF), qkv).astype(BF)
    place = slice(at, at + rows.shape[0])
    q[place, :] = packed[:, :channels]
    k[place, :] = packed[:, channels : 2 * channels].astype(F32)
    v[place, :] = packed[:, 2 * channels :].astype(F32)


def attend_windows(places, bias, q, k, v, mixed):
    heads, _, span = bias.shape
    channels = q.shape[1]
    block = span - 3 * RIM // 2
    size = channels // heads
    scale = 1.0 / math.sqrt(size)
    stacked = heads * block
    head_row = lax.broadcasted_iota(jnp.int32, (heads, block, channels), 0).reshape(stacked, channels)
    head_lane = lax.broadcasted_iota(jnp.int32, (stacked, channels), 1) // size
    own_head = jnp.where(head_row == head_lane, 1.0, 0.0).astype(BF)
    lane_head = lax.broadcasted_iota(jnp.int32, (block, channels), 1) // size
    ones = jnp.ones((span, channels), BF)

    def picked(stack):
        out = stack[:block]
        for head in range(1, heads):
            out = jnp.where(lane_head == head, stack[head * block : (head + 1) * block], out)
        return out

    scores = []
    for query_at, _, key_at in places:
        spread = jnp.concatenate([q[pl.ds(query_at, block), :]] * heads, axis=0) * own_head
        scores.append(dot_nt(spread, k[pl.ds(key_at, span), :].astype(BF)))
    raised = []
    for (_, bias_at, _), score in zip(places, scores):
        tile = bias[:, pl.ds(bias_at, block), :].reshape(stacked, span).astype(F32)
        score = score * scale + tile
        raised.append(jnp.exp(score - jnp.max(score, axis=-1, keepdims=True)).astype(BF))
    for (query_at, _, key_at), weights in zip(places, raised):
        values = jnp.concatenate([v[pl.ds(key_at, span), :].astype(BF), ones], axis=1)
        out = dot(weights, values)
        mixed[pl.ds(query_at, block), :] = (picked(out[:, :channels]) / picked(out[:, channels:])).astype(BF)


class starts_from:
    def __init__(self, starts, base):
        self.starts, self.base, self.shape = starts, base, starts.shape

    def __getitem__(self, window):
        return self.starts[window] - self.base


def window_group(windows, edge):
    return next(size for size in (15, 12, 10, 6, 5, 4, 3, 2, 1) if (windows - 2 * edge) % size == 0)


def inner_windows(offsets, bias, q, k, v, mixed, edge_q, edge_k, edge_v, ready=None):
    windows = offsets.shape[0]
    rows = q.shape[0]
    block = rows // windows
    edge = RIM // block
    group = window_group(windows, edge)

    def one_group(step, carry):
        if ready is not None:
            ready(step)
        places = []
        for member in range(group):
            window = edge + step * group + member
            at = pl.multiple_of(window * block, block)
            places.append((at, at, offsets[window]))
        attend_windows(places, bias, q, k, v, mixed)
        return carry

    lax.fori_loop(0, (windows - 2 * edge) // group, one_group, 0)
    edge_q[:RIM, :] = q[:RIM, :]
    edge_q[RIM:, :] = q[rows - RIM :, :]
    for source, target in ((k, edge_k), (v, edge_v)):
        target[: 2 * RIM, :] = source[: 2 * RIM, :]
        target[2 * RIM :, :] = source[rows - 2 * RIM :, :]


def edge_windows(offsets, bias, gain, qkv, near, far, side, edge_q, edge_k, edge_v, k, v, mixed):
    windows = offsets.shape[0]
    channels = edge_q.shape[1]
    block = bias.shape[2] - 3 * RIM // 2
    rows = windows * block
    edge = RIM // block
    for source, target in ((edge_k, k), (edge_v, v)):
        target[RIM : 3 * RIM, :] = source[: 2 * RIM, :]
        target[3 * RIM : 5 * RIM, :] = source[2 * RIM :, :]
    normed = norm_rows(jnp.concatenate([near, far], axis=0), gain).astype(BF)
    packed = dot(normed, qkv[:, channels:]).astype(BF).astype(F32)
    near_at = pl.multiple_of(jnp.where(side == 0, 5 * RIM, 0), RIM)
    far_at = pl.multiple_of(5 * RIM - near_at, RIM)
    for at, part in ((near_at, packed[:RIM]), (far_at, packed[RIM:])):
        k[pl.ds(at, RIM), :] = part[:, :channels]
        v[pl.ds(at, RIM), :] = part[:, channels:]
    places = []
    for member in range(edge):
        places.append((member * block, member * block, offsets[member]))
    for member in range(edge):
        window = windows - edge + member
        at = RIM + member * block
        places.append((at, at, offsets[window] - (rows - 4 * RIM)))
    attend_windows(places, bias, edge_q, k, v, mixed)


def fetches(sources, targets, sems, first=0):
    return [
        pltpu.make_async_copy(source, target, sems.at[first + index])
        for index, (source, target) in enumerate(zip(sources, targets))
    ]


def first_inner(
    info, acts_far, gain_far, qkv_far, starts_far, bias_far, mixed, edge_q, edge_k, edge_v, edge_bias,
    q, k, v, acts, gain, qkv, starts, bias, sems, bias_sems, *, pieces
):
    rows = acts.shape[0]
    windows = starts.shape[0]
    block = rows // windows
    span = window_group(windows, RIM // block) * block
    part = rows // pieces
    cuts = [pl.ds(index * part, part) for index in range(pieces)]
    small = fetches([gain_far, qkv_far, starts_far], [gain, qkv, starts], sems)
    moving = fetches([acts_far.at[cut, :] for cut in cuts], [acts.at[cut, :] for cut in cuts], sems, 3)
    ends = fetches(
        [bias_far.at[:, pl.ds(at, RIM), :] for at in (0, rows - RIM)],
        [edge_bias.at[:, pl.ds(at, RIM), :] for at in (0, RIM)],
        sems,
        3 + pieces,
    )

    def tile(step):
        place = pl.ds(pl.multiple_of(RIM + step * span, block), span)
        return pltpu.make_async_copy(bias_far.at[:, place, :], bias.at[:, place, :], bias_sems.at[step])

    for copy in moving[:1] + small + moving[1:]:
        copy.start()
    for copy in small:
        copy.wait()
    step = 256
    for index, copy in enumerate(moving):
        copy.wait()
        if index == 0:
            for group in range(bias_sems.shape[0]):
                tile(group).start()
            for end in ends:
                end.start()
        for at in range(index * part, (index + 1) * part, step):
            project(acts[at : at + step, :], gain[...], qkv[...], q, k, v, at)
    inner_windows(
        starts_from(starts, info[4]), bias, q, k, v, mixed, edge_q, edge_k, edge_v, lambda index: tile(index).wait()
    )
    for end in ends:
        end.wait()


def first_edge(
    info, offsets, ids, acts, near, far, gain, qkv, out_weight, up, mixed, edge_q, edge_k, edge_v, bias,
    atoms, send, keep, near_message, far_message, k, v, edge_mixed, *, share
):
    side = info[0]
    rows = acts.shape[0]
    close_inner(acts, mixed, out_weight, atoms)
    edge_windows(
        starts_from(offsets, info[4] - RIM), bias, gain[...], qkv[...], near[...].astype(F32), far[...].astype(F32), side,
        edge_q, edge_k, edge_v, k, v, edge_mixed,
    )
    close_edge(acts, edge_mixed, out_weight, atoms)
    step = 256
    tokens = 2 * send.shape[0]
    half = tokens // 2
    head_ids = ids[:, :RIM]
    tail_ids = ids[:, rows - RIM :]
    for message, last in ((near_message, 1 - side), (far_message, side)):
        at = pl.multiple_of(last * (rows - RIM), RIM)
        message[:RIM, :] = atoms[pl.ds(at, RIM), :]
        sent = head_ids + last * (tail_ids - head_ids)
        coded = jnp.concatenate([sent >> 6, sent & 63], axis=1).astype(F32)
        message[RIM:, :] = jnp.broadcast_to(coded, (16, 2 * RIM)).astype(BF)
    member = one_hot(token_of(tokens, share, 1 - side) + info[1] * tokens, ids[...])
    wide = up.shape[1]
    atom_rows = atoms[...]
    for at in range(0, wide, step):
        feat = jnp.maximum(dot(atom_rows, up[:, at : at + step]), 0.0).astype(BF)
        sums = dot(member, feat).astype(BF)
        send[:, at : at + step] = sums[:half]
        keep[:, at : at + step] = sums[half:]
    count = dot(member, jnp.ones((rows, LANES), BF))
    high = jnp.floor(count * (1.0 / 64.0))
    low = count - 64.0 * high
    lane = lax.broadcasted_iota(jnp.int32, (tokens, LANES), 1)
    pieces = jnp.where(lane == 0, high, jnp.where(lane == 1, low, 0.0)).astype(BF)
    send[:, wide:] = pieces[:half]
    keep[:, wide:] = pieces[half:]


def close_inner(acts, mixed, out_weight, out):
    rows = acts.shape[0]
    step = 256
    for at in range(0, rows, step):
        first, last = max(at, RIM), min(at + step, rows - RIM)
        part = acts[first:last, :].astype(F32) + dot(mixed[first:last, :], out_weight[...])
        out[first:last, :] = part.astype(BF)


def close_edge(acts, mixed, out_weight, out):
    rows = acts.shape[0]
    moved = dot(mixed[...], out_weight[...])
    out[:RIM, :] = (acts[:RIM, :].astype(F32) + moved[:RIM]).astype(BF)
    out[rows - RIM :, :] = (acts[rows - RIM :, :].astype(F32) + moved[RIM:]).astype(BF)


def mean_tokens(*refs, count):
    parts, gain, act, normed = refs[:count], refs[count], refs[count + 1], refs[count + 2]
    total = parts[0][...].astype(F32)
    for part in parts[1:]:
        total = total + part[...].astype(F32)
    wide = act.shape[1]
    atoms = total[:, wide : wide + 1] * 64.0 + total[:, wide + 1 : wide + 2]
    rounded = (total[:, :wide] / atoms).astype(BF)
    act[...] = rounded
    normed[...] = norm_rows(rounded.astype(F32), gain[...]).astype(BF)


def query_tokens(info, weight_far, gain, own_act, *refs, others):
    other_acts = refs[:others]
    act, queries, gates, query_weight, gate_weight, sems = refs[others:]
    share, wide = own_act.shape
    copies = fetches(
        [weight_far.at[:, pl.ds(0, wide)], weight_far.at[:, pl.ds(3 * wide, wide)]], [query_weight, gate_weight], sems
    )
    for copy in copies:
        copy.start()
    pairs = others + 1
    place = info[2]
    act[pl.ds(pl.multiple_of(place * share, share), share), :] = own_act[...]
    for step in range(1, pairs):
        at = lax.rem(place - step + pairs, pairs) * share
        act[pl.ds(pl.multiple_of(at, share), share), :] = other_acts[step - 1][...]
    normed = norm_rows(act[...].astype(F32), gain[...]).astype(BF)
    copies[0].wait()
    queries[...] = dot(normed, query_weight[...]).astype(BF)
    copies[1].wait()
    raw = dot(normed, gate_weight[...]).astype(BF).astype(F32)
    gates[...] = jax.nn.sigmoid(raw)


def place_keys(info, own, near, tokens, steps, solo):
    share = own[0].shape[0]
    group = LANES // share
    place = info[1] & (group - 1)
    lead = 2 * share if solo else 0
    for own_rows, near_rows, step in zip(own, near, steps):
        if solo and step < group:
            places = (0, share)
        else:
            at = lead + (step // group - (steps[0] + solo) // group) * 2 * LANES + (place ^ (step % group)) * share
            places = (at, at + LANES)
        for rows, at in zip((own_rows, near_rows), places):
            tokens[pl.ds(pl.multiple_of(at, share), share), :] = rows[...]


def bias_pieces(info, biases_far, block, targets, share):
    count = targets[0].shape[1]
    group = LANES // share
    side, row = info[0], info[1]
    slot = pl.multiple_of(((row // group) ^ block) * LANES, LANES)
    sources, places = [], []
    for bias_far, target in zip(biases_far, targets):
        for pair in range(count // share):
            at = pl.multiple_of((2 * pair + side) * share, share)
            sources.append(bias_far.at[:, pl.ds(at, share), pl.ds(slot, LANES)])
            places.append(target.at[:, pl.ds(pair * share, share), :])
    return sources, places


def split_bias(info, slots, bias, rest):
    heads, count = bias.shape[0], bias.shape[1]
    lane = lax.broadcasted_iota(jnp.int32, (count, LANES), 1)
    lower = lane < LANES // 2
    first = info[1] & 1
    for head in range(heads):
        own, near = slots[0, head].astype(F32), slots[1, head].astype(F32)
        low = jnp.where(lower, own, pltpu.roll(near, LANES // 2, 1))
        high = jnp.where(lower, pltpu.roll(own, LANES // 2, 1), near)
        bias[head] = jnp.where(first == 0, low, high).astype(BF)
        rest[head, :, :LANES] = jnp.where(first == 0, high, low).astype(BF)


def attend_heads(queries, bias, keys, values, previous, keep):
    count, wide = queries.shape
    heads = bias.shape[0]
    size = wide // heads
    scale = 1.0 / math.sqrt(size)
    span = keys.shape[0] // LANES
    lane = lax.broadcasted_iota(jnp.int32, (count, LANES), 1)
    out = [None] * (wide // LANES)
    together = 4
    for start in range(0, heads, together):
        members = []
        for head in range(start, start + together):
            first, last = head * size, (head + 1) * size
            low, high = first // LANES, -(-last // LANES)
            chunk = slice(low * LANES, high * LANES)
            chunk_lane = lax.broadcasted_iota(jnp.int32, (count, (high - low) * LANES), 1) + low * LANES
            inside = (chunk_lane >= first) & (chunk_lane < last)
            query = jnp.where(inside, queries[:, chunk].astype(F32), 0.0).astype(BF)
            members.append((head, first, low, high, dot_nt(query, keys[:, chunk])))
        raised = []
        for head, first, low, high, score in members:
            score = score * scale + bias[head].astype(F32)
            top = jnp.broadcast_to(jnp.max(score, axis=-1, keepdims=True), (count, LANES))
            if previous is not None:
                former = previous[1][head]
                top = jnp.maximum(top, former)
            weights = jnp.exp(score - jnp.concatenate([top] * span, axis=1))
            total = jnp.broadcast_to(jnp.sum(weights, axis=-1, keepdims=True), (count, LANES))
            fade = None
            if previous is not None:
                fade = jnp.exp(former - top)
                total = total + fade * previous[2][head]
            keep(head, top, total)
            raised.append((weights.astype(BF), fade, total))
        for (head, first, low, high, _), (weights, fade, total) in zip(members, raised):
            mixed = dot(weights, values[:, low * LANES : high * LANES])
            if previous is not None:
                inverse = 1.0 / total
            for block in range(low, high):
                piece = mixed[:, (block - low) * LANES : (block - low + 1) * LANES]
                if previous is not None:
                    piece = (piece + fade * previous[0][:, block * LANES : (block + 1) * LANES]) * inverse
                if out[block] is not None:
                    piece = jnp.where(lane + block * LANES >= first, piece, out[block])
                out[block] = piece
    return out


def attend_first(info, weight_far, queries, own_far, near_far, *refs, steps, solo):
    rows_count = len(steps)
    own, near = refs[:rows_count], refs[rows_count : 2 * rows_count]
    key_weight, value_weight, rest_bias, mixed, tops, totals, tokens, keys, values, bias, slots, sems = refs[
        2 * rows_count :
    ]
    share, wide = own[0].shape
    weights = fetches(
        [weight_far.at[:, pl.ds(wide, wide)], weight_far.at[:, pl.ds(2 * wide, wide)]], [key_weight, value_weight], sems
    )
    biases_far = (own_far, near_far)
    targets = (slots.at[0], slots.at[1]) if solo else [bias.at[:, :, pl.ds(at, LANES)] for at in (0, LANES)]
    now = fetches(*bias_pieces(info, biases_far, 0, targets, share), sems, 2)
    later = []
    lead = LANES if solo else 0
    for block in range((rest_bias.shape[2] - lead) // (2 * LANES)):
        first = lead + block * 2 * LANES
        targets = [rest_bias.at[:, :, pl.ds(at, LANES)] for at in (first, first + LANES)]
        sources, places = bias_pieces(info, biases_far, block + 1, targets, share)
        later += fetches(sources, places, sems, 2 + len(now) + len(later))
    for copy in weights + now + later:
        copy.start()
    place_keys(info, own, near, tokens, steps, solo)
    weights[0].wait()
    keys[...] = dot(tokens[...], key_weight[...]).astype(BF)
    weights[1].wait()
    values[...] = dot(tokens[...], value_weight[...]).astype(BF)
    for copy in now:
        copy.wait()
    if solo:
        split_bias(info, slots, bias, rest_bias)

    def keep(head, top, total):
        tops[head] = top
        totals[head] = total

    out = attend_heads(queries, bias, keys, values, None, keep)
    for block, piece in enumerate(out):
        mixed[:, block * LANES : (block + 1) * LANES] = piece
    for copy in later:
        copy.wait()


def attend_rest(queries, key_weight, value_weight, bias, info, former, former_top, former_total, *refs, steps, solo):
    rows_count = len(steps)
    own, near = refs[:rows_count], refs[rows_count : 2 * rows_count]
    packed, tokens, keys, values = refs[2 * rows_count :]
    heads = bias.shape[0]
    count, wide = queries.shape
    place_keys(info, own, near, tokens, steps, solo)
    keys[...] = dot(tokens[...], key_weight[...]).astype(BF)
    values[...] = dot(tokens[...], value_weight[...]).astype(BF)
    lane = lax.broadcasted_iota(jnp.int32, (count, LANES), 1)
    ends = [jnp.zeros((count, LANES), F32), jnp.ones((count, LANES), F32)]

    def keep(head, top, total):
        ends[0] = jnp.where(lane == head, top, ends[0])
        ends[1] = jnp.where(lane == head, total, ends[1])

    out = attend_heads(queries, bias, keys, values, (former, former_top, former_total), keep)
    for block, piece in enumerate(out):
        packed[:, block * LANES : (block + 1) * LANES] = piece.astype(BF)
    logs = ends[0] + jnp.log(ends[1])
    first = logs.astype(BF).astype(F32)
    rest = logs - first
    second = rest.astype(BF).astype(F32)
    rest = rest - second
    packed[:, wide:] = (first + pltpu.roll(second, heads, 1) + pltpu.roll(rest, 2 * heads, 1)).astype(BF)


def finish_tokens(act, gates, token_out, down, *refs, parts_count):
    parts, back = refs[:parts_count], refs[parts_count]
    count, wide = act.shape
    heads = 16
    size = wide // heads
    logs = []
    for part in parts:
        packed = part[:, wide:].astype(F32)
        logs.append(
            packed + pltpu.roll(packed, LANES - heads, 1) + pltpu.roll(packed, LANES - 2 * heads, 1)
        )
    top = functools.reduce(jnp.maximum, logs)
    weights = [jnp.exp(log - top) for log in logs]
    total = functools.reduce(jnp.add, weights)
    head = lax.broadcasted_iota(jnp.int32, (LANES, wide), 0)
    feature = lax.broadcasted_iota(jnp.int32, (LANES, wide), 1)
    expand = jnp.where((feature >= head * size) & (feature < (head + 1) * size), 1.0, 0.0).astype(BF)
    mixed = jnp.zeros((count, wide), F32)
    for part, weight in zip(parts, weights):
        factor = weight / total
        coarse = factor.astype(BF)
        fine = (factor - coarse.astype(F32)).astype(BF)
        mixed = mixed + (dot(coarse, expand) + dot(fine, expand)) * part[:, :wide].astype(F32)
    gated = (mixed * gates[...]).astype(BF)
    result = (act[...].astype(F32) + dot(gated, token_out[...])).astype(BF)
    back[...] = dot(result, down[...]).astype(BF)


def second_inner(
    info, offsets, ids, atoms1, own_back, near_back, gain, qkv, bias,
    atoms2, mixed, edge_q, edge_k, edge_v, q, k, v, *, share
):
    tokens = 2 * own_back.shape[0]
    table = jnp.concatenate([own_back[...], near_back[...]], axis=0)
    table_ids = (token_of(tokens, share, info[0], 1) + info[1] * tokens).astype(F32)
    step = 256
    for at in range(0, atoms1.shape[0], step):
        members = []
        for first in range(at, at + step, LANES):
            atom_ids = jnp.broadcast_to(ids[:, first : first + LANES].astype(F32), (LANES, LANES)).T
            members.append(
                jnp.concatenate(
                    [one_hot(table_ids[:, t : t + LANES], atom_ids) for t in range(0, tokens, LANES)], axis=1
                )
            )
        member = jnp.concatenate(members, axis=0)
        atoms2[at : at + step, :] = (atoms1[at : at + step, :].astype(F32) + dot(member, table)).astype(BF)
    for at in range(0, atoms1.shape[0], step):
        project(atoms2[at : at + step, :], gain[...], qkv[...], q, k, v, at)
    inner_windows(starts_from(offsets, info[4]), bias, q, k, v, mixed, edge_q, edge_k, edge_v)


def second_edge(
    info, offsets, atoms2, near, far, own_back, near_back, far_back, gain, qkv, out_weight, bias,
    mixed, edge_q, edge_k, edge_v, result, k, v, edge_mixed, ends, *, share, columns
):
    side, column = info[0], info[3]
    close_inner(atoms2, mixed, out_weight, result)
    ends[:, :RIM, :] = bias[:, :RIM, :]
    ends[:, RIM:, :] = bias[:, bias.shape[1] - RIM :, :]
    tokens = 2 * own_back.shape[0]
    table = jnp.concatenate([own_back[...], near_back[...]], axis=0)
    table_ids = token_of(tokens, share, side)
    first_token = (info[1] * tokens).astype(F32)

    def rim_ids(message):
        packed = message[RIM:, :].astype(F32)
        return (packed[0:1, :RIM] * 64.0 + packed[0:1, RIM:] - first_token).astype(jnp.int32)

    near_rows = near[:RIM, :].astype(F32) + dot_tn(one_hot(table_ids, rim_ids(near)), table)
    far_token = rim_ids(far)
    beyond = lax.broadcasted_iota(jnp.int32, (RIM, 1), 0) + jnp.where(
        column == 0, -RIM, jnp.where(column == columns - 1, tokens, 4 * tokens)
    )
    far_rows = (
        far[:RIM, :].astype(F32)
        + dot_tn(one_hot(table_ids, far_token), table)
        + dot_tn(one_hot(beyond, far_token), far_back[...])
    )
    edge_windows(
        starts_from(offsets, info[4] - RIM), ends, gain[...], qkv[...], near_rows.astype(BF).astype(F32), far_rows.astype(BF).astype(F32), side,
        edge_q, edge_k, edge_v, k, v, edge_mixed,
    )
    close_edge(atoms2, edge_mixed, out_weight, result)


def stay(x):
    return pltpu.with_memory_space_constraint(x, pltpu.HBM)


def call(kernel, outs, scratch, specs, flops, limit=20):
    return pl.pallas_call(
        kernel,
        out_shape=outs,
        in_specs=specs,
        out_specs=jax.tree.map(lambda _: VMEM, outs),
        scratch_shapes=scratch,
        compiler_params=pltpu.CompilerParams(vmem_limit_bytes=limit * 1024 * 1024),
        cost_estimate=pl.CostEstimate(flops=flops, bytes_accessed=1_000, transcendentals=1_000),
    )


def body(
    atom_acts, first_gain, first_qkv, first_out, second_gain, second_qkv, second_out, atom_bias, window_start,
    atom_token, up_weight, token_gain, token_weight, token_out, down_weight, pair_bias,
):
    rows, channels = atom_acts.shape
    heads, tok_rows, slots = pair_bias.shape
    wide = token_weight.shape[0]
    row_count, col_count = lax.axis_size("row"), lax.axis_size("col")
    pairs = col_count // 2
    share = tok_rows // col_count
    half = tok_rows // 2
    row, col = lax.axis_index("row"), lax.axis_index("col")
    side, pair = col % 2, col // 2
    info = jnp.stack([side, row, pair, col, (row * col_count + col) * rows]).astype(jnp.int32)
    devices = row_count * col_count
    group_count = lax.axis_size("group")

    def to_near(x):
        return lax.ppermute(x, "col", [(i, i ^ 1) for i in range(col_count)])

    def swapped(x, swap):
        pairs_list = []
        for i in range(group_count * devices):
            group_at, at = divmod(i, devices)
            if at in swap:
                target = group_at * devices + swap[at]
            else:
                target = (group_at ^ 1) * devices + at if group_count % 2 == 0 else i
            pairs_list.append((i, target))
        return lax.ppermute(x, ("group", "row", "col"), pairs_list)

    def to_far(x):
        return swapped(x, {i: i + 1 if i % 2 else i - 1 for i in range(1, devices - 1)})

    def to_beyond(x):
        swap = {}
        for i in range(1, row_count):
            first, last = i * col_count, i * col_count - 1
            for one, other in ((first, first - col_count + 1), (last, last + col_count - 1)):
                swap[one], swap[other] = other, one
        if col_count > 4:
            for i in range(devices):
                if 2 <= i % col_count < col_count - 2:
                    swap[i] = i ^ 1
        return swapped(x, swap)

    def along_pairs(x, step):
        return lax.ppermute(
            x, "col", [(2 * i + k, 2 * ((i + step) % pairs) + k) for i in range(pairs) for k in range(2)]
        )

    def along_rows(x, step):
        return lax.ppermute(x, "row", [(i, i ^ step) for i in range(row_count)])

    def rim_of(x, last):
        return lax.dynamic_slice_in_dim(x, jnp.where(last, rows - RIM, 0), RIM, axis=0)

    near_acts = to_near(rim_of(atom_acts, side == 0))
    far_acts = to_far(rim_of(atom_acts, side == 1))

    ids = atom_token.reshape(1, rows)
    inner_scratch = [
        pltpu.VMEM((rows, channels), BF),
        pltpu.VMEM((rows, channels), F32),
        pltpu.VMEM((rows, channels), F32),
    ]
    edge_scratch = [
        pltpu.VMEM((6 * RIM, channels), F32),
        pltpu.VMEM((6 * RIM, channels), F32),
        pltpu.VMEM((2 * RIM, channels), BF),
    ]
    atom_shape = jax.ShapeDtypeStruct((rows, channels), BF)
    edge_shapes = [
        jax.ShapeDtypeStruct((2 * RIM, channels), BF),
        jax.ShapeDtypeStruct((4 * RIM, channels), F32),
        jax.ShapeDtypeStruct((4 * RIM, channels), F32),
    ]
    packed_shape = jax.ShapeDtypeStruct((half, wide + LANES), BF)
    first_gain, second_gain = first_gain.reshape(1, -1), second_gain.reshape(1, -1)
    pieces = 2
    windows = window_start.shape[0]
    edge = RIM * windows // rows
    groups = (windows - 2 * edge) // window_group(windows, edge)
    first_args = [atom_acts, first_gain, first_qkv]
    mixed1 = call(
        functools.partial(first_inner, pieces=pieces),
        [atom_shape] + edge_shapes + [jax.ShapeDtypeStruct((atom_bias.shape[0], 2 * RIM, atom_bias.shape[2]), BF)],
        inner_scratch
        + [pltpu.VMEM(x.shape, x.dtype) for x in first_args]
        + [pltpu.SMEM(window_start.shape, jnp.int32), pltpu.VMEM(atom_bias.shape, BF)]
        + [pltpu.SemaphoreType.DMA((5 + pieces,)), pltpu.SemaphoreType.DMA((groups,))],
        [SMEM] + [HBM] * 5,
        1_500_000_000,
        16,
    )(info, *map(stay, first_args), stay(window_start), stay(atom_bias))
    message_shape = jax.ShapeDtypeStruct((RIM + 16, channels), BF)
    atoms1, send, keep, near_message, far_message = call(
        functools.partial(first_edge, share=share),
        [atom_shape, packed_shape, packed_shape, message_shape, message_shape],
        edge_scratch,
        [SMEM, SMEM] + [VMEM] * 13,
        2_000_000_000,
        16,
    )(
        info, window_start, ids, atom_acts, near_acts, far_acts, first_gain, first_qkv, first_out,
        up_weight, *mixed1,
    )

    chip_sum = (keep.astype(F32) + to_near(send).astype(F32)).astype(BF)
    chip_sum, near_bias = lax.optimization_barrier((chip_sum, pair_bias))
    bias_near = to_near(near_bias)
    sums = [lax.dynamic_slice_in_dim(chip_sum, pair * share, share, axis=0)]
    for step in range(1, pairs):
        piece = lax.dynamic_slice_in_dim(chip_sum, (pair + step) % pairs * share, share, axis=0)
        sums.append(along_pairs(piece, step))
    share_shape = jax.ShapeDtypeStruct((share, wide), BF)
    gain_row = token_gain.reshape(1, -1)
    act, normed = call(
        functools.partial(mean_tokens, count=len(sums)), [share_shape] * 2, [], [VMEM] * (len(sums) + 1), 1_000_000
    )(*sums, gain_row)

    group = LANES // share
    solo = group == 2
    split = 1 if solo else group
    moved_keys = [along_rows(normed, step) for step in range(row_count - 1, 0, -1)]
    own_keys = [normed] + moved_keys[::-1]
    near_keys = [to_near(x) for x in own_keys[:split]]
    other_acts = [along_pairs(act, step) for step in range(1, pairs)]
    half_shape = jax.ShapeDtypeStruct((half, wide), BF)
    wide_shape = jax.ShapeDtypeStruct((half, wide), F32)
    act_rows, queries, gates = call(
        functools.partial(query_tokens, others=len(other_acts)),
        [half_shape, half_shape, wide_shape],
        [pltpu.VMEM((wide, wide), BF)] * 2 + [pltpu.SemaphoreType.DMA((2,))],
        [SMEM, HBM] + [VMEM] * (2 + len(other_acts)),
        1_000,
    )(info, stay(token_weight), gain_row, act, *other_acts)

    rest = row_count - split

    def key_scratch(count):
        return [pltpu.VMEM((2 * count * share, wide), BF)] * 3

    def bias_shape(count):
        return jax.ShapeDtypeStruct((heads, half, 2 * count * share), BF)

    head_shape = jax.ShapeDtypeStruct((heads, half, LANES), F32)
    weight_shape = jax.ShapeDtypeStruct((wide, wide), BF)
    copies = 2 + 2 * pairs * (row_count // group)
    bias_scratch = [
        pltpu.VMEM((heads, half, 2 * split * share), BF),
        pltpu.VMEM((2, heads, half, LANES), BF),
        pltpu.SemaphoreType.DMA((copies,)),
    ]
    *held, mixed, tops, totals = call(
        functools.partial(attend_first, steps=list(range(split)), solo=solo),
        [weight_shape, weight_shape, bias_shape(rest), wide_shape, head_shape, head_shape],
        key_scratch(split) + bias_scratch,
        [SMEM, HBM, VMEM, HBM, HBM] + [VMEM] * (2 * split),
        1_000,
    )(info, stay(token_weight), queries, stay(pair_bias), stay(bias_near), *own_keys[:split], *near_keys)
    rest_keys, mixed = lax.optimization_barrier((own_keys[split:], mixed))
    rest_near = [to_near(x) for x in rest_keys]
    part = call(
        functools.partial(attend_rest, steps=list(range(split, row_count)), solo=solo),
        packed_shape,
        key_scratch(rest),
        [VMEM] * 4 + [SMEM] + [VMEM] * (3 + 2 * rest),
        2_000_000_000,
    )(queries, *held, info, mixed, tops, totals, *rest_keys, *rest_near)

    near_message, far_message, part = lax.optimization_barrier((near_message, far_message, part))
    parts = [along_pairs(part, step) for step in range(1, pairs)]
    near_message, far_message, parts = lax.optimization_barrier(
        (to_near(near_message), to_far(far_message), parts)
    )
    parts = [part] + parts
    own_back = call(
        functools.partial(finish_tokens, parts_count=pairs),
        jax.ShapeDtypeStruct((half, channels), BF),
        [],
        [VMEM] * (4 + pairs),
        200_000_000,
    )(act_rows, gates, token_out, down_weight, *parts)

    near_back = to_near(own_back)
    if share >= RIM:
        last_rows = own_back[half - RIM :]
        first_rows = own_back[:RIM]
    else:
        both = jnp.where(side == 0, jnp.stack([own_back, near_back]), jnp.stack([near_back, own_back]))
        both = both.reshape(2, pairs, share, channels).transpose(1, 0, 2, 3).reshape(tok_rows, channels)
        last_rows = both[tok_rows - RIM :]
        first_rows = both[:RIM]
    far_back = to_beyond(jnp.where(side == 1, last_rows, first_rows))

    atoms2, *mixed2 = call(
        functools.partial(second_inner, share=share),
        [atom_shape, atom_shape] + edge_shapes,
        inner_scratch,
        [SMEM, SMEM] + [VMEM] * 7,
        1_500_000_000,
        16,
    )(info, window_start, ids, atoms1, own_back, near_back, second_gain, second_qkv, atom_bias)
    return call(
        functools.partial(second_edge, share=share, columns=col_count),
        atom_shape,
        edge_scratch + [pltpu.VMEM((atom_bias.shape[0], 2 * RIM, atom_bias.shape[2]), BF)],
        [SMEM, SMEM] + [VMEM] * 14,
        300_000_000,
        16,
    )(
        info, window_start, atoms2, near_message, far_message, own_back, near_back, far_back,
        second_gain, second_qkv, second_out, atom_bias, *mixed2,
    )


def solution(mesh):
    atoms = P(("group", "row", "col"))
    in_specs = (
        P(("group", "row", "col"), None),
        P(), P(), P(), P(), P(), P(),
        P(None, ("group", "row", "col"), None),
        atoms,
        atoms,
        P(), P(), P(), P(), P(),
        P(None, ("group", "row"), "col"),
    )
    out_specs = P(("group", "row", "col"), None)
    return jax.shard_map(body, mesh=mesh, in_specs=in_specs, out_specs=out_specs, check_vma=False)
```

```python
import functools
import math

import jax
import jax.numpy as jnp
from jax import lax
from jax.experimental import pallas as pl
from jax.experimental.pallas import tpu as pltpu
from jax.sharding import PartitionSpec as P

BF = jnp.bfloat16
F32 = jnp.float32
RIM = 64
LANES = 128
VMEM = pl.BlockSpec(memory_space=pltpu.VMEM)
SMEM = pl.BlockSpec(memory_space=pltpu.SMEM)
HBM = pl.BlockSpec(memory_space=pltpu.HBM)


def dot(a, b):
    return jnp.dot(a, b, preferred_element_type=F32)


def dot_nt(a, b):
    return lax.dot_general(a, b, (((1,), (1,)), ((), ())), preferred_element_type=F32)


def dot_tn(a, b):
    return lax.dot_general(a, b, (((0,), (0,)), ((), ())), preferred_element_type=F32)


def norm_rows(values, gain):
    center = values - jnp.mean(values, axis=-1, keepdims=True)
    spread = jnp.mean(center * center, axis=-1, keepdims=True)
    return center * lax.rsqrt(spread + 1e-05) * gain


def token_of(count, share, first_parity, dim=0):
    half = count // 2
    row = lax.broadcasted_iota(jnp.int32, (count, 1) if dim == 0 else (1, count), dim)
    second = (row >= half).astype(jnp.int32)
    inner = row - second * half
    shift = share.bit_length() - 1
    share_pair = inner >> shift
    inside = inner & (share - 1)
    parity = first_parity + second - 2 * first_parity * second
    return (2 * share_pair + parity) * share + inside


def one_hot(table_ids, atom_ids):
    return jnp.where(table_ids == atom_ids, 1.0, 0.0).astype(BF)


def project(rows, gain, qkv, q, k, v, at):
    channels = rows.shape[1]
    packed = dot(norm_rows(rows.astype(F32), gain).astype(BF), qkv).astype(BF)
    place = slice(at, at + rows.shape[0])
    q[place, :] = packed[:, :channels]
    k[place, :] = packed[:, channels : 2 * channels].astype(F32)
    v[place, :] = packed[:, 2 * channels :].astype(F32)


def attend_windows(places, bias, q, k, v, mixed):
    heads, _, span = bias.shape
    channels = q.shape[1]
    block = span - 3 * RIM // 2
    size = channels // heads
    scale = 1.0 / math.sqrt(size)
    stacked = heads * block
    head_row = lax.broadcasted_iota(jnp.int32, (heads, block, channels), 0).reshape(stacked, channels)
    head_lane = lax.broadcasted_iota(jnp.int32, (stacked, channels), 1) // size
    own_head = jnp.where(head_row == head_lane, 1.0, 0.0).astype(BF)
    lane_head = lax.broadcasted_iota(jnp.int32, (block, channels), 1) // size
    ones = jnp.ones((span, channels), BF)

    def picked(stack):
        out = stack[:block]
        for head in range(1, heads):
            out = jnp.where(lane_head == head, stack[head * block : (head + 1) * block], out)
        return out

    scores = []
    for query_at, _, key_at in places:
        spread = jnp.concatenate([q[pl.ds(query_at, block), :]] * heads, axis=0) * own_head
        scores.append(dot_nt(spread, k[pl.ds(key_at, span), :].astype(BF)))
    raised = []
    for (_, bias_at, _), score in zip(places, scores):
        tile = bias[:, pl.ds(bias_at, block), :].reshape(stacked, span).astype(F32)
        score = score * scale + tile
        raised.append(jnp.exp(score - jnp.max(score, axis=-1, keepdims=True)).astype(BF))
    for (query_at, _, key_at), weights in zip(places, raised):
        values = jnp.concatenate([v[pl.ds(key_at, span), :].astype(BF), ones], axis=1)
        out = dot(weights, values)
        mixed[pl.ds(query_at, block), :] = (picked(out[:, :channels]) / picked(out[:, channels:])).astype(BF)


class starts_from:
    def __init__(self, starts, base):
        self.starts, self.base, self.shape = starts, base, starts.shape

    def __getitem__(self, window):
        return self.starts[window] - self.base


def window_group(windows, edge):
    return next(size for size in (15, 12, 10, 6, 5, 4, 3, 2, 1) if (windows - 2 * edge) % size == 0)


def inner_windows(offsets, bias, q, k, v, mixed, edge_q, edge_k, edge_v, ready=None):
    windows = offsets.shape[0]
    rows = q.shape[0]
    block = rows // windows
    edge = RIM // block
    group = window_group(windows, edge)

    def one_group(step, carry):
        if ready is not None:
            ready(step)
        places = []
        for member in range(group):
            window = edge + step * group + member
            at = pl.multiple_of(window * block, block)
            places.append((at, at, offsets[window]))
        attend_windows(places, bias, q, k, v, mixed)
        return carry

    lax.fori_loop(0, (windows - 2 * edge) // group, one_group, 0)
    edge_q[:RIM, :] = q[:RIM, :]
    edge_q[RIM:, :] = q[rows - RIM :, :]
    for source, target in ((k, edge_k), (v, edge_v)):
        target[: 2 * RIM, :] = source[: 2 * RIM, :]
        target[2 * RIM :, :] = source[rows - 2 * RIM :, :]


def edge_windows(offsets, bias, gain, qkv, near, far, side, edge_q, edge_k, edge_v, k, v, mixed):
    windows = offsets.shape[0]
    channels = edge_q.shape[1]
    block = bias.shape[2] - 3 * RIM // 2
    rows = windows * block
    edge = RIM // block
    for source, target in ((edge_k, k), (edge_v, v)):
        target[RIM : 3 * RIM, :] = source[: 2 * RIM, :]
        target[3 * RIM : 5 * RIM, :] = source[2 * RIM :, :]
    normed = norm_rows(jnp.concatenate([near, far], axis=0), gain).astype(BF)
    packed = dot(normed, qkv[:, channels:]).astype(BF).astype(F32)
    near_at = pl.multiple_of(jnp.where(side == 0, 5 * RIM, 0), RIM)
    far_at = pl.multiple_of(5 * RIM - near_at, RIM)
    for at, part in ((near_at, packed[:RIM]), (far_at, packed[RIM:])):
        k[pl.ds(at, RIM), :] = part[:, :channels]
        v[pl.ds(at, RIM), :] = part[:, channels:]
    places = []
    for member in range(edge):
        places.append((member * block, member * block, offsets[member]))
    for member in range(edge):
        window = windows - edge + member
        at = RIM + member * block
        places.append((at, at, offsets[window] - (rows - 4 * RIM)))
    attend_windows(places, bias, edge_q, k, v, mixed)


def fetches(sources, targets, sems, first=0):
    return [
        pltpu.make_async_copy(source, target, sems.at[first + index])
        for index, (source, target) in enumerate(zip(sources, targets))
    ]


def first_inner(
    info, acts_far, gain_far, qkv_far, starts_far, bias_far, mixed, edge_q, edge_k, edge_v, edge_bias,
    q, k, v, acts, gain, qkv, starts, bias, sems, bias_sems, *, pieces
):
    rows = acts.shape[0]
    windows = starts.shape[0]
    block = rows // windows
    span = window_group(windows, RIM // block) * block
    part = rows // pieces
    cuts = [pl.ds(index * part, part) for index in range(pieces)]
    small = fetches([gain_far, qkv_far, starts_far], [gain, qkv, starts], sems)
    moving = fetches([acts_far.at[cut, :] for cut in cuts], [acts.at[cut, :] for cut in cuts], sems, 3)
    ends = fetches(
        [bias_far.at[:, pl.ds(at, RIM), :] for at in (0, rows - RIM)],
        [edge_bias.at[:, pl.ds(at, RIM), :] for at in (0, RIM)],
        sems,
        3 + pieces,
    )

    def tile(step):
        place = pl.ds(pl.multiple_of(RIM + step * span, block), span)
        return pltpu.make_async_copy(bias_far.at[:, place, :], bias.at[:, place, :], bias_sems.at[step])

    for copy in moving[:1] + small + moving[1:]:
        copy.start()
    for copy in small:
        copy.wait()
    step = 256
    for index, copy in enumerate(moving):
        copy.wait()
        if index == 0:
            for group in range(bias_sems.shape[0]):
                tile(group).start()
            for end in ends:
                end.start()
        for at in range(index * part, (index + 1) * part, step):
            project(acts[at : at + step, :], gain[...], qkv[...], q, k, v, at)
    inner_windows(
        starts_from(starts, info[4]), bias, q, k, v, mixed, edge_q, edge_k, edge_v, lambda index: tile(index).wait()
    )
    for end in ends:
        end.wait()


def first_edge(
    info, offsets, ids, acts, near, far, gain, qkv, out_weight, up, mixed, edge_q, edge_k, edge_v, bias,
    atoms, send, keep, near_message, far_message, k, v, edge_mixed, *, share
):
    side = info[0]
    rows = acts.shape[0]
    close_inner(acts, mixed, out_weight, atoms)
    edge_windows(
        starts_from(offsets, info[4] - RIM), bias, gain[...], qkv[...], near[...].astype(F32), far[...].astype(F32), side,
        edge_q, edge_k, edge_v, k, v, edge_mixed,
    )
    close_edge(acts, edge_mixed, out_weight, atoms)
    step = 256
    tokens = 2 * send.shape[0]
    half = tokens // 2
    head_ids = ids[:, :RIM]
    tail_ids = ids[:, rows - RIM :]
    for message, last in ((near_message, 1 - side), (far_message, side)):
        at = pl.multiple_of(last * (rows - RIM), RIM)
        message[:RIM, :] = atoms[pl.ds(at, RIM), :]
        sent = head_ids + last * (tail_ids - head_ids)
        coded = jnp.concatenate([sent >> 6, sent & 63], axis=1).astype(F32)
        message[RIM:, :] = jnp.broadcast_to(coded, (16, 2 * RIM)).astype(BF)
    member = one_hot(token_of(tokens, share, 1 - side) + info[1] * tokens, ids[...])
    wide = up.shape[1]
    atom_rows = atoms[...]
    for at in range(0, wide, step):
        feat = jnp.maximum(dot(atom_rows, up[:, at : at + step]), 0.0).astype(BF)
        sums = dot(member, feat).astype(BF)
        send[:, at : at + step] = sums[:half]
        keep[:, at : at + step] = sums[half:]
    count = dot(member, jnp.ones((rows, LANES), BF))
    high = jnp.floor(count * (1.0 / 64.0))
    low = count - 64.0 * high
    lane = lax.broadcasted_iota(jnp.int32, (tokens, LANES), 1)
    pieces = jnp.where(lane == 0, high, jnp.where(lane == 1, low, 0.0)).astype(BF)
    send[:, wide:] = pieces[:half]
    keep[:, wide:] = pieces[half:]


def close_inner(acts, mixed, out_weight, out):
    rows = acts.shape[0]
    step = 256
    for at in range(0, rows, step):
        first, last = max(at, RIM), min(at + step, rows - RIM)
        part = acts[first:last, :].astype(F32) + dot(mixed[first:last, :], out_weight[...])
        out[first:last, :] = part.astype(BF)


def close_edge(acts, mixed, out_weight, out):
    rows = acts.shape[0]
    moved = dot(mixed[...], out_weight[...])
    out[:RIM, :] = (acts[:RIM, :].astype(F32) + moved[:RIM]).astype(BF)
    out[rows - RIM :, :] = (acts[rows - RIM :, :].astype(F32) + moved[RIM:]).astype(BF)


def mean_tokens(*refs, count):
    parts, gain, act, normed = refs[:count], refs[count], refs[count + 1], refs[count + 2]
    total = parts[0][...].astype(F32)
    for part in parts[1:]:
        total = total + part[...].astype(F32)
    wide = act.shape[1]
    atoms = total[:, wide : wide + 1] * 64.0 + total[:, wide + 1 : wide + 2]
    rounded = (total[:, :wide] / atoms).astype(BF)
    act[...] = rounded
    normed[...] = norm_rows(rounded.astype(F32), gain[...]).astype(BF)


def place_keys(info, own, near, tokens, steps, solo):
    share = own[0].shape[0]
    group = LANES // share
    place = info[1] & (group - 1)
    lead = 2 * share if solo else 0
    for own_rows, near_rows, step in zip(own, near, steps):
        if solo and step < group:
            places = (0, share)
        else:
            at = lead + (step // group - (0 not in steps)) * 2 * LANES + (place ^ (step % group)) * share
            places = (at, at + LANES)
        for rows, at in zip((own_rows, near_rows), places):
            tokens[pl.ds(pl.multiple_of(at, share), share), :] = rows[...]


def bias_pieces(info, biases_far, block, targets, share):
    count = targets[0].shape[1]
    group = LANES // share
    side, row = info[0], info[1]
    slot = pl.multiple_of(((row // group) ^ block) * LANES, LANES)
    sources, places = [], []
    for bias_far, target in zip(biases_far, targets):
        for pair in range(count // share):
            at = pl.multiple_of((2 * pair + side) * share, share)
            sources.append(bias_far.at[:, pl.ds(at, share), pl.ds(slot, LANES)])
            places.append(target.at[:, pl.ds(pair * share, share), :])
    return sources, places


def split_bias(info, slots, bias, rest):
    heads, count = bias.shape[0], bias.shape[1]
    lane = lax.broadcasted_iota(jnp.int32, (count, LANES), 1)
    lower = lane < LANES // 2
    first = info[1] & 1
    for head in range(heads):
        own, near = slots[0, head].astype(F32), slots[1, head].astype(F32)
        low = jnp.where(lower, own, pltpu.roll(near, LANES // 2, 1))
        high = jnp.where(lower, pltpu.roll(own, LANES // 2, 1), near)
        bias[head] = jnp.where(first == 0, low, high).astype(BF)
        rest[head, :, :LANES] = jnp.where(first == 0, high, low).astype(BF)


def attend_heads(queries, biases, keys, values, previous, keep):
    count, wide = queries.shape
    heads = biases[0].shape[0]
    size = wide // heads
    scale = 1.0 / math.sqrt(size)
    span = keys.shape[0] // LANES
    lane = lax.broadcasted_iota(jnp.int32, (count, LANES), 1)
    out = [None] * (wide // LANES)
    together = 4
    for start in range(0, heads, together):
        members = []
        for head in range(start, start + together):
            first, last = head * size, (head + 1) * size
            low, high = first // LANES, -(-last // LANES)
            chunk = slice(low * LANES, high * LANES)
            chunk_lane = lax.broadcasted_iota(jnp.int32, (count, (high - low) * LANES), 1) + low * LANES
            inside = (chunk_lane >= first) & (chunk_lane < last)
            query = jnp.where(inside, queries[:, chunk].astype(F32), 0.0).astype(BF)
            members.append((head, first, low, high, dot_nt(query, keys[:, chunk])))
        raised = []
        for head, first, low, high, score in members:
            tile = jnp.concatenate([bias[head] for bias in biases], axis=1)
            score = score * scale + tile.astype(F32)
            top = jnp.broadcast_to(jnp.max(score, axis=-1, keepdims=True), (count, LANES))
            if previous is not None:
                former = previous[1][head]
                top = jnp.maximum(top, former)
            weights = jnp.exp(score - jnp.concatenate([top] * span, axis=1))
            total = jnp.broadcast_to(jnp.sum(weights, axis=-1, keepdims=True), (count, LANES))
            fade = None
            if previous is not None:
                fade = jnp.exp(former - top)
                total = total + fade * previous[2][head]
            keep(head, top, total)
            raised.append((weights.astype(BF), fade, total))
        for (head, first, low, high, _), (weights, fade, total) in zip(members, raised):
            mixed = dot(weights, values[:, low * LANES : high * LANES])
            if previous is not None:
                inverse = 1.0 / total
            for block in range(low, high):
                piece = mixed[:, (block - low) * LANES : (block - low + 1) * LANES]
                if previous is not None:
                    piece = (piece + fade * previous[0][:, block * LANES : (block + 1) * LANES]) * inverse
                if out[block] is not None:
                    piece = jnp.where(lane + block * LANES >= first, piece, out[block])
                out[block] = piece
    return out


def attend_first(info, weight_far, gain, own_act, own_far, near_far, *refs, others, steps, solo):
    rows_count = len(steps)
    other_acts, refs = refs[:others], refs[others:]
    own, near, refs = refs[:rows_count], refs[rows_count : 2 * rows_count], refs[2 * rows_count :]
    act, queries, gates, key_weight, value_weight, pair_bias, mixed, tops, totals = refs[:9]
    query_weight, gate_weight, tokens, keys, values, bias, slots, sems = refs[9:]
    share, wide = own[0].shape
    weights = fetches(
        [weight_far.at[:, pl.ds(part * wide, wide)] for part in range(4)],
        [query_weight, key_weight, value_weight, gate_weight],
        sems,
    )
    targets = (slots.at[0], slots.at[1]) if solo else [bias.at[:, :, pl.ds(at, LANES)] for at in (0, LANES)]
    tiles = fetches(*bias_pieces(info, (own_far, near_far), 0, targets, share), sems, 4)
    for copy in weights[:3] + tiles + weights[3:]:
        copy.start()
    pairs = others + 1
    place = info[2]
    act[pl.ds(pl.multiple_of(place * share, share), share), :] = own_act[...]
    for step in range(1, pairs):
        at = lax.rem(place - step + pairs, pairs) * share
        act[pl.ds(pl.multiple_of(at, share), share), :] = other_acts[step - 1][...]
    normed = norm_rows(act[...].astype(F32), gain[...]).astype(BF)
    place_keys(info, own, near, tokens, steps, solo)
    weights[0].wait()
    queries[...] = dot(normed, query_weight[...]).astype(BF)
    weights[1].wait()
    keys[...] = dot(tokens[...], key_weight[...]).astype(BF)
    weights[2].wait()
    values[...] = dot(tokens[...], value_weight[...]).astype(BF)
    for copy in tiles:
        copy.wait()
    if solo:
        split_bias(info, slots, bias, pair_bias)
    else:
        pair_bias[...] = jnp.zeros(pair_bias.shape, BF)

    def keep(head, top, total):
        tops[head] = top
        totals[head] = total

    out = attend_heads(queries, [bias], keys, values, None, keep)
    for block, piece in enumerate(out):
        mixed[:, block * LANES : (block + 1) * LANES] = piece
    weights[3].wait()
    gates[...] = jax.nn.sigmoid(dot(normed, gate_weight[...]).astype(BF).astype(F32))


def attend_rest(
    info, own_far, near_far, queries, key_weight, value_weight, pair_bias, former, former_top, former_total,
    *refs, steps, solo
):
    rows_count = len(steps)
    own, near = refs[:rows_count], refs[rows_count : 2 * rows_count]
    packed, tokens, keys, values, bias, sems = refs[2 * rows_count :]
    heads = bias.shape[0]
    count, wide = queries.shape
    tiles = []
    for block in range(bias.shape[2] // (2 * LANES)):
        targets = [bias.at[:, :, pl.ds((2 * block + half) * LANES, LANES)] for half in range(2)]
        sources, places = bias_pieces(info, (own_far, near_far), block + 1, targets, own[0].shape[0])
        tiles += fetches(sources, places, sems, len(tiles))
    for copy in tiles:
        copy.start()
    place_keys(info, own, near, tokens, steps, solo)
    keys[...] = dot(tokens[...], key_weight[...]).astype(BF)
    values[...] = dot(tokens[...], value_weight[...]).astype(BF)
    for copy in tiles:
        copy.wait()
    lane = lax.broadcasted_iota(jnp.int32, (count, LANES), 1)
    ends = [jnp.zeros((count, LANES), F32), jnp.ones((count, LANES), F32)]

    def keep(head, top, total):
        ends[0] = jnp.where(lane == head, top, ends[0])
        ends[1] = jnp.where(lane == head, total, ends[1])

    biases = [pair_bias, bias] if solo else [bias]
    out = attend_heads(queries, biases, keys, values, (former, former_top, former_total), keep)
    for block, piece in enumerate(out):
        packed[:, block * LANES : (block + 1) * LANES] = piece.astype(BF)
    logs = ends[0] + jnp.log(ends[1])
    first = logs.astype(BF).astype(F32)
    rest = logs - first
    second = rest.astype(BF).astype(F32)
    rest = rest - second
    packed[:, wide:] = (first + pltpu.roll(second, heads, 1) + pltpu.roll(rest, 2 * heads, 1)).astype(BF)


def finish_tokens(act, gates, token_out, down, *refs, parts_count):
    parts, back = refs[:parts_count], refs[parts_count]
    count, wide = act.shape
    heads = 16
    size = wide // heads
    logs = []
    for part in parts:
        packed = part[:, wide:].astype(F32)
        logs.append(
            packed + pltpu.roll(packed, LANES - heads, 1) + pltpu.roll(packed, LANES - 2 * heads, 1)
        )
    top = functools.reduce(jnp.maximum, logs)
    weights = [jnp.exp(log - top) for log in logs]
    total = functools.reduce(jnp.add, weights)
    head = lax.broadcasted_iota(jnp.int32, (LANES, wide), 0)
    feature = lax.broadcasted_iota(jnp.int32, (LANES, wide), 1)
    expand = jnp.where((feature >= head * size) & (feature < (head + 1) * size), 1.0, 0.0).astype(BF)
    mixed = jnp.zeros((count, wide), F32)
    for part, weight in zip(parts, weights):
        factor = weight / total
        coarse = factor.astype(BF)
        fine = (factor - coarse.astype(F32)).astype(BF)
        mixed = mixed + (dot(coarse, expand) + dot(fine, expand)) * part[:, :wide].astype(F32)
    gated = (mixed * gates[...]).astype(BF)
    result = (act[...].astype(F32) + dot(gated, token_out[...])).astype(BF)
    back[...] = dot(result, down[...]).astype(BF)


def second_inner(
    info, offsets, ids, atoms1, own_back, near_back, gain, qkv, bias,
    atoms2, mixed, edge_q, edge_k, edge_v, q, k, v, *, share
):
    tokens = 2 * own_back.shape[0]
    table = jnp.concatenate([own_back[...], near_back[...]], axis=0)
    table_ids = (token_of(tokens, share, info[0], 1) + info[1] * tokens).astype(F32)
    step = 256
    for at in range(0, atoms1.shape[0], step):
        members = []
        for first in range(at, at + step, LANES):
            atom_ids = jnp.broadcast_to(ids[:, first : first + LANES].astype(F32), (LANES, LANES)).T
            members.append(
                jnp.concatenate(
                    [one_hot(table_ids[:, t : t + LANES], atom_ids) for t in range(0, tokens, LANES)], axis=1
                )
            )
        member = jnp.concatenate(members, axis=0)
        atoms2[at : at + step, :] = (atoms1[at : at + step, :].astype(F32) + dot(member, table)).astype(BF)
    for at in range(0, atoms1.shape[0], step):
        project(atoms2[at : at + step, :], gain[...], qkv[...], q, k, v, at)
    inner_windows(starts_from(offsets, info[4]), bias, q, k, v, mixed, edge_q, edge_k, edge_v)


def second_edge(
    info, offsets, atoms2, near, far, own_back, near_back, far_back, gain, qkv, out_weight, bias,
    mixed, edge_q, edge_k, edge_v, result, k, v, edge_mixed, ends, *, share, columns
):
    side, column = info[0], info[3]
    close_inner(atoms2, mixed, out_weight, result)
    ends[:, :RIM, :] = bias[:, :RIM, :]
    ends[:, RIM:, :] = bias[:, bias.shape[1] - RIM :, :]
    tokens = 2 * own_back.shape[0]
    table = jnp.concatenate([own_back[...], near_back[...]], axis=0)
    table_ids = token_of(tokens, share, side)
    first_token = (info[1] * tokens).astype(F32)

    def rim_ids(message):
        packed = message[RIM:, :].astype(F32)
        return (packed[0:1, :RIM] * 64.0 + packed[0:1, RIM:] - first_token).astype(jnp.int32)

    near_rows = near[:RIM, :].astype(F32) + dot_tn(one_hot(table_ids, rim_ids(near)), table)
    far_token = rim_ids(far)
    beyond = lax.broadcasted_iota(jnp.int32, (RIM, 1), 0) + jnp.where(
        column == 0, -RIM, jnp.where(column == columns - 1, tokens, 4 * tokens)
    )
    far_rows = (
        far[:RIM, :].astype(F32)
        + dot_tn(one_hot(table_ids, far_token), table)
        + dot_tn(one_hot(beyond, far_token), far_back[...])
    )
    edge_windows(
        starts_from(offsets, info[4] - RIM), ends, gain[...], qkv[...], near_rows.astype(BF).astype(F32), far_rows.astype(BF).astype(F32), side,
        edge_q, edge_k, edge_v, k, v, edge_mixed,
    )
    close_edge(atoms2, edge_mixed, out_weight, result)


def stay(x):
    return pltpu.with_memory_space_constraint(x, pltpu.HBM)


def call(kernel, outs, scratch, specs, flops, limit=20):
    return pl.pallas_call(
        kernel,
        out_shape=outs,
        in_specs=specs,
        out_specs=jax.tree.map(lambda _: VMEM, outs),
        scratch_shapes=scratch,
        compiler_params=pltpu.CompilerParams(vmem_limit_bytes=limit * 1024 * 1024),
        cost_estimate=pl.CostEstimate(flops=flops, bytes_accessed=1_000, transcendentals=1_000),
    )


def body(
    atom_acts, first_gain, first_qkv, first_out, second_gain, second_qkv, second_out, atom_bias, window_start,
    atom_token, up_weight, token_gain, token_weight, token_out, down_weight, pair_bias,
):
    rows, channels = atom_acts.shape
    heads, tok_rows, slots = pair_bias.shape
    wide = token_weight.shape[0]
    row_count, col_count = lax.axis_size("row"), lax.axis_size("col")
    pairs = col_count // 2
    share = tok_rows // col_count
    half = tok_rows // 2
    row, col = lax.axis_index("row"), lax.axis_index("col")
    side, pair = col % 2, col // 2
    info = jnp.stack([side, row, pair, col, (row * col_count + col) * rows]).astype(jnp.int32)
    devices = row_count * col_count
    group_count = lax.axis_size("group")

    def to_near(x):
        return lax.ppermute(x, "col", [(i, i ^ 1) for i in range(col_count)])

    def swapped(x, swap):
        pairs_list = []
        for i in range(group_count * devices):
            group_at, at = divmod(i, devices)
            if at in swap:
                target = group_at * devices + swap[at]
            else:
                target = (group_at ^ 1) * devices + at if group_count % 2 == 0 else i
            pairs_list.append((i, target))
        return lax.ppermute(x, ("group", "row", "col"), pairs_list)

    def to_far(x):
        return swapped(x, {i: i + 1 if i % 2 else i - 1 for i in range(1, devices - 1)})

    def to_beyond(x):
        swap = {}
        for i in range(1, row_count):
            first, last = i * col_count, i * col_count - 1
            for one, other in ((first, first - col_count + 1), (last, last + col_count - 1)):
                swap[one], swap[other] = other, one
        if col_count > 4:
            for i in range(devices):
                if 2 <= i % col_count < col_count - 2:
                    swap[i] = i ^ 1
        return swapped(x, swap)

    def along_pairs(x, step):
        return lax.ppermute(
            x, "col", [(2 * i + k, 2 * ((i + step) % pairs) + k) for i in range(pairs) for k in range(2)]
        )

    def along_rows(x, step):
        return lax.ppermute(x, "row", [(i, i ^ step) for i in range(row_count)])

    def rim_of(x, last):
        return lax.dynamic_slice_in_dim(x, jnp.where(last, rows - RIM, 0), RIM, axis=0)

    near_acts = to_near(rim_of(atom_acts, side == 0))
    far_acts = to_far(rim_of(atom_acts, side == 1))

    ids = atom_token.reshape(1, rows)
    inner_scratch = [
        pltpu.VMEM((rows, channels), BF),
        pltpu.VMEM((rows, channels), F32),
        pltpu.VMEM((rows, channels), F32),
    ]
    edge_scratch = [
        pltpu.VMEM((6 * RIM, channels), F32),
        pltpu.VMEM((6 * RIM, channels), F32),
        pltpu.VMEM((2 * RIM, channels), BF),
    ]
    atom_shape = jax.ShapeDtypeStruct((rows, channels), BF)
    edge_shapes = [
        jax.ShapeDtypeStruct((2 * RIM, channels), BF),
        jax.ShapeDtypeStruct((4 * RIM, channels), F32),
        jax.ShapeDtypeStruct((4 * RIM, channels), F32),
    ]
    packed_shape = jax.ShapeDtypeStruct((half, wide + LANES), BF)
    first_gain, second_gain = first_gain.reshape(1, -1), second_gain.reshape(1, -1)
    pieces = 2
    windows = window_start.shape[0]
    edge = RIM * windows // rows
    groups = (windows - 2 * edge) // window_group(windows, edge)
    first_args = [atom_acts, first_gain, first_qkv]
    mixed1 = call(
        functools.partial(first_inner, pieces=pieces),
        [atom_shape] + edge_shapes + [jax.ShapeDtypeStruct((atom_bias.shape[0], 2 * RIM, atom_bias.shape[2]), BF)],
        inner_scratch
        + [pltpu.VMEM(x.shape, x.dtype) for x in first_args]
        + [pltpu.SMEM(window_start.shape, jnp.int32), pltpu.VMEM(atom_bias.shape, BF)]
        + [pltpu.SemaphoreType.DMA((5 + pieces,)), pltpu.SemaphoreType.DMA((groups,))],
        [SMEM] + [HBM] * 5,
        1_500_000_000,
        16,
    )(info, *map(stay, first_args), stay(window_start), stay(atom_bias))
    message_shape = jax.ShapeDtypeStruct((RIM + 16, channels), BF)
    atoms1, send, keep, near_message, far_message = call(
        functools.partial(first_edge, share=share),
        [atom_shape, packed_shape, packed_shape, message_shape, message_shape],
        edge_scratch,
        [SMEM, SMEM] + [VMEM] * 13,
        2_000_000_000,
        16,
    )(
        info, window_start, ids, atom_acts, near_acts, far_acts, first_gain, first_qkv, first_out,
        up_weight, *mixed1,
    )

    chip_sum = (keep.astype(F32) + to_near(send).astype(F32)).astype(BF)
    chip_sum, near_bias = lax.optimization_barrier((chip_sum, pair_bias))
    bias_near = to_near(near_bias)
    sums = [lax.dynamic_slice_in_dim(chip_sum, pair * share, share, axis=0)]
    for step in range(1, pairs):
        piece = lax.dynamic_slice_in_dim(chip_sum, (pair + step) % pairs * share, share, axis=0)
        sums.append(along_pairs(piece, step))
    sums, bias_near = lax.optimization_barrier((sums, bias_near))
    share_shape = jax.ShapeDtypeStruct((share, wide), BF)
    gain_row = token_gain.reshape(1, -1)
    act, normed = call(
        functools.partial(mean_tokens, count=len(sums)), [share_shape] * 2, [], [VMEM] * (len(sums) + 1), 1_000_000
    )(*sums, gain_row)

    group = LANES // share
    solo = group == 2
    split = 1 if solo else group
    own_keys = [normed] + [along_rows(normed, step) for step in range(1, row_count)]
    near_keys = [to_near(x) for x in own_keys[:split]]
    other_acts = [along_pairs(act, step) for step in range(1, pairs)]
    half_shape = jax.ShapeDtypeStruct((half, wide), BF)
    wide_shape = jax.ShapeDtypeStruct((half, wide), F32)
    rest = row_count - split

    def key_scratch(count):
        return [pltpu.VMEM((2 * count * share, wide), BF)] * 3

    head_shape = jax.ShapeDtypeStruct((heads, half, LANES), F32)
    weight_shape = jax.ShapeDtypeStruct((wide, wide), BF)
    tile_count = 2 * pairs
    act_rows, queries, gates, *held, mixed, tops, totals = call(
        functools.partial(attend_first, others=len(other_acts), steps=list(range(split)), solo=solo),
        [half_shape, half_shape, wide_shape, weight_shape, weight_shape]
        + [jax.ShapeDtypeStruct((heads, half, LANES), BF), wide_shape, head_shape, head_shape],
        [pltpu.VMEM((wide, wide), BF)] * 2
        + key_scratch(split)
        + [pltpu.VMEM((heads, half, 2 * split * share), BF), pltpu.VMEM((2, heads, half, LANES), BF)]
        + [pltpu.SemaphoreType.DMA((4 + tile_count,))],
        [SMEM, HBM, VMEM, VMEM, HBM, HBM] + [VMEM] * (len(other_acts) + 2 * split),
        1_000,
        24,
    )(
        info, stay(token_weight), gain_row, act, stay(pair_bias), stay(bias_near), *other_acts,
        *own_keys[:split], *near_keys,
    )
    rest_steps = sorted(range(split, row_count), key=lambda step: (step >= group, -step))
    rest_keys, mixed = lax.optimization_barrier(([own_keys[step] for step in rest_steps], mixed))
    rest_near = [to_near(x) for x in rest_keys]
    blocks = row_count // group - 1
    part = call(
        functools.partial(attend_rest, steps=rest_steps, solo=solo),
        packed_shape,
        key_scratch(rest)
        + [pltpu.VMEM((heads, half, 2 * LANES * blocks), BF), pltpu.SemaphoreType.DMA((tile_count * blocks,))],
        [SMEM, HBM, HBM] + [VMEM] * (7 + 2 * rest),
        2_000_000_000,
    )(
        info, stay(pair_bias), stay(bias_near), queries, *held, mixed, tops, totals, *rest_keys, *rest_near,
    )

    near_message, far_message, part = lax.optimization_barrier((near_message, far_message, part))
    parts = [along_pairs(part, step) for step in range(1, pairs)]
    near_message, far_message, parts = lax.optimization_barrier(
        (to_near(near_message), to_far(far_message), parts)
    )
    parts = [part] + parts
    own_back = call(
        functools.partial(finish_tokens, parts_count=pairs),
        jax.ShapeDtypeStruct((half, channels), BF),
        [],
        [VMEM] * (4 + pairs),
        200_000_000,
    )(act_rows, gates, token_out, down_weight, *parts)

    near_back = to_near(own_back)
    if share >= RIM:
        last_rows = own_back[half - RIM :]
        first_rows = own_back[:RIM]
    else:
        both = jnp.where(side == 0, jnp.stack([own_back, near_back]), jnp.stack([near_back, own_back]))
        both = both.reshape(2, pairs, share, channels).transpose(1, 0, 2, 3).reshape(tok_rows, channels)
        last_rows = both[tok_rows - RIM :]
        first_rows = both[:RIM]
    far_back = to_beyond(jnp.where(side == 1, last_rows, first_rows))

    atoms2, *mixed2 = call(
        functools.partial(second_inner, share=share),
        [atom_shape, atom_shape] + edge_shapes,
        inner_scratch,
        [SMEM, SMEM] + [VMEM] * 7,
        1_500_000_000,
        16,
    )(info, window_start, ids, atoms1, own_back, near_back, second_gain, second_qkv, atom_bias)
    return call(
        functools.partial(second_edge, share=share, columns=col_count),
        atom_shape,
        edge_scratch + [pltpu.VMEM((atom_bias.shape[0], 2 * RIM, atom_bias.shape[2]), BF)],
        [SMEM, SMEM] + [VMEM] * 14,
        300_000_000,
        16,
    )(
        info, window_start, atoms2, near_message, far_message, own_back, near_back, far_back,
        second_gain, second_qkv, second_out, atom_bias, *mixed2,
    )


def solution(mesh):
    atoms = P(("group", "row", "col"))
    in_specs = (
        P(("group", "row", "col"), None),
        P(), P(), P(), P(), P(), P(),
        P(None, ("group", "row", "col"), None),
        atoms,
        atoms,
        P(), P(), P(), P(), P(),
        P(None, ("group", "row"), "col"),
    )
    out_specs = P(("group", "row", "col"), None)
    return jax.shard_map(body, mesh=mesh, in_specs=in_specs, out_specs=out_specs, check_vma=False)
```

```python
import functools
import math

import jax
import jax.numpy as jnp
from jax import lax
from jax.experimental import pallas as pl
from jax.experimental.pallas import tpu as pltpu
from jax.sharding import PartitionSpec as P

BF = jnp.bfloat16
F32 = jnp.float32
RIM = 64
LANES = 128
VMEM = pl.BlockSpec(memory_space=pltpu.VMEM)
SMEM = pl.BlockSpec(memory_space=pltpu.SMEM)
HBM = pl.BlockSpec(memory_space=pltpu.HBM)


def dot(a, b):
    return jnp.dot(a, b, preferred_element_type=F32)


def dot_nt(a, b):
    return lax.dot_general(a, b, (((1,), (1,)), ((), ())), preferred_element_type=F32)


def dot_tn(a, b):
    return lax.dot_general(a, b, (((0,), (0,)), ((), ())), preferred_element_type=F32)


def norm_rows(values, gain):
    center = values - jnp.mean(values, axis=-1, keepdims=True)
    spread = jnp.mean(center * center, axis=-1, keepdims=True)
    return center * lax.rsqrt(spread + 1e-05) * gain


def token_of(count, share, first_parity, dim=0):
    half = count // 2
    row = lax.broadcasted_iota(jnp.int32, (count, 1) if dim == 0 else (1, count), dim)
    second = (row >= half).astype(jnp.int32)
    inner = row - second * half
    shift = share.bit_length() - 1
    share_pair = inner >> shift
    inside = inner & (share - 1)
    parity = first_parity + second - 2 * first_parity * second
    return (2 * share_pair + parity) * share + inside


def one_hot(table_ids, atom_ids):
    return jnp.where(table_ids == atom_ids, 1.0, 0.0).astype(BF)


def project(rows, gain, qkv, q, k, v, at):
    channels = rows.shape[1]
    packed = dot(norm_rows(rows.astype(F32), gain).astype(BF), qkv).astype(BF)
    place = slice(at, at + rows.shape[0])
    q[place, :] = packed[:, :channels]
    k[place, :] = packed[:, channels : 2 * channels].astype(F32)
    v[place, :] = packed[:, 2 * channels :].astype(F32)


def attend_windows(places, bias, q, k, v, mixed):
    heads, _, span = bias.shape
    channels = q.shape[1]
    block = span - 3 * RIM // 2
    size = channels // heads
    scale = 1.0 / math.sqrt(size)
    stacked = heads * block
    head_row = lax.broadcasted_iota(jnp.int32, (heads, block, channels), 0).reshape(stacked, channels)
    head_lane = lax.broadcasted_iota(jnp.int32, (stacked, channels), 1) // size
    own_head = jnp.where(head_row == head_lane, 1.0, 0.0).astype(BF)
    lane_head = lax.broadcasted_iota(jnp.int32, (block, channels), 1) // size
    ones = jnp.ones((span, channels), BF)

    def picked(stack):
        out = stack[:block]
        for head in range(1, heads):
            out = jnp.where(lane_head == head, stack[head * block : (head + 1) * block], out)
        return out

    yield
    scores = []
    for query_at, _, key_at in places:
        spread = jnp.concatenate([q[pl.ds(query_at, block), :]] * heads, axis=0) * own_head
        scores.append(dot_nt(spread, k[pl.ds(key_at, span), :].astype(BF)))
    yield
    raised = []
    for (_, bias_at, _), score in zip(places, scores):
        tile = bias[:, pl.ds(bias_at, block), :].reshape(stacked, span).astype(F32)
        score = score * scale + tile
        raised.append(jnp.exp(score - jnp.max(score, axis=-1, keepdims=True)).astype(BF))
    yield
    for (query_at, _, key_at), weights in zip(places, raised):
        values = jnp.concatenate([v[pl.ds(key_at, span), :].astype(BF), ones], axis=1)
        out = dot(weights, values)
        mixed[pl.ds(query_at, block), :] = (picked(out[:, :channels]) / picked(out[:, channels:])).astype(BF)


class starts_from:
    def __init__(self, starts, base):
        self.starts, self.base, self.shape = starts, base, starts.shape

    def __getitem__(self, window):
        return self.starts[window] - self.base


def window_group(windows, edge):
    return next(size for size in (15, 12, 10, 6, 5, 4, 3, 2, 1) if (windows - 2 * edge) % size == 0)


def inner_windows(offsets, bias, q, k, v, mixed, edge_q, edge_k, edge_v, ready=None):
    windows = offsets.shape[0]
    rows = q.shape[0]
    block = rows // windows
    edge = RIM // block
    group = window_group(windows, edge)

    def one_group(step, carry):
        if ready is not None:
            ready(step)
        places = []
        for member in range(group):
            window = edge + step * group + member
            at = pl.multiple_of(window * block, block)
            places.append((at, at, offsets[window]))
        for _ in attend_windows(places, bias, q, k, v, mixed):
            pass
        return carry

    lax.fori_loop(0, (windows - 2 * edge) // group, one_group, 0)
    edge_q[:RIM, :] = q[:RIM, :]
    edge_q[RIM:, :] = q[rows - RIM :, :]
    for source, target in ((k, edge_k), (v, edge_v)):
        target[: 2 * RIM, :] = source[: 2 * RIM, :]
        target[2 * RIM :, :] = source[rows - 2 * RIM :, :]


def edge_windows(offsets, bias, gain, qkv, near, far, side, edge_q, edge_k, edge_v, k, v, mixed):
    windows = offsets.shape[0]
    channels = edge_q.shape[1]
    block = bias.shape[2] - 3 * RIM // 2
    rows = windows * block
    edge = RIM // block
    for source, target in ((edge_k, k), (edge_v, v)):
        target[RIM : 3 * RIM, :] = source[: 2 * RIM, :]
        target[3 * RIM : 5 * RIM, :] = source[2 * RIM :, :]
    normed = norm_rows(jnp.concatenate([near, far], axis=0), gain).astype(BF)
    yield
    packed = dot(normed, qkv[:, channels:]).astype(BF).astype(F32)
    near_at = pl.multiple_of(jnp.where(side == 0, 5 * RIM, 0), RIM)
    far_at = pl.multiple_of(5 * RIM - near_at, RIM)
    for at, part in ((near_at, packed[:RIM]), (far_at, packed[RIM:])):
        k[pl.ds(at, RIM), :] = part[:, :channels]
        v[pl.ds(at, RIM), :] = part[:, channels:]
    places = []
    for member in range(edge):
        places.append((member * block, member * block, offsets[member]))
    for member in range(edge):
        window = windows - edge + member
        at = RIM + member * block
        places.append((at, at, offsets[window] - (rows - 4 * RIM)))
    yield from attend_windows(places, bias, edge_q, k, v, mixed)


def fetches(sources, targets, sems, first=0):
    return [
        pltpu.make_async_copy(source, target, sems.at[first + index])
        for index, (source, target) in enumerate(zip(sources, targets))
    ]


def first_inner(
    info, acts_far, gain_far, qkv_far, starts_far, bias_far, mixed, edge_q, edge_k, edge_v, edge_bias,
    q, k, v, acts, gain, qkv, starts, bias, sems, bias_sems, *, pieces
):
    rows = acts.shape[0]
    windows = starts.shape[0]
    block = rows // windows
    span = window_group(windows, RIM // block) * block
    part = rows // pieces
    cuts = [pl.ds(index * part, part) for index in range(pieces)]
    small = fetches([gain_far, qkv_far, starts_far], [gain, qkv, starts], sems)
    moving = fetches([acts_far.at[cut, :] for cut in cuts], [acts.at[cut, :] for cut in cuts], sems, 3)
    ends = fetches(
        [bias_far.at[:, pl.ds(at, RIM), :] for at in (0, rows - RIM)],
        [edge_bias.at[:, pl.ds(at, RIM), :] for at in (0, RIM)],
        sems,
        3 + pieces,
    )

    def tile(step):
        place = pl.ds(pl.multiple_of(RIM + step * span, block), span)
        return pltpu.make_async_copy(bias_far.at[:, place, :], bias.at[:, place, :], bias_sems.at[step])

    for copy in moving[:1] + small + moving[1:]:
        copy.start()
    for copy in small:
        copy.wait()
    step = 256
    for index, copy in enumerate(moving):
        copy.wait()
        if index == 0:
            for group in range(bias_sems.shape[0]):
                tile(group).start()
            for end in ends:
                end.start()
        for at in range(index * part, (index + 1) * part, step):
            project(acts[at : at + step, :], gain[...], qkv[...], q, k, v, at)
    inner_windows(
        starts_from(starts, info[4]), bias, q, k, v, mixed, edge_q, edge_k, edge_v, lambda index: tile(index).wait()
    )
    for end in ends:
        end.wait()


def first_edge(
    info, offsets, ids, acts, near, far, gain, qkv, out_weight, up, mixed, edge_q, edge_k, edge_v, bias,
    atoms, send, keep, near_message, far_message, k, v, edge_mixed, *, share
):
    side = info[0]
    rows = acts.shape[0]
    edges = edge_windows(
        starts_from(offsets, info[4] - RIM), bias, gain[...], qkv[...], near[...].astype(F32), far[...].astype(F32), side,
        edge_q, edge_k, edge_v, k, v, edge_mixed,
    )
    step = 256
    tokens = 2 * send.shape[0]
    half = tokens // 2
    wide = up.shape[1]
    next(edges)
    close_inner(acts, mixed, out_weight, atoms)
    member = one_hot(token_of(tokens, share, 1 - side) + info[1] * tokens, ids[...])
    next(edges)
    inner = slice(step, rows - step)
    inner_atoms = atoms[inner, :]
    partial_sums = []
    for at in range(0, wide, step):
        feat = jnp.maximum(dot(inner_atoms, up[:, at : at + step]), 0.0).astype(BF)
        partial_sums.append(dot(member[:, inner], feat))
        next(edges, None)
    for _ in edges:
        pass
    close_edge(acts, edge_mixed, out_weight, atoms)
    head_ids = ids[:, :RIM]
    tail_ids = ids[:, rows - RIM :]
    for message, last in ((near_message, 1 - side), (far_message, side)):
        at = pl.multiple_of(last * (rows - RIM), RIM)
        message[:RIM, :] = atoms[pl.ds(at, RIM), :]
        sent = head_ids + last * (tail_ids - head_ids)
        coded = jnp.concatenate([sent >> 6, sent & 63], axis=1).astype(F32)
        message[RIM:, :] = jnp.broadcast_to(coded, (16, 2 * RIM)).astype(BF)
    outer_atoms = jnp.concatenate([atoms[:step, :], atoms[rows - step :, :]], axis=0)
    outer_member = jnp.concatenate([member[:, :step], member[:, rows - step :]], axis=1)
    for at, partial_sum in zip(range(0, wide, step), partial_sums):
        feat = jnp.maximum(dot(outer_atoms, up[:, at : at + step]), 0.0).astype(BF)
        sums = (partial_sum + dot(outer_member, feat)).astype(BF)
        send[:, at : at + step] = sums[:half]
        keep[:, at : at + step] = sums[half:]
    count = dot(member, jnp.ones((rows, LANES), BF))
    high = jnp.floor(count * (1.0 / 64.0))
    low = count - 64.0 * high
    lane = lax.broadcasted_iota(jnp.int32, (tokens, LANES), 1)
    pieces = jnp.where(lane == 0, high, jnp.where(lane == 1, low, 0.0)).astype(BF)
    send[:, wide:] = pieces[:half]
    keep[:, wide:] = pieces[half:]


def close_inner(acts, mixed, out_weight, out, part=0, parts=1):
    rows = acts.shape[0]
    step = 256
    for at in range(rows // parts * part, rows // parts * (part + 1), step):
        first, last = max(at, RIM), min(at + step, rows - RIM)
        moved = acts[first:last, :].astype(F32) + dot(mixed[first:last, :], out_weight[...])
        out[first:last, :] = moved.astype(BF)


def close_edge(acts, mixed, out_weight, out):
    rows = acts.shape[0]
    moved = dot(mixed[...], out_weight[...])
    out[:RIM, :] = (acts[:RIM, :].astype(F32) + moved[:RIM]).astype(BF)
    out[rows - RIM :, :] = (acts[rows - RIM :, :].astype(F32) + moved[RIM:]).astype(BF)


def mean_tokens(*refs, count):
    parts, gain, act, normed = refs[:count], refs[count], refs[count + 1], refs[count + 2]
    total = parts[0][...].astype(F32)
    for part in parts[1:]:
        total = total + part[...].astype(F32)
    wide = act.shape[1]
    atoms = total[:, wide : wide + 1] * 64.0 + total[:, wide + 1 : wide + 2]
    rounded = (total[:, :wide] / atoms).astype(BF)
    act[...] = rounded
    normed[...] = norm_rows(rounded.astype(F32), gain[...]).astype(BF)


def place_keys(info, own, near, tokens, steps, solo):
    share = own[0].shape[0]
    group = LANES // share
    place = info[1] & (group - 1)
    lead = 2 * share if solo else 0
    for own_rows, near_rows, step in zip(own, near, steps):
        if solo and step < group:
            places = (0, share)
        else:
            at = lead + (step // group - (0 not in steps)) * 2 * LANES + (place ^ (step % group)) * share
            places = (at, at + LANES)
        for rows, at in zip((own_rows, near_rows), places):
            tokens[pl.ds(pl.multiple_of(at, share), share), :] = rows[...]


def bias_pieces(info, biases_far, block, targets, share):
    count = targets[0].shape[1]
    group = LANES // share
    side, row = info[0], info[1]
    slot = pl.multiple_of(((row // group) ^ block) * LANES, LANES)
    sources, places = [], []
    for bias_far, target in zip(biases_far, targets):
        for pair in range(count // share):
            at = pl.multiple_of((2 * pair + side) * share, share)
            sources.append(bias_far.at[:, pl.ds(at, share), pl.ds(slot, LANES)])
            places.append(target.at[:, pl.ds(pair * share, share), :])
    return sources, places


def split_bias(info, slots, bias, rest):
    heads, count = bias.shape[0], bias.shape[1]
    lane = lax.broadcasted_iota(jnp.int32, (count, LANES), 1)
    lower = lane < LANES // 2
    first = info[1] & 1
    for head in range(heads):
        own, near = slots[0, head].astype(F32), slots[1, head].astype(F32)
        low = jnp.where(lower, own, pltpu.roll(near, LANES // 2, 1))
        high = jnp.where(lower, pltpu.roll(own, LANES // 2, 1), near)
        bias[head] = jnp.where(first == 0, low, high).astype(BF)
        rest[head, :, :LANES] = jnp.where(first == 0, high, low).astype(BF)


def attend_heads(queries, biases, keys, values, previous, keep):
    count, wide = queries.shape
    heads = biases[0].shape[0]
    size = wide // heads
    scale = 1.0 / math.sqrt(size)
    span = keys.shape[0] // LANES
    lane = lax.broadcasted_iota(jnp.int32, (count, LANES), 1)
    out = [None] * (wide // LANES)
    together = 4
    for start in range(0, heads, together):
        members = []
        for head in range(start, start + together):
            first, last = head * size, (head + 1) * size
            low, high = first // LANES, -(-last // LANES)
            chunk = slice(low * LANES, high * LANES)
            chunk_lane = lax.broadcasted_iota(jnp.int32, (count, (high - low) * LANES), 1) + low * LANES
            inside = (chunk_lane >= first) & (chunk_lane < last)
            query = jnp.where(inside, queries[:, chunk].astype(F32), 0.0).astype(BF)
            members.append((head, first, low, high, dot_nt(query, keys[:, chunk])))
        raised = []
        for head, first, low, high, score in members:
            tile = jnp.concatenate([bias[head] for bias in biases], axis=1)
            score = score * scale + tile.astype(F32)
            top = jnp.broadcast_to(jnp.max(score, axis=-1, keepdims=True), (count, LANES))
            if previous is not None:
                former = previous[1][head]
                top = jnp.maximum(top, former)
            weights = jnp.exp(score - jnp.concatenate([top] * span, axis=1))
            total = jnp.broadcast_to(jnp.sum(weights, axis=-1, keepdims=True), (count, LANES))
            fade = None
            if previous is not None:
                fade = jnp.exp(former - top)
                total = total + fade * previous[2][head]
            keep(head, top, total)
            raised.append((weights.astype(BF), fade, total))
        for (head, first, low, high, _), (weights, fade, total) in zip(members, raised):
            mixed = dot(weights, values[:, low * LANES : high * LANES])
            if previous is not None:
                inverse = 1.0 / total
            for block in range(low, high):
                piece = mixed[:, (block - low) * LANES : (block - low + 1) * LANES]
                if previous is not None:
                    piece = (piece + fade * previous[0][:, block * LANES : (block + 1) * LANES]) * inverse
                if out[block] is not None:
                    piece = jnp.where(lane + block * LANES >= first, piece, out[block])
                out[block] = piece
    return out


def attend_first(info, weight_far, gain, own_act, own_far, near_far, *refs, others, steps, solo):
    rows_count = len(steps)
    other_acts, refs = refs[:others], refs[others:]
    own, near, refs = refs[:rows_count], refs[rows_count : 2 * rows_count], refs[2 * rows_count :]
    act, queries, gates, key_weight, value_weight, pair_bias, rest_bias, mixed, tops, totals = refs[:10]
    query_weight, gate_weight, tokens, keys, values, bias, slots, sems = refs[10:]
    share, wide = own[0].shape
    weights = fetches(
        [weight_far.at[:, pl.ds(part * wide, wide)] for part in range(4)],
        [query_weight, key_weight, value_weight, gate_weight],
        sems,
    )
    targets = (slots.at[0], slots.at[1]) if solo else [bias.at[:, :, pl.ds(at, LANES)] for at in (0, LANES)]
    tiles = fetches(*bias_pieces(info, (own_far, near_far), 0, targets, share), sems, 4)
    later = []
    for block in range(rest_bias.shape[2] // (2 * LANES)):
        targets = [rest_bias.at[:, :, pl.ds((2 * block + half) * LANES, LANES)] for half in range(2)]
        sources, places = bias_pieces(info, (own_far, near_far), block + 1, targets, share)
        later += fetches(sources, places, sems, 4 + len(tiles) + len(later))
    for copy in weights[:3] + tiles + weights[3:] + later:
        copy.start()
    pairs = others + 1
    place = info[2]
    act[pl.ds(pl.multiple_of(place * share, share), share), :] = own_act[...]
    for step in range(1, pairs):
        at = lax.rem(place - step + pairs, pairs) * share
        act[pl.ds(pl.multiple_of(at, share), share), :] = other_acts[step - 1][...]
    normed = norm_rows(act[...].astype(F32), gain[...]).astype(BF)
    place_keys(info, own, near, tokens, steps, solo)
    weights[0].wait()
    queries[...] = dot(normed, query_weight[...]).astype(BF)
    weights[1].wait()
    keys[...] = dot(tokens[...], key_weight[...]).astype(BF)
    weights[2].wait()
    values[...] = dot(tokens[...], value_weight[...]).astype(BF)
    for copy in tiles:
        copy.wait()
    if solo:
        split_bias(info, slots, bias, pair_bias)
    else:
        pair_bias[...] = jnp.zeros(pair_bias.shape, BF)

    def keep(head, top, total):
        tops[head] = top
        totals[head] = total

    out = attend_heads(queries, [bias], keys, values, None, keep)
    for block, piece in enumerate(out):
        mixed[:, block * LANES : (block + 1) * LANES] = piece
    weights[3].wait()
    gates[...] = jax.nn.sigmoid(dot(normed, gate_weight[...]).astype(BF).astype(F32))
    for copy in later:
        copy.wait()


def attend_rest(
    info, queries, key_weight, value_weight, pair_bias, bias, former, former_top, former_total, *refs, steps, solo
):
    rows_count = len(steps)
    own, near = refs[:rows_count], refs[rows_count : 2 * rows_count]
    packed, tokens, keys, values = refs[2 * rows_count :]
    heads = bias.shape[0]
    count, wide = queries.shape
    place_keys(info, own, near, tokens, steps, solo)
    keys[...] = dot(tokens[...], key_weight[...]).astype(BF)
    values[...] = dot(tokens[...], value_weight[...]).astype(BF)
    lane = lax.broadcasted_iota(jnp.int32, (count, LANES), 1)
    ends = [jnp.zeros((count, LANES), F32), jnp.ones((count, LANES), F32)]

    def keep(head, top, total):
        ends[0] = jnp.where(lane == head, top, ends[0])
        ends[1] = jnp.where(lane == head, total, ends[1])

    biases = [pair_bias, bias] if solo else [bias]
    out = attend_heads(queries, biases, keys, values, (former, former_top, former_total), keep)
    for block, piece in enumerate(out):
        packed[:, block * LANES : (block + 1) * LANES] = piece.astype(BF)
    logs = ends[0] + jnp.log(ends[1])
    first = logs.astype(BF).astype(F32)
    rest = logs - first
    second = rest.astype(BF).astype(F32)
    rest = rest - second
    packed[:, wide:] = (first + pltpu.roll(second, heads, 1) + pltpu.roll(rest, 2 * heads, 1)).astype(BF)


def finish_tokens(act, gates, token_out, down, *refs, parts_count, heads):
    parts, back = refs[:parts_count], refs[parts_count]
    count, wide = act.shape
    size = wide // heads
    logs = []
    for part in parts:
        packed = part[:, wide:].astype(F32)
        logs.append(
            packed + pltpu.roll(packed, LANES - heads, 1) + pltpu.roll(packed, LANES - 2 * heads, 1)
        )
    top = functools.reduce(jnp.maximum, logs)
    weights = [jnp.exp(log - top) for log in logs]
    total = functools.reduce(jnp.add, weights)
    head = lax.broadcasted_iota(jnp.int32, (LANES, wide), 0)
    feature = lax.broadcasted_iota(jnp.int32, (LANES, wide), 1)
    expand = jnp.where((feature >= head * size) & (feature < (head + 1) * size), 1.0, 0.0).astype(BF)
    mixed = jnp.zeros((count, wide), F32)
    for part, weight in zip(parts, weights):
        factor = weight / total
        coarse = factor.astype(BF)
        fine = (factor - coarse.astype(F32)).astype(BF)
        mixed = mixed + (dot(coarse, expand) + dot(fine, expand)) * part[:, :wide].astype(F32)
    gated = (mixed * gates[...]).astype(BF)
    result = (act[...].astype(F32) + dot(gated, token_out[...])).astype(BF)
    back[...] = dot(result, down[...]).astype(BF)


def second_inner(
    info, offsets, ids, atoms1, own_back, near_back, gain, qkv, bias,
    atoms2, mixed, edge_q, edge_k, edge_v, q, k, v, *, share
):
    tokens = 2 * own_back.shape[0]
    table = jnp.concatenate([own_back[...], near_back[...]], axis=0)
    table_ids = (token_of(tokens, share, info[0], 1) + info[1] * tokens).astype(F32)
    step = 256
    for at in range(0, atoms1.shape[0], step):
        members = []
        for first in range(at, at + step, LANES):
            atom_ids = jnp.broadcast_to(ids[:, first : first + LANES].astype(F32), (LANES, LANES)).T
            members.append(
                jnp.concatenate(
                    [one_hot(table_ids[:, t : t + LANES], atom_ids) for t in range(0, tokens, LANES)], axis=1
                )
            )
        member = jnp.concatenate(members, axis=0)
        atoms2[at : at + step, :] = (atoms1[at : at + step, :].astype(F32) + dot(member, table)).astype(BF)
    for at in range(0, atoms1.shape[0], step):
        project(atoms2[at : at + step, :], gain[...], qkv[...], q, k, v, at)
    inner_windows(starts_from(offsets, info[4]), bias, q, k, v, mixed, edge_q, edge_k, edge_v)


def second_edge(
    info, offsets, atoms2, near, far, own_back, near_back, far_back, gain, qkv, out_weight, bias,
    mixed, edge_q, edge_k, edge_v, result, k, v, edge_mixed, ends, *, share, columns
):
    side, column = info[0], info[3]
    ends[:, :RIM, :] = bias[:, :RIM, :]
    ends[:, RIM:, :] = bias[:, bias.shape[1] - RIM :, :]
    tokens = 2 * own_back.shape[0]
    table = jnp.concatenate([own_back[...], near_back[...]], axis=0)
    table_ids = token_of(tokens, share, side)
    first_token = (info[1] * tokens).astype(F32)

    def rim_ids(message):
        packed = message[RIM:, :].astype(F32)
        return (packed[0:1, :RIM] * 64.0 + packed[0:1, RIM:] - first_token).astype(jnp.int32)

    near_rows = near[:RIM, :].astype(F32) + dot_tn(one_hot(table_ids, rim_ids(near)), table)
    far_token = rim_ids(far)
    beyond = lax.broadcasted_iota(jnp.int32, (RIM, 1), 0) + jnp.where(
        column == 0, -RIM, jnp.where(column == columns - 1, tokens, 4 * tokens)
    )
    far_rows = (
        far[:RIM, :].astype(F32)
        + dot_tn(one_hot(table_ids, far_token), table)
        + dot_tn(one_hot(beyond, far_token), far_back[...])
    )
    edges = edge_windows(
        starts_from(offsets, info[4] - RIM), ends, gain[...], qkv[...], near_rows.astype(BF).astype(F32), far_rows.astype(BF).astype(F32), side,
        edge_q, edge_k, edge_v, k, v, edge_mixed,
    )
    parts = 4
    for part in range(parts):
        next(edges)
        close_inner(atoms2, mixed, out_weight, result, part, parts)
    for _ in edges:
        pass
    close_edge(atoms2, edge_mixed, out_weight, result)


def stay(x):
    return pltpu.with_memory_space_constraint(x, pltpu.HBM)


def call(kernel, outs, scratch, specs, flops, limit=20):
    return pl.pallas_call(
        kernel,
        out_shape=outs,
        in_specs=specs,
        out_specs=jax.tree.map(lambda _: VMEM, outs),
        scratch_shapes=scratch,
        compiler_params=pltpu.CompilerParams(vmem_limit_bytes=limit * 1024 * 1024),
        cost_estimate=pl.CostEstimate(flops=flops, bytes_accessed=1_000, transcendentals=1_000),
    )


def body(
    atom_acts, first_gain, first_qkv, first_out, second_gain, second_qkv, second_out, atom_bias, window_start,
    atom_token, up_weight, token_gain, token_weight, token_out, down_weight, pair_bias,
):
    rows, channels = atom_acts.shape
    heads, tok_rows, slots = pair_bias.shape
    wide = token_weight.shape[0]
    row_count, col_count = lax.axis_size("row"), lax.axis_size("col")
    pairs = col_count // 2
    share = tok_rows // col_count
    half = tok_rows // 2
    row, col = lax.axis_index("row"), lax.axis_index("col")
    side, pair = col % 2, col // 2
    info = jnp.stack([side, row, pair, col, (row * col_count + col) * rows]).astype(jnp.int32)
    devices = row_count * col_count
    group_count = lax.axis_size("group")

    def to_near(x):
        return lax.ppermute(x, "col", [(i, i ^ 1) for i in range(col_count)])

    def swapped(x, swap):
        pairs_list = []
        for i in range(group_count * devices):
            group_at, at = divmod(i, devices)
            if at in swap:
                target = group_at * devices + swap[at]
            else:
                target = (group_at ^ 1) * devices + at if group_count % 2 == 0 else i
            pairs_list.append((i, target))
        return lax.ppermute(x, ("group", "row", "col"), pairs_list)

    def to_far(x):
        return swapped(x, {i: i + 1 if i % 2 else i - 1 for i in range(1, devices - 1)})

    def to_beyond(x):
        swap = {}
        for i in range(1, row_count):
            first, last = i * col_count, i * col_count - 1
            for one, other in ((first, first - col_count + 1), (last, last + col_count - 1)):
                swap[one], swap[other] = other, one
        if col_count > 4:
            for i in range(devices):
                if 2 <= i % col_count < col_count - 2:
                    swap[i] = i ^ 1
        return swapped(x, swap)

    def along_pairs(x, step):
        return lax.ppermute(
            x, "col", [(2 * i + k, 2 * ((i + step) % pairs) + k) for i in range(pairs) for k in range(2)]
        )

    def along_rows(x, step):
        return lax.ppermute(x, "row", [(i, i ^ step) for i in range(row_count)])

    def rim_of(x, last):
        return lax.dynamic_slice_in_dim(x, jnp.where(last, rows - RIM, 0), RIM, axis=0)

    near_acts = to_near(rim_of(atom_acts, side == 0))
    far_acts = to_far(rim_of(atom_acts, side == 1))

    ids = atom_token.reshape(1, rows)
    inner_scratch = [
        pltpu.VMEM((rows, channels), BF),
        pltpu.VMEM((rows, channels), F32),
        pltpu.VMEM((rows, channels), F32),
    ]
    edge_scratch = [
        pltpu.VMEM((6 * RIM, channels), F32),
        pltpu.VMEM((6 * RIM, channels), F32),
        pltpu.VMEM((2 * RIM, channels), BF),
    ]
    atom_shape = jax.ShapeDtypeStruct((rows, channels), BF)
    edge_shapes = [
        jax.ShapeDtypeStruct((2 * RIM, channels), BF),
        jax.ShapeDtypeStruct((4 * RIM, channels), F32),
        jax.ShapeDtypeStruct((4 * RIM, channels), F32),
    ]
    packed_shape = jax.ShapeDtypeStruct((half, wide + LANES), BF)
    first_gain, second_gain = first_gain.reshape(1, -1), second_gain.reshape(1, -1)
    pieces = 2
    windows = window_start.shape[0]
    edge = RIM * windows // rows
    groups = (windows - 2 * edge) // window_group(windows, edge)
    first_args = [atom_acts, first_gain, first_qkv]
    mixed1 = call(
        functools.partial(first_inner, pieces=pieces),
        [atom_shape] + edge_shapes + [jax.ShapeDtypeStruct((atom_bias.shape[0], 2 * RIM, atom_bias.shape[2]), BF)],
        inner_scratch
        + [pltpu.VMEM(x.shape, x.dtype) for x in first_args]
        + [pltpu.SMEM(window_start.shape, jnp.int32), pltpu.VMEM(atom_bias.shape, BF)]
        + [pltpu.SemaphoreType.DMA((5 + pieces,)), pltpu.SemaphoreType.DMA((groups,))],
        [SMEM] + [HBM] * 5,
        1_500_000_000,
        16,
    )(info, *map(stay, first_args), stay(window_start), stay(atom_bias))
    message_shape = jax.ShapeDtypeStruct((RIM + 16, channels), BF)
    atoms1, send, keep, near_message, far_message = call(
        functools.partial(first_edge, share=share),
        [atom_shape, packed_shape, packed_shape, message_shape, message_shape],
        edge_scratch,
        [SMEM, SMEM] + [VMEM] * 13,
        2_000_000_000,
        16,
    )(
        info, window_start, ids, atom_acts, near_acts, far_acts, first_gain, first_qkv, first_out,
        up_weight, *mixed1,
    )

    chip_sum = (keep.astype(F32) + to_near(send).astype(F32)).astype(BF)
    chip_sum, near_bias, near_message, far_message = lax.optimization_barrier(
        (chip_sum, pair_bias, near_message, far_message)
    )
    bias_near = to_near(near_bias)
    sums = [lax.dynamic_slice_in_dim(chip_sum, pair * share, share, axis=0)]
    for step in range(1, pairs):
        piece = lax.dynamic_slice_in_dim(chip_sum, (pair + step) % pairs * share, share, axis=0)
        sums.append(along_pairs(piece, step))
    near_message, far_message = to_near(near_message), to_far(far_message)
    sums, bias_near, near_message, far_message = lax.optimization_barrier(
        (sums, bias_near, near_message, far_message)
    )
    share_shape = jax.ShapeDtypeStruct((share, wide), BF)
    gain_row = token_gain.reshape(1, -1)
    act, normed = call(
        functools.partial(mean_tokens, count=len(sums)), [share_shape] * 2, [], [VMEM] * (len(sums) + 1), 1_000_000
    )(*sums, gain_row)

    group = LANES // share
    solo = group == 2
    split = 1 if solo else group
    own_keys = [normed] + [along_rows(normed, step) for step in range(1, row_count)]
    near_keys = [to_near(x) for x in own_keys[:split]]
    other_acts = [along_pairs(act, step) for step in range(1, pairs)]
    half_shape = jax.ShapeDtypeStruct((half, wide), BF)
    wide_shape = jax.ShapeDtypeStruct((half, wide), F32)
    rest = row_count - split

    def key_scratch(count):
        return [pltpu.VMEM((2 * count * share, wide), BF)] * 3

    head_shape = jax.ShapeDtypeStruct((heads, half, LANES), F32)
    weight_shape = jax.ShapeDtypeStruct((wide, wide), BF)
    tile_count = 2 * pairs
    blocks = row_count // group - 1
    act_rows, queries, gates, *held, mixed, tops, totals = call(
        functools.partial(attend_first, others=len(other_acts), steps=list(range(split)), solo=solo),
        [half_shape, half_shape, wide_shape, weight_shape, weight_shape]
        + [jax.ShapeDtypeStruct((heads, half, LANES), BF), jax.ShapeDtypeStruct((heads, half, 2 * LANES * blocks), BF)]
        + [wide_shape, head_shape, head_shape],
        [pltpu.VMEM((wide, wide), BF)] * 2
        + key_scratch(split)
        + [pltpu.VMEM((heads, half, 2 * split * share), BF), pltpu.VMEM((2, heads, half, LANES), BF)]
        + [pltpu.SemaphoreType.DMA((4 + tile_count * (blocks + 1),))],
        [SMEM, HBM, VMEM, VMEM, HBM, HBM] + [VMEM] * (len(other_acts) + 2 * split),
        1_000,
        24,
    )(
        info, stay(token_weight), gain_row, act, stay(pair_bias), stay(bias_near), *other_acts,
        *own_keys[:split], *near_keys,
    )
    rest_steps = sorted(range(split, row_count), key=lambda step: (step < group, step))
    rest_keys, mixed = lax.optimization_barrier(([own_keys[step] for step in rest_steps], mixed))
    rest_near = [to_near(x) for x in rest_keys]
    part = call(
        functools.partial(attend_rest, steps=rest_steps, solo=solo),
        packed_shape,
        key_scratch(rest),
        [SMEM] + [VMEM] * (8 + 2 * rest),
        2_000_000_000,
    )(info, queries, *held, mixed, tops, totals, *rest_keys, *rest_near)

    parts = [part] + [along_pairs(part, step) for step in range(1, pairs)]
    own_back = call(
        functools.partial(finish_tokens, parts_count=pairs, heads=heads),
        jax.ShapeDtypeStruct((half, channels), BF),
        [],
        [VMEM] * (4 + pairs),
        200_000_000,
    )(act_rows, gates, token_out, down_weight, *parts)

    near_back = to_near(own_back)
    if share >= RIM:
        last_rows = own_back[half - RIM :]
        first_rows = own_back[:RIM]
    else:
        both = jnp.where(side == 0, jnp.stack([own_back, near_back]), jnp.stack([near_back, own_back]))
        both = both.reshape(2, pairs, share, channels).transpose(1, 0, 2, 3).reshape(tok_rows, channels)
        last_rows = both[tok_rows - RIM :]
        first_rows = both[:RIM]
    far_back = to_beyond(jnp.where(side == 1, last_rows, first_rows))

    atoms2, *mixed2 = call(
        functools.partial(second_inner, share=share),
        [atom_shape, atom_shape] + edge_shapes,
        inner_scratch,
        [SMEM, SMEM] + [VMEM] * 7,
        1_500_000_000,
        16,
    )(info, window_start, ids, atoms1, own_back, near_back, second_gain, second_qkv, atom_bias)
    return call(
        functools.partial(second_edge, share=share, columns=col_count),
        atom_shape,
        edge_scratch + [pltpu.VMEM((atom_bias.shape[0], 2 * RIM, atom_bias.shape[2]), BF)],
        [SMEM, SMEM] + [VMEM] * 14,
        300_000_000,
        16,
    )(
        info, window_start, atoms2, near_message, far_message, own_back, near_back, far_back,
        second_gain, second_qkv, second_out, atom_bias, *mixed2,
    )


def solution(mesh):
    atoms = P(("group", "row", "col"))
    in_specs = (
        P(("group", "row", "col"), None),
        P(), P(), P(), P(), P(), P(),
        P(None, ("group", "row", "col"), None),
        atoms,
        atoms,
        P(), P(), P(), P(), P(),
        P(None, ("group", "row"), "col"),
    )
    out_specs = P(("group", "row", "col"), None)
    return jax.shard_map(body, mesh=mesh, in_specs=in_specs, out_specs=out_specs, check_vma=False)
```

```python
import functools
import math

import jax
import jax.numpy as jnp
from jax import lax
from jax.experimental import pallas as pl
from jax.experimental.pallas import tpu as pltpu
from jax.sharding import PartitionSpec as P

BF = jnp.bfloat16
F32 = jnp.float32
RIM = 64
LANES = 128
VMEM = pl.BlockSpec(memory_space=pltpu.VMEM)
SMEM = pl.BlockSpec(memory_space=pltpu.SMEM)
HBM = pl.BlockSpec(memory_space=pltpu.HBM)


def dot(a, b):
    return jnp.dot(a, b, preferred_element_type=F32)


def dot_nt(a, b):
    return lax.dot_general(a, b, (((1,), (1,)), ((), ())), preferred_element_type=F32)


def dot_tn(a, b):
    return lax.dot_general(a, b, (((0,), (0,)), ((), ())), preferred_element_type=F32)


def norm_rows(values, gain):
    center = values - jnp.mean(values, axis=-1, keepdims=True)
    spread = jnp.mean(center * center, axis=-1, keepdims=True)
    return center * lax.rsqrt(spread + 1e-05) * gain


def token_of(count, share, first_parity, dim=0):
    half = count // 2
    row = lax.broadcasted_iota(jnp.int32, (count, 1) if dim == 0 else (1, count), dim)
    second = (row >= half).astype(jnp.int32)
    inner = row - second * half
    shift = share.bit_length() - 1
    share_pair = inner >> shift
    inside = inner & (share - 1)
    parity = first_parity + second - 2 * first_parity * second
    return (2 * share_pair + parity) * share + inside


def one_hot(table_ids, atom_ids):
    return jnp.where(table_ids == atom_ids, 1.0, 0.0).astype(BF)


def project(rows, gain, qkv, q, k, v, at):
    channels = rows.shape[1]
    packed = dot(norm_rows(rows.astype(F32), gain).astype(BF), qkv).astype(BF)
    place = slice(at, at + rows.shape[0])
    q[place, :] = packed[:, :channels]
    k[place, :] = packed[:, channels : 2 * channels].astype(F32)
    v[place, :] = packed[:, 2 * channels :].astype(F32)


def attend_windows(places, bias, q, k, v, mixed):
    heads, _, span = bias.shape
    channels = q.shape[1]
    block = span - 3 * RIM // 2
    size = channels // heads
    scale = 1.0 / math.sqrt(size)
    stacked = heads * block
    head_row = lax.broadcasted_iota(jnp.int32, (heads, block, channels), 0).reshape(stacked, channels)
    head_lane = lax.broadcasted_iota(jnp.int32, (stacked, channels), 1) // size
    own_head = jnp.where(head_row == head_lane, 1.0, 0.0).astype(BF)
    lane_head = lax.broadcasted_iota(jnp.int32, (block, channels), 1) // size
    ones = jnp.ones((span, channels), BF)

    def picked(stack):
        out = stack[:block]
        for head in range(1, heads):
            out = jnp.where(lane_head == head, stack[head * block : (head + 1) * block], out)
        return out

    yield
    scores = []
    for query_at, _, key_at in places:
        spread = jnp.concatenate([q[pl.ds(query_at, block), :]] * heads, axis=0) * own_head
        scores.append(dot_nt(spread, k[pl.ds(key_at, span), :].astype(BF)))
    yield
    raised = []
    for (_, bias_at, _), score in zip(places, scores):
        tile = bias[:, pl.ds(bias_at, block), :].reshape(stacked, span).astype(F32)
        score = score * scale + tile
        raised.append(jnp.exp(score - jnp.max(score, axis=-1, keepdims=True)).astype(BF))
    yield
    for (query_at, _, key_at), weights in zip(places, raised):
        values = jnp.concatenate([v[pl.ds(key_at, span), :].astype(BF), ones], axis=1)
        out = dot(weights, values)
        mixed[pl.ds(query_at, block), :] = (picked(out[:, :channels]) / picked(out[:, channels:])).astype(BF)


class starts_from:
    def __init__(self, starts, base):
        self.starts, self.base, self.shape = starts, base, starts.shape

    def __getitem__(self, window):
        return self.starts[window] - self.base


def window_group(windows, edge):
    return next(size for size in (15, 12, 10, 6, 5, 4, 3, 2, 1) if (windows - 2 * edge) % size == 0)


def inner_windows(offsets, bias, q, k, v, mixed, edge_q, edge_k, edge_v, ready=None):
    windows = offsets.shape[0]
    rows = q.shape[0]
    block = rows // windows
    edge = RIM // block
    group = window_group(windows, edge)

    def one_group(step, carry):
        if ready is not None:
            ready(step)
        places = []
        for member in range(group):
            window = edge + step * group + member
            at = pl.multiple_of(window * block, block)
            places.append((at, at, offsets[window]))
        for _ in attend_windows(places, bias, q, k, v, mixed):
            pass
        return carry

    lax.fori_loop(0, (windows - 2 * edge) // group, one_group, 0)
    edge_q[:RIM, :] = q[:RIM, :]
    edge_q[RIM:, :] = q[rows - RIM :, :]
    for source, target in ((k, edge_k), (v, edge_v)):
        target[: 2 * RIM, :] = source[: 2 * RIM, :]
        target[2 * RIM :, :] = source[rows - 2 * RIM :, :]


def edge_windows(offsets, bias, gain, qkv, near, far, side, edge_q, edge_k, edge_v, k, v, mixed):
    windows = offsets.shape[0]
    channels = edge_q.shape[1]
    block = bias.shape[2] - 3 * RIM // 2
    rows = windows * block
    edge = RIM // block
    for source, target in ((edge_k, k), (edge_v, v)):
        target[RIM : 3 * RIM, :] = source[: 2 * RIM, :]
        target[3 * RIM : 5 * RIM, :] = source[2 * RIM :, :]
    normed = norm_rows(jnp.concatenate([near, far], axis=0), gain).astype(BF)
    yield
    packed = dot(normed, qkv[:, channels:]).astype(BF).astype(F32)
    near_at = pl.multiple_of(jnp.where(side == 0, 5 * RIM, 0), RIM)
    far_at = pl.multiple_of(5 * RIM - near_at, RIM)
    for at, part in ((near_at, packed[:RIM]), (far_at, packed[RIM:])):
        k[pl.ds(at, RIM), :] = part[:, :channels]
        v[pl.ds(at, RIM), :] = part[:, channels:]
    places = []
    for member in range(edge):
        places.append((member * block, member * block, offsets[member]))
    for member in range(edge):
        window = windows - edge + member
        at = RIM + member * block
        places.append((at, at, offsets[window] - (rows - 4 * RIM)))
    yield from attend_windows(places, bias, edge_q, k, v, mixed)


def fetches(sources, targets, sems, first=0):
    return [
        pltpu.make_async_copy(source, target, sems.at[first + index])
        for index, (source, target) in enumerate(zip(sources, targets))
    ]


def first_inner(
    info, acts_far, gain_far, qkv_far, starts_far, bias_far, mixed, edge_q, edge_k, edge_v, edge_bias,
    q, k, v, acts, gain, qkv, starts, bias, sems, bias_sems, *, pieces
):
    rows = acts.shape[0]
    windows = starts.shape[0]
    block = rows // windows
    span = window_group(windows, RIM // block) * block
    part = rows // pieces
    cuts = [pl.ds(index * part, part) for index in range(pieces)]
    small = fetches([gain_far, qkv_far, starts_far], [gain, qkv, starts], sems)
    moving = fetches([acts_far.at[cut, :] for cut in cuts], [acts.at[cut, :] for cut in cuts], sems, 3)
    ends = fetches(
        [bias_far.at[:, pl.ds(at, RIM), :] for at in (0, rows - RIM)],
        [edge_bias.at[:, pl.ds(at, RIM), :] for at in (0, RIM)],
        sems,
        3 + pieces,
    )

    def tile(step):
        place = pl.ds(pl.multiple_of(RIM + step * span, block), span)
        return pltpu.make_async_copy(bias_far.at[:, place, :], bias.at[:, place, :], bias_sems.at[step])

    for copy in moving[:1] + small + moving[1:]:
        copy.start()
    for copy in small:
        copy.wait()
    step = 256
    for index, copy in enumerate(moving):
        copy.wait()
        if index == 0:
            for group in range(bias_sems.shape[0]):
                tile(group).start()
            for end in ends:
                end.start()
        for at in range(index * part, (index + 1) * part, step):
            project(acts[at : at + step, :], gain[...], qkv[...], q, k, v, at)
    inner_windows(
        starts_from(starts, info[4]), bias, q, k, v, mixed, edge_q, edge_k, edge_v, lambda index: tile(index).wait()
    )
    for end in ends:
        end.wait()


def first_edge(
    info, offsets, ids, acts, near, far, gain, qkv, out_weight, up, mixed, edge_q, edge_k, edge_v, bias,
    atoms, send, keep, near_message, far_message, k, v, edge_mixed, *, share
):
    side = info[0]
    rows = acts.shape[0]
    edges = edge_windows(
        starts_from(offsets, info[4] - RIM), bias, gain[...], qkv[...], near[...].astype(F32), far[...].astype(F32), side,
        edge_q, edge_k, edge_v, k, v, edge_mixed,
    )
    step = 256
    tokens = 2 * send.shape[0]
    half = tokens // 2
    wide = up.shape[1]
    next(edges)
    close_inner(acts, mixed, out_weight, atoms)
    member = one_hot(token_of(tokens, share, 1 - side) + info[1] * tokens, ids[...])
    next(edges)
    inner = slice(step, rows - step)
    inner_atoms = atoms[inner, :]
    partial_sums = []
    for at in range(0, wide, step):
        feat = jnp.maximum(dot(inner_atoms, up[:, at : at + step]), 0.0).astype(BF)
        partial_sums.append(dot(member[:, inner], feat))
        next(edges, None)
    for _ in edges:
        pass
    close_edge(acts, edge_mixed, out_weight, atoms)
    head_ids = ids[:, :RIM]
    tail_ids = ids[:, rows - RIM :]
    for message, last in ((near_message, 1 - side), (far_message, side)):
        at = pl.multiple_of(last * (rows - RIM), RIM)
        message[:RIM, :] = atoms[pl.ds(at, RIM), :]
        sent = head_ids + last * (tail_ids - head_ids)
        coded = jnp.concatenate([sent >> 6, sent & 63], axis=1).astype(F32)
        message[RIM:, :] = jnp.broadcast_to(coded, (16, 2 * RIM)).astype(BF)
    outer_atoms = jnp.concatenate([atoms[:step, :], atoms[rows - step :, :]], axis=0)
    outer_member = jnp.concatenate([member[:, :step], member[:, rows - step :]], axis=1)
    for at, partial_sum in zip(range(0, wide, step), partial_sums):
        feat = jnp.maximum(dot(outer_atoms, up[:, at : at + step]), 0.0).astype(BF)
        sums = (partial_sum + dot(outer_member, feat)).astype(BF)
        send[:, at : at + step] = sums[:half]
        keep[:, at : at + step] = sums[half:]
    count = dot(member, jnp.ones((rows, LANES), BF))
    high = jnp.floor(count * (1.0 / 64.0))
    low = count - 64.0 * high
    lane = lax.broadcasted_iota(jnp.int32, (tokens, LANES), 1)
    pieces = jnp.where(lane == 0, high, jnp.where(lane == 1, low, 0.0)).astype(BF)
    send[:, wide:] = pieces[:half]
    keep[:, wide:] = pieces[half:]


def close_inner(acts, mixed, out_weight, out, part=0, parts=1):
    rows = acts.shape[0]
    step = 256
    for at in range(rows // parts * part, rows // parts * (part + 1), step):
        first, last = max(at, RIM), min(at + step, rows - RIM)
        moved = acts[first:last, :].astype(F32) + dot(mixed[first:last, :], out_weight[...])
        out[first:last, :] = moved.astype(BF)


def close_edge(acts, mixed, out_weight, out):
    rows = acts.shape[0]
    moved = dot(mixed[...], out_weight[...])
    out[:RIM, :] = (acts[:RIM, :].astype(F32) + moved[:RIM]).astype(BF)
    out[rows - RIM :, :] = (acts[rows - RIM :, :].astype(F32) + moved[RIM:]).astype(BF)


def mean_tokens(*refs, count):
    parts, gain, act, normed = refs[:count], refs[count], refs[count + 1], refs[count + 2]
    total = parts[0][...].astype(F32)
    for part in parts[1:]:
        total = total + part[...].astype(F32)
    wide = act.shape[1]
    atoms = total[:, wide : wide + 1] * 64.0 + total[:, wide + 1 : wide + 2]
    rounded = (total[:, :wide] / atoms).astype(BF)
    act[...] = rounded
    normed[...] = norm_rows(rounded.astype(F32), gain[...]).astype(BF)


def place_keys(info, own, near, tokens, steps, solo):
    share = own[0].shape[0]
    group = LANES // share
    place = info[1] & (group - 1)
    lead = 2 * share if solo else 0
    for own_rows, near_rows, step in zip(own, near, steps):
        if solo and step < group:
            places = (0, share)
        else:
            at = lead + (step // group - (0 not in steps)) * 2 * LANES + (place ^ (step % group)) * share
            places = (at, at + LANES)
        for rows, at in zip((own_rows, near_rows), places):
            tokens[pl.ds(pl.multiple_of(at, share), share), :] = rows[...]


def bias_pieces(info, biases_far, block, targets, share):
    count = targets[0].shape[1]
    group = LANES // share
    side, row = info[0], info[1]
    slot = pl.multiple_of(((row // group) ^ block) * LANES, LANES)
    sources, places = [], []
    for bias_far, target in zip(biases_far, targets):
        for pair in range(count // share):
            at = pl.multiple_of((2 * pair + side) * share, share)
            sources.append(bias_far.at[:, pl.ds(at, share), pl.ds(slot, LANES)])
            places.append(target.at[:, pl.ds(pair * share, share), :])
    return sources, places


def split_bias(info, slots, bias, rest):
    heads, count = bias.shape[0], bias.shape[1]
    lane = lax.broadcasted_iota(jnp.int32, (count, LANES), 1)
    lower = lane < LANES // 2
    first = info[1] & 1
    for head in range(heads):
        own, near = slots[0, head].astype(F32), slots[1, head].astype(F32)
        low = jnp.where(lower, own, pltpu.roll(near, LANES // 2, 1))
        high = jnp.where(lower, pltpu.roll(own, LANES // 2, 1), near)
        bias[head] = jnp.where(first == 0, low, high).astype(BF)
        rest[head, :, :LANES] = jnp.where(first == 0, high, low).astype(BF)


def attend_heads(queries, biases, keys, values, previous, keep):
    count, wide = queries.shape
    heads = biases[0].shape[0]
    size = wide // heads
    scale = 1.0 / math.sqrt(size)
    span = keys.shape[0] // LANES
    lane = lax.broadcasted_iota(jnp.int32, (count, LANES), 1)
    out = [None] * (wide // LANES)
    together = 4
    for start in range(0, heads, together):
        members = []
        for head in range(start, start + together):
            first, last = head * size, (head + 1) * size
            low, high = first // LANES, -(-last // LANES)
            chunk = slice(low * LANES, high * LANES)
            chunk_lane = lax.broadcasted_iota(jnp.int32, (count, (high - low) * LANES), 1) + low * LANES
            inside = (chunk_lane >= first) & (chunk_lane < last)
            query = jnp.where(inside, queries[:, chunk].astype(F32), 0.0).astype(BF)
            members.append((head, first, low, high, dot_nt(query, keys[:, chunk])))
        raised = []
        for head, first, low, high, score in members:
            tile = jnp.concatenate([bias[head] for bias in biases], axis=1)
            score = score * scale + tile.astype(F32)
            top = jnp.broadcast_to(jnp.max(score, axis=-1, keepdims=True), (count, LANES))
            if previous is not None:
                former = previous[1][head]
                top = jnp.maximum(top, former)
            weights = jnp.exp(score - jnp.concatenate([top] * span, axis=1))
            total = jnp.broadcast_to(jnp.sum(weights, axis=-1, keepdims=True), (count, LANES))
            fade = None
            if previous is not None:
                fade = jnp.exp(former - top)
                total = total + fade * previous[2][head]
            keep(head, top, total)
            raised.append((weights.astype(BF), fade, total))
        for (head, first, low, high, _), (weights, fade, total) in zip(members, raised):
            mixed = dot(weights, values[:, low * LANES : high * LANES])
            if previous is not None:
                inverse = 1.0 / total
            for block in range(low, high):
                piece = mixed[:, (block - low) * LANES : (block - low + 1) * LANES]
                if previous is not None:
                    piece = (piece + fade * previous[0][:, block * LANES : (block + 1) * LANES]) * inverse
                if out[block] is not None:
                    piece = jnp.where(lane + block * LANES >= first, piece, out[block])
                out[block] = piece
    return out


def attend_first(info, weight_far, gain, own_act, own_far, near_far, *refs, others, steps, solo):
    rows_count = len(steps)
    other_acts, refs = refs[:others], refs[others:]
    own, near, refs = refs[:rows_count], refs[rows_count : 2 * rows_count], refs[2 * rows_count :]
    act, queries, gates, key_weight, value_weight, pair_bias, rest_bias, mixed, tops, totals = refs[:10]
    query_weight, gate_weight, tokens, keys, values, bias, slots, sems = refs[10:]
    share, wide = own[0].shape
    weights = fetches(
        [weight_far.at[:, pl.ds(part * wide, wide)] for part in range(4)],
        [query_weight, key_weight, value_weight, gate_weight],
        sems,
    )
    targets = (slots.at[0], slots.at[1]) if solo else [bias.at[:, :, pl.ds(at, LANES)] for at in (0, LANES)]
    tiles = fetches(*bias_pieces(info, (own_far, near_far), 0, targets, share), sems, 4)
    later = []
    for block in range(rest_bias.shape[2] // (2 * LANES)):
        targets = [rest_bias.at[:, :, pl.ds((2 * block + half) * LANES, LANES)] for half in range(2)]
        sources, places = bias_pieces(info, (own_far, near_far), block + 1, targets, share)
        later += fetches(sources, places, sems, 4 + len(tiles) + len(later))
    for copy in weights[:3] + tiles + weights[3:] + later:
        copy.start()
    pairs = others + 1
    place = info[2]
    act[pl.ds(pl.multiple_of(place * share, share), share), :] = own_act[...]
    for step in range(1, pairs):
        at = lax.rem(place - step + pairs, pairs) * share
        act[pl.ds(pl.multiple_of(at, share), share), :] = other_acts[step - 1][...]
    normed = norm_rows(act[...].astype(F32), gain[...]).astype(BF)
    place_keys(info, own, near, tokens, steps, solo)
    weights[0].wait()
    queries[...] = dot(normed, query_weight[...]).astype(BF)
    weights[1].wait()
    keys[...] = dot(tokens[...], key_weight[...]).astype(BF)
    weights[2].wait()
    values[...] = dot(tokens[...], value_weight[...]).astype(BF)
    for copy in tiles:
        copy.wait()
    if solo:
        split_bias(info, slots, bias, pair_bias)
    else:
        pair_bias[...] = jnp.zeros(pair_bias.shape, BF)

    def keep(head, top, total):
        tops[head] = top
        totals[head] = total

    out = attend_heads(queries, [bias], keys, values, None, keep)
    for block, piece in enumerate(out):
        mixed[:, block * LANES : (block + 1) * LANES] = piece
    weights[3].wait()
    gates[...] = jax.nn.sigmoid(dot(normed, gate_weight[...]).astype(BF).astype(F32))
    for copy in later:
        copy.wait()


def attend_rest(
    info, queries, key_weight, value_weight, pair_bias, rest_bias, former, former_top, former_total, *refs,
    steps, solo, part, parts
):
    if part == 0:
        rows_count = len(steps)
        own, near = refs[:rows_count], refs[rows_count : 2 * rows_count]
        packed, tokens, keys, values = refs[2 * rows_count :]
        place_keys(info, own, near, tokens, steps, solo)
    else:
        tokens, packed, keys, values = refs
    heads = rest_bias.shape[0] // parts
    count = queries.shape[0]
    wide = keys.shape[1]
    some_heads = pl.ds(part * heads, heads)
    some = pl.ds(part * wide, wide)
    keys[...] = dot(tokens[...], key_weight[:, some]).astype(BF)
    values[...] = dot(tokens[...], value_weight[:, some]).astype(BF)
    lane = lax.broadcasted_iota(jnp.int32, (count, LANES), 1)
    ends = [jnp.zeros((count, LANES), F32), jnp.ones((count, LANES), F32)]

    def keep(head, top, total):
        ends[0] = jnp.where(lane == head, top, ends[0])
        ends[1] = jnp.where(lane == head, total, ends[1])

    biases = [ref.at[some_heads] for ref in ((pair_bias, rest_bias) if solo else (rest_bias,))]
    previous = (former.at[:, some], former_top.at[some_heads], former_total.at[some_heads])
    out = attend_heads(queries.at[:, some], biases, keys, values, previous, keep)
    for block, piece in enumerate(out):
        packed[:, block * LANES : (block + 1) * LANES] = piece.astype(BF)
    logs = ends[0] + jnp.log(ends[1])
    first = logs.astype(BF).astype(F32)
    rest = logs - first
    second = rest.astype(BF).astype(F32)
    rest = rest - second
    packed[:, wide:] = (first + pltpu.roll(second, heads, 1) + pltpu.roll(rest, 2 * heads, 1)).astype(BF)


def finish_part(so_far, gates, token_out, *refs, heads, size, part):
    parts, refs = refs[:-2], refs[-2:]
    count = so_far.shape[0]
    some = heads * size
    head = lax.broadcasted_iota(jnp.int32, (LANES, some), 0)
    feature = lax.broadcasted_iota(jnp.int32, (LANES, some), 1)
    expand = jnp.where((feature >= head * size) & (feature < (head + 1) * size), 1.0, 0.0).astype(BF)
    logs = []
    for piece in parts:
        packed = piece[:, some:].astype(F32)
        logs.append(packed + pltpu.roll(packed, LANES - heads, 1) + pltpu.roll(packed, LANES - 2 * heads, 1))
    top = functools.reduce(jnp.maximum, logs)
    weights = [jnp.exp(log - top) for log in logs]
    total = functools.reduce(jnp.add, weights)
    mixed = jnp.zeros((count, some), F32)
    for piece, weight in zip(parts, weights):
        factor = weight / total
        coarse = factor.astype(BF)
        fine = (factor - coarse.astype(F32)).astype(BF)
        mixed = mixed + (dot(coarse, expand) + dot(fine, expand)) * piece[:, :some].astype(F32)
    place = slice(part * some, (part + 1) * some)
    gated = (mixed * gates[:, place]).astype(BF)
    result = so_far[...].astype(F32) + dot(gated, token_out[place, :])
    down, out = refs
    if part == 0:
        out[...] = result
    else:
        out[...] = dot(result.astype(BF), down[...]).astype(BF)


def second_inner(
    info, offsets, ids, atoms1, own_back, near_back, gain, qkv, bias,
    atoms2, mixed, edge_q, edge_k, edge_v, q, k, v, *, share
):
    tokens = 2 * own_back.shape[0]
    table = jnp.concatenate([own_back[...], near_back[...]], axis=0)
    table_ids = (token_of(tokens, share, info[0], 1) + info[1] * tokens).astype(F32)
    step = 256
    for at in range(0, atoms1.shape[0], step):
        members = []
        for first in range(at, at + step, LANES):
            atom_ids = jnp.broadcast_to(ids[:, first : first + LANES].astype(F32), (LANES, LANES)).T
            members.append(
                jnp.concatenate(
                    [one_hot(table_ids[:, t : t + LANES], atom_ids) for t in range(0, tokens, LANES)], axis=1
                )
            )
        member = jnp.concatenate(members, axis=0)
        atoms2[at : at + step, :] = (atoms1[at : at + step, :].astype(F32) + dot(member, table)).astype(BF)
    for at in range(0, atoms1.shape[0], step):
        project(atoms2[at : at + step, :], gain[...], qkv[...], q, k, v, at)
    inner_windows(starts_from(offsets, info[4]), bias, q, k, v, mixed, edge_q, edge_k, edge_v)


def second_edge(
    info, offsets, atoms2, near, far, own_back, near_back, far_back, gain, qkv, out_weight, bias,
    mixed, edge_q, edge_k, edge_v, result, k, v, edge_mixed, ends, *, share, columns
):
    side, column = info[0], info[3]
    ends[:, :RIM, :] = bias[:, :RIM, :]
    ends[:, RIM:, :] = bias[:, bias.shape[1] - RIM :, :]
    tokens = 2 * own_back.shape[0]
    table = jnp.concatenate([own_back[...], near_back[...]], axis=0)
    table_ids = token_of(tokens, share, side)
    first_token = (info[1] * tokens).astype(F32)

    def rim_ids(message):
        packed = message[RIM:, :].astype(F32)
        return (packed[0:1, :RIM] * 64.0 + packed[0:1, RIM:] - first_token).astype(jnp.int32)

    near_rows = near[:RIM, :].astype(F32) + dot_tn(one_hot(table_ids, rim_ids(near)), table)
    far_token = rim_ids(far)
    beyond = lax.broadcasted_iota(jnp.int32, (RIM, 1), 0) + jnp.where(
        column == 0, -RIM, jnp.where(column == columns - 1, tokens, 4 * tokens)
    )
    far_rows = (
        far[:RIM, :].astype(F32)
        + dot_tn(one_hot(table_ids, far_token), table)
        + dot_tn(one_hot(beyond, far_token), far_back[...])
    )
    edges = edge_windows(
        starts_from(offsets, info[4] - RIM), ends, gain[...], qkv[...], near_rows.astype(BF).astype(F32), far_rows.astype(BF).astype(F32), side,
        edge_q, edge_k, edge_v, k, v, edge_mixed,
    )
    parts = 4
    for part in range(parts):
        next(edges)
        close_inner(atoms2, mixed, out_weight, result, part, parts)
    for _ in edges:
        pass
    close_edge(atoms2, edge_mixed, out_weight, result)


def stay(x):
    return pltpu.with_memory_space_constraint(x, pltpu.HBM)


def call(kernel, outs, scratch, specs, flops, limit=20):
    return pl.pallas_call(
        kernel,
        out_shape=outs,
        in_specs=specs,
        out_specs=jax.tree.map(lambda _: VMEM, outs),
        scratch_shapes=scratch,
        compiler_params=pltpu.CompilerParams(vmem_limit_bytes=limit * 1024 * 1024),
        cost_estimate=pl.CostEstimate(flops=flops, bytes_accessed=1_000, transcendentals=1_000),
    )


def body(
    atom_acts, first_gain, first_qkv, first_out, second_gain, second_qkv, second_out, atom_bias, window_start,
    atom_token, up_weight, token_gain, token_weight, token_out, down_weight, pair_bias,
):
    rows, channels = atom_acts.shape
    heads, tok_rows, slots = pair_bias.shape
    wide = token_weight.shape[0]
    row_count, col_count = lax.axis_size("row"), lax.axis_size("col")
    pairs = col_count // 2
    share = tok_rows // col_count
    half = tok_rows // 2
    row, col = lax.axis_index("row"), lax.axis_index("col")
    side, pair = col % 2, col // 2
    info = jnp.stack([side, row, pair, col, (row * col_count + col) * rows]).astype(jnp.int32)
    devices = row_count * col_count
    group_count = lax.axis_size("group")

    def to_near(x):
        return lax.ppermute(x, "col", [(i, i ^ 1) for i in range(col_count)])

    def swapped(x, swap):
        pairs_list = []
        for i in range(group_count * devices):
            group_at, at = divmod(i, devices)
            if at in swap:
                target = group_at * devices + swap[at]
            else:
                target = (group_at ^ 1) * devices + at if group_count % 2 == 0 else i
            pairs_list.append((i, target))
        return lax.ppermute(x, ("group", "row", "col"), pairs_list)

    def to_far(x):
        return swapped(x, {i: i + 1 if i % 2 else i - 1 for i in range(1, devices - 1)})

    def to_beyond(x):
        swap = {}
        for i in range(1, row_count):
            first, last = i * col_count, i * col_count - 1
            for one, other in ((first, first - col_count + 1), (last, last + col_count - 1)):
                swap[one], swap[other] = other, one
        if col_count > 4:
            for i in range(devices):
                if 2 <= i % col_count < col_count - 2:
                    swap[i] = i ^ 1
        return swapped(x, swap)

    def along_pairs(x, step):
        return lax.ppermute(
            x, "col", [(2 * i + k, 2 * ((i + step) % pairs) + k) for i in range(pairs) for k in range(2)]
        )

    def along_rows(x, step):
        return lax.ppermute(x, "row", [(i, i ^ step) for i in range(row_count)])

    def rim_of(x, last):
        return lax.dynamic_slice_in_dim(x, jnp.where(last, rows - RIM, 0), RIM, axis=0)

    near_acts = to_near(rim_of(atom_acts, side == 0))
    far_acts = to_far(rim_of(atom_acts, side == 1))

    ids = atom_token.reshape(1, rows)
    inner_scratch = [
        pltpu.VMEM((rows, channels), BF),
        pltpu.VMEM((rows, channels), F32),
        pltpu.VMEM((rows, channels), F32),
    ]
    edge_scratch = [
        pltpu.VMEM((6 * RIM, channels), F32),
        pltpu.VMEM((6 * RIM, channels), F32),
        pltpu.VMEM((2 * RIM, channels), BF),
    ]
    atom_shape = jax.ShapeDtypeStruct((rows, channels), BF)
    edge_shapes = [
        jax.ShapeDtypeStruct((2 * RIM, channels), BF),
        jax.ShapeDtypeStruct((4 * RIM, channels), F32),
        jax.ShapeDtypeStruct((4 * RIM, channels), F32),
    ]
    packed_shape = jax.ShapeDtypeStruct((half, wide + LANES), BF)
    first_gain, second_gain = first_gain.reshape(1, -1), second_gain.reshape(1, -1)
    pieces = 2
    windows = window_start.shape[0]
    edge = RIM * windows // rows
    groups = (windows - 2 * edge) // window_group(windows, edge)
    first_args = [atom_acts, first_gain, first_qkv]
    mixed1 = call(
        functools.partial(first_inner, pieces=pieces),
        [atom_shape] + edge_shapes + [jax.ShapeDtypeStruct((atom_bias.shape[0], 2 * RIM, atom_bias.shape[2]), BF)],
        inner_scratch
        + [pltpu.VMEM(x.shape, x.dtype) for x in first_args]
        + [pltpu.SMEM(window_start.shape, jnp.int32), pltpu.VMEM(atom_bias.shape, BF)]
        + [pltpu.SemaphoreType.DMA((5 + pieces,)), pltpu.SemaphoreType.DMA((groups,))],
        [SMEM] + [HBM] * 5,
        1_500_000_000,
        16,
    )(info, *map(stay, first_args), stay(window_start), stay(atom_bias))
    message_shape = jax.ShapeDtypeStruct((RIM + 16, channels), BF)
    atoms1, send, keep, near_message, far_message = call(
        functools.partial(first_edge, share=share),
        [atom_shape, packed_shape, packed_shape, message_shape, message_shape],
        edge_scratch,
        [SMEM, SMEM] + [VMEM] * 13,
        2_000_000_000,
        16,
    )(
        info, window_start, ids, atom_acts, near_acts, far_acts, first_gain, first_qkv, first_out,
        up_weight, *mixed1,
    )

    chip_sum = (keep.astype(F32) + to_near(send).astype(F32)).astype(BF)
    chip_sum, near_bias, near_message, far_message = lax.optimization_barrier(
        (chip_sum, pair_bias, near_message, far_message)
    )
    bias_near = to_near(near_bias)
    sums = [lax.dynamic_slice_in_dim(chip_sum, pair * share, share, axis=0)]
    for step in range(1, pairs):
        piece = lax.dynamic_slice_in_dim(chip_sum, (pair + step) % pairs * share, share, axis=0)
        sums.append(along_pairs(piece, step))
    near_message, far_message = to_near(near_message), to_far(far_message)
    sums, bias_near, near_message, far_message = lax.optimization_barrier(
        (sums, bias_near, near_message, far_message)
    )
    share_shape = jax.ShapeDtypeStruct((share, wide), BF)
    gain_row = token_gain.reshape(1, -1)
    act, normed = call(
        functools.partial(mean_tokens, count=len(sums)), [share_shape] * 2, [], [VMEM] * (len(sums) + 1), 1_000_000
    )(*sums, gain_row)

    group = LANES // share
    solo = group == 2
    split = 1 if solo else group
    own_keys = [normed] + [along_rows(normed, step) for step in range(1, row_count)]
    near_keys = [to_near(x) for x in own_keys[:split]]
    other_acts = [along_pairs(act, step) for step in range(1, pairs)]
    half_shape = jax.ShapeDtypeStruct((half, wide), BF)
    wide_shape = jax.ShapeDtypeStruct((half, wide), F32)
    rest = row_count - split

    def key_scratch(count):
        return [pltpu.VMEM((2 * count * share, wide), BF)] * 3

    head_shape = jax.ShapeDtypeStruct((heads, half, LANES), F32)
    weight_shape = jax.ShapeDtypeStruct((wide, wide), BF)
    tile_count = 2 * pairs
    blocks = row_count // group - 1
    act_rows, queries, gates, *held, mixed, tops, totals = call(
        functools.partial(attend_first, others=len(other_acts), steps=list(range(split)), solo=solo),
        [half_shape, half_shape, wide_shape, weight_shape, weight_shape]
        + [jax.ShapeDtypeStruct((heads, half, LANES), BF), jax.ShapeDtypeStruct((heads, half, 2 * LANES * blocks), BF)]
        + [wide_shape, head_shape, head_shape],
        [pltpu.VMEM((wide, wide), BF)] * 2
        + key_scratch(split)
        + [pltpu.VMEM((heads, half, 2 * split * share), BF), pltpu.VMEM((2, heads, half, LANES), BF)]
        + [pltpu.SemaphoreType.DMA((4 + tile_count * (blocks + 1),))],
        [SMEM, HBM, VMEM, VMEM, HBM, HBM] + [VMEM] * (len(other_acts) + 2 * split),
        1_000,
        24,
    )(
        info, stay(token_weight), gain_row, act, stay(pair_bias), stay(bias_near), *other_acts,
        *own_keys[:split], *near_keys,
    )
    rest_steps = sorted(range(split, row_count), key=lambda step: (step < group, step))
    rest_keys, mixed = lax.optimization_barrier(([own_keys[step] for step in rest_steps], mixed))
    rest_near = [to_near(x) for x in rest_keys]
    halves = 2
    some = wide // halves
    key_rows = jax.ShapeDtypeStruct((2 * rest * share, wide), BF)
    rest_scratch = [pltpu.VMEM((2 * rest * share, some), BF)] * 2
    part_shape = jax.ShapeDtypeStruct((half, some + LANES), BF)
    rest_args = [info, queries, *held, mixed, tops, totals]
    early_part, key_rows = call(
        functools.partial(attend_rest, steps=rest_steps, solo=solo, part=0, parts=halves),
        [part_shape, key_rows],
        rest_scratch,
        [SMEM] + [VMEM] * (8 + 2 * rest),
        2_000_000_000,
    )(*rest_args, *rest_keys, *rest_near)
    late_part = call(
        functools.partial(attend_rest, steps=rest_steps, solo=solo, part=1, parts=halves),
        part_shape,
        rest_scratch,
        [SMEM] + [VMEM] * 9,
        2_000_000_000,
    )(*rest_args, key_rows)
    early_parts = [along_pairs(early_part, step) for step in range(1, pairs)]
    late_parts = [along_pairs(late_part, step) for step in range(1, pairs)]
    def finish(so_far, part, pieces, out):
        return call(
            functools.partial(finish_part, heads=heads // halves, size=wide // heads, part=part),
            out,
            [],
            [VMEM] * (4 + pairs),
            200_000_000,
        )(so_far, gates, token_out, *pieces, down_weight)

    result = finish(act_rows, 0, [early_part] + early_parts, wide_shape)
    own_back = finish(result, 1, [late_part] + late_parts, jax.ShapeDtypeStruct((half, channels), BF))

    near_back = to_near(own_back)
    if share >= RIM:
        last_rows = own_back[half - RIM :]
        first_rows = own_back[:RIM]
    else:
        both = jnp.where(side == 0, jnp.stack([own_back, near_back]), jnp.stack([near_back, own_back]))
        both = both.reshape(2, pairs, share, channels).transpose(1, 0, 2, 3).reshape(tok_rows, channels)
        last_rows = both[tok_rows - RIM :]
        first_rows = both[:RIM]
    far_back = to_beyond(jnp.where(side == 1, last_rows, first_rows))

    atoms2, *mixed2 = call(
        functools.partial(second_inner, share=share),
        [atom_shape, atom_shape] + edge_shapes,
        inner_scratch,
        [SMEM, SMEM] + [VMEM] * 7,
        1_500_000_000,
        16,
    )(info, window_start, ids, atoms1, own_back, near_back, second_gain, second_qkv, atom_bias)
    return call(
        functools.partial(second_edge, share=share, columns=col_count),
        atom_shape,
        edge_scratch + [pltpu.VMEM((atom_bias.shape[0], 2 * RIM, atom_bias.shape[2]), BF)],
        [SMEM, SMEM] + [VMEM] * 14,
        300_000_000,
        16,
    )(
        info, window_start, atoms2, near_message, far_message, own_back, near_back, far_back,
        second_gain, second_qkv, second_out, atom_bias, *mixed2,
    )


def solution(mesh):
    atoms = P(("group", "row", "col"))
    in_specs = (
        P(("group", "row", "col"), None),
        P(), P(), P(), P(), P(), P(),
        P(None, ("group", "row", "col"), None),
        atoms,
        atoms,
        P(), P(), P(), P(), P(),
        P(None, ("group", "row"), "col"),
    )
    out_specs = P(("group", "row", "col"), None)
    return jax.shard_map(body, mesh=mesh, in_specs=in_specs, out_specs=out_specs, check_vma=False)
```

```python
import functools
import math

import jax
import jax.numpy as jnp
from jax import lax
from jax.experimental import pallas as pl
from jax.experimental.pallas import tpu as pltpu
from jax.sharding import PartitionSpec as P

BF = jnp.bfloat16
F32 = jnp.float32
RIM = 64
LANES = 128
VMEM = pl.BlockSpec(memory_space=pltpu.VMEM)
SMEM = pl.BlockSpec(memory_space=pltpu.SMEM)
HBM = pl.BlockSpec(memory_space=pltpu.HBM)


def dot(a, b):
    return jnp.dot(a, b, preferred_element_type=F32)


def dot_nt(a, b):
    return lax.dot_general(a, b, (((1,), (1,)), ((), ())), preferred_element_type=F32)


def dot_tn(a, b):
    return lax.dot_general(a, b, (((0,), (0,)), ((), ())), preferred_element_type=F32)


def norm_rows(values, gain):
    center = values - jnp.mean(values, axis=-1, keepdims=True)
    spread = jnp.mean(center * center, axis=-1, keepdims=True)
    return center * lax.rsqrt(spread + 1e-05) * gain


def token_of(count, share, first_parity, dim=0):
    half = count // 2
    row = lax.broadcasted_iota(jnp.int32, (count, 1) if dim == 0 else (1, count), dim)
    second = (row >= half).astype(jnp.int32)
    inner = row - second * half
    shift = share.bit_length() - 1
    share_pair = inner >> shift
    inside = inner & (share - 1)
    parity = first_parity + second - 2 * first_parity * second
    return (2 * share_pair + parity) * share + inside


def one_hot(table_ids, atom_ids):
    return jnp.where(table_ids == atom_ids, 1.0, 0.0).astype(BF)


def project(rows, gain, qkv, q, k, v, at):
    channels = rows.shape[1]
    packed = dot(norm_rows(rows.astype(F32), gain).astype(BF), qkv).astype(BF)
    place = slice(at, at + rows.shape[0])
    q[place, :] = packed[:, :channels]
    k[place, :] = packed[:, channels : 2 * channels].astype(F32)
    v[place, :] = packed[:, 2 * channels :].astype(F32)


def attend_windows(places, bias, q, k, v, mixed):
    heads, _, span = bias.shape
    channels = q.shape[1]
    block = span - 3 * RIM // 2
    size = channels // heads
    scale = 1.0 / math.sqrt(size)
    stacked = heads * block
    head_row = lax.broadcasted_iota(jnp.int32, (heads, block, channels), 0).reshape(stacked, channels)
    head_lane = lax.broadcasted_iota(jnp.int32, (stacked, channels), 1) // size
    own_head = jnp.where(head_row == head_lane, 1.0, 0.0).astype(BF)
    lane_head = lax.broadcasted_iota(jnp.int32, (block, channels), 1) // size
    ones = jnp.ones((span, channels), BF)

    def picked(stack):
        out = stack[:block]
        for head in range(1, heads):
            out = jnp.where(lane_head == head, stack[head * block : (head + 1) * block], out)
        return out

    yield
    scores = []
    for query_at, _, key_at in places:
        spread = jnp.concatenate([q[pl.ds(query_at, block), :]] * heads, axis=0) * own_head
        scores.append(dot_nt(spread, k[pl.ds(key_at, span), :].astype(BF)))
    yield
    raised = []
    for (_, bias_at, _), score in zip(places, scores):
        tile = bias[:, pl.ds(bias_at, block), :].reshape(stacked, span).astype(F32)
        score = score * scale + tile
        raised.append(jnp.exp(score - jnp.max(score, axis=-1, keepdims=True)).astype(BF))
    yield
    for (query_at, _, key_at), weights in zip(places, raised):
        values = jnp.concatenate([v[pl.ds(key_at, span), :].astype(BF), ones], axis=1)
        out = dot(weights, values)
        mixed[pl.ds(query_at, block), :] = (picked(out[:, :channels]) / picked(out[:, channels:])).astype(BF)


class starts_from:
    def __init__(self, starts, base):
        self.starts, self.base, self.shape = starts, base, starts.shape

    def __getitem__(self, window):
        return self.starts[window] - self.base


def window_group(windows, edge):
    return next(size for size in (30, 20, 15, 12, 10, 6, 5, 4, 3, 2, 1) if (windows - 2 * edge) % size == 0)


def inner_windows(offsets, bias, q, k, v, mixed, edge_q, edge_k, edge_v, ready=None):
    windows = offsets.shape[0]
    rows = q.shape[0]
    block = rows // windows
    edge = RIM // block
    group = window_group(windows, edge)

    def one_group(step, carry):
        if ready is not None:
            ready(step)
        places = []
        for member in range(group):
            window = edge + step * group + member
            at = pl.multiple_of(window * block, block)
            places.append((at, at, offsets[window]))
        for _ in attend_windows(places, bias, q, k, v, mixed):
            pass
        return carry

    lax.fori_loop(0, (windows - 2 * edge) // group, one_group, 0)
    edge_q[:RIM, :] = q[:RIM, :]
    edge_q[RIM:, :] = q[rows - RIM :, :]
    for source, target in ((k, edge_k), (v, edge_v)):
        target[: 2 * RIM, :] = source[: 2 * RIM, :]
        target[2 * RIM :, :] = source[rows - 2 * RIM :, :]


def edge_windows(offsets, bias, gain, qkv, near, far, side, edge_q, edge_k, edge_v, k, v, mixed):
    windows = offsets.shape[0]
    channels = edge_q.shape[1]
    block = bias.shape[2] - 3 * RIM // 2
    rows = windows * block
    edge = RIM // block
    for source, target in ((edge_k, k), (edge_v, v)):
        target[RIM : 3 * RIM, :] = source[: 2 * RIM, :]
        target[3 * RIM : 5 * RIM, :] = source[2 * RIM :, :]
    normed = norm_rows(jnp.concatenate([near, far], axis=0), gain).astype(BF)
    yield
    packed = dot(normed, qkv[:, channels:]).astype(BF).astype(F32)
    near_at = pl.multiple_of(jnp.where(side == 0, 5 * RIM, 0), RIM)
    far_at = pl.multiple_of(5 * RIM - near_at, RIM)
    for at, part in ((near_at, packed[:RIM]), (far_at, packed[RIM:])):
        k[pl.ds(at, RIM), :] = part[:, :channels]
        v[pl.ds(at, RIM), :] = part[:, channels:]
    places = []
    for member in range(edge):
        places.append((member * block, member * block, offsets[member]))
    for member in range(edge):
        window = windows - edge + member
        at = RIM + member * block
        places.append((at, at, offsets[window] - (rows - 4 * RIM)))
    yield from attend_windows(places, bias, edge_q, k, v, mixed)


def fetches(sources, targets, sems, first=0):
    return [
        pltpu.make_async_copy(source, target, sems.at[first + index])
        for index, (source, target) in enumerate(zip(sources, targets))
    ]


def first_inner(
    info, acts_far, gain_far, qkv_far, starts_far, bias_far, mixed, edge_q, edge_k, edge_v, edge_bias,
    q, k, v, acts, gain, qkv, starts, bias, sems, bias_sems, *, pieces
):
    rows = acts.shape[0]
    windows = starts.shape[0]
    block = rows // windows
    span = window_group(windows, RIM // block) * block
    part = rows // pieces
    cuts = [pl.ds(index * part, part) for index in range(pieces)]
    small = fetches([gain_far, qkv_far, starts_far], [gain, qkv, starts], sems)
    moving = fetches([acts_far.at[cut, :] for cut in cuts], [acts.at[cut, :] for cut in cuts], sems, 3)
    ends = fetches(
        [bias_far.at[:, pl.ds(at, RIM), :] for at in (0, rows - RIM)],
        [edge_bias.at[:, pl.ds(at, RIM), :] for at in (0, RIM)],
        sems,
        3 + pieces,
    )

    def tile(step):
        place = pl.ds(pl.multiple_of(RIM + step * span, block), span)
        return pltpu.make_async_copy(bias_far.at[:, place, :], bias.at[:, place, :], bias_sems.at[step])

    for copy in moving[:1] + small + moving[1:]:
        copy.start()
    for copy in small:
        copy.wait()
    step = 256
    for index, copy in enumerate(moving):
        copy.wait()
        if index == 0:
            for group in range(bias_sems.shape[0]):
                tile(group).start()
            for end in ends:
                end.start()
        for at in range(index * part, (index + 1) * part, step):
            project(acts[at : at + step, :], gain[...], qkv[...], q, k, v, at)
    inner_windows(
        starts_from(starts, info[4]), bias, q, k, v, mixed, edge_q, edge_k, edge_v, lambda index: tile(index).wait()
    )
    for end in ends:
        end.wait()


def first_edge(
    info, offsets, ids, acts, near, far, gain, qkv, out_weight, up, mixed, edge_q, edge_k, edge_v, bias,
    atoms, send, keep, near_message, far_message, k, v, edge_mixed, *, share
):
    side = info[0]
    rows = acts.shape[0]
    edges = edge_windows(
        starts_from(offsets, info[4] - RIM), bias, gain[...], qkv[...], near[...].astype(F32), far[...].astype(F32), side,
        edge_q, edge_k, edge_v, k, v, edge_mixed,
    )
    step = 256
    tokens = 2 * send.shape[0]
    half = tokens // 2
    wide = up.shape[1]
    next(edges)
    close_inner(acts, mixed, out_weight, atoms)
    member = one_hot(token_of(tokens, share, 1 - side) + info[1] * tokens, ids[...])
    next(edges)
    inner = slice(step, rows - step)
    inner_atoms = atoms[inner, :]
    partial_sums = []
    for at in range(0, wide, step):
        feat = jnp.maximum(dot(inner_atoms, up[:, at : at + step]), 0.0).astype(BF)
        partial_sums.append(dot(member[:, inner], feat))
        next(edges, None)
    for _ in edges:
        pass
    close_edge(acts, edge_mixed, out_weight, atoms)
    head_ids = ids[:, :RIM]
    tail_ids = ids[:, rows - RIM :]
    for message, last in ((near_message, 1 - side), (far_message, side)):
        at = pl.multiple_of(last * (rows - RIM), RIM)
        message[:RIM, :] = atoms[pl.ds(at, RIM), :]
        sent = head_ids + last * (tail_ids - head_ids)
        coded = jnp.concatenate([sent >> 6, sent & 63], axis=1).astype(F32)
        message[RIM:, :] = jnp.broadcast_to(coded, (16, 2 * RIM)).astype(BF)
    outer_atoms = jnp.concatenate([atoms[:step, :], atoms[rows - step :, :]], axis=0)
    outer_member = jnp.concatenate([member[:, :step], member[:, rows - step :]], axis=1)
    for at, partial_sum in zip(range(0, wide, step), partial_sums):
        feat = jnp.maximum(dot(outer_atoms, up[:, at : at + step]), 0.0).astype(BF)
        sums = (partial_sum + dot(outer_member, feat)).astype(BF)
        send[:, at : at + step] = sums[:half]
        keep[:, at : at + step] = sums[half:]
    count = dot(member, jnp.ones((rows, LANES), BF))
    high = jnp.floor(count * (1.0 / 64.0))
    low = count - 64.0 * high
    lane = lax.broadcasted_iota(jnp.int32, (tokens, LANES), 1)
    pieces = jnp.where(lane == 0, high, jnp.where(lane == 1, low, 0.0)).astype(BF)
    send[:, wide:] = pieces[:half]
    keep[:, wide:] = pieces[half:]


def close_inner(acts, mixed, out_weight, out, part=0, parts=1):
    rows = acts.shape[0]
    step = 256
    for at in range(rows // parts * part, rows // parts * (part + 1), step):
        first, last = max(at, RIM), min(at + step, rows - RIM)
        moved = acts[first:last, :].astype(F32) + dot(mixed[first:last, :], out_weight[...])
        out[first:last, :] = moved.astype(BF)


def close_edge(acts, mixed, out_weight, out):
    rows = acts.shape[0]
    moved = dot(mixed[...], out_weight[...])
    out[:RIM, :] = (acts[:RIM, :].astype(F32) + moved[:RIM]).astype(BF)
    out[rows - RIM :, :] = (acts[rows - RIM :, :].astype(F32) + moved[RIM:]).astype(BF)


def mean_tokens(*refs, count):
    parts, gain, act, normed = refs[:count], refs[count], refs[count + 1], refs[count + 2]
    total = parts[0][...].astype(F32)
    for part in parts[1:]:
        total = total + part[...].astype(F32)
    wide = act.shape[1]
    atoms = total[:, wide : wide + 1] * 64.0 + total[:, wide + 1 : wide + 2]
    rounded = (total[:, :wide] / atoms).astype(BF)
    act[...] = rounded
    normed[...] = norm_rows(rounded.astype(F32), gain[...]).astype(BF)


def place_keys(info, own, near, tokens, steps, solo):
    share = own[0].shape[0]
    group = LANES // share
    place = info[1] & (group - 1)
    lead = 2 * share if solo else 0
    for own_rows, near_rows, step in zip(own, near, steps):
        if solo and step < group:
            places = (0, share)
        else:
            at = lead + (step // group - (0 not in steps)) * 2 * LANES + (place ^ (step % group)) * share
            places = (at, at + LANES)
        for rows, at in zip((own_rows, near_rows), places):
            tokens[pl.ds(pl.multiple_of(at, share), share), :] = rows[...]


def bias_pieces(info, biases_far, block, targets, share):
    count = targets[0].shape[1]
    group = LANES // share
    side, row = info[0], info[1]
    slot = pl.multiple_of(((row // group) ^ block) * LANES, LANES)
    sources, places = [], []
    for bias_far, target in zip(biases_far, targets):
        for pair in range(count // share):
            at = pl.multiple_of((2 * pair + side) * share, share)
            sources.append(bias_far.at[:, pl.ds(at, share), pl.ds(slot, LANES)])
            places.append(target.at[:, pl.ds(pair * share, share), :])
    return sources, places


def split_bias(info, slots, bias, rest):
    heads, count = bias.shape[0], bias.shape[1]
    lane = lax.broadcasted_iota(jnp.int32, (count, LANES), 1)
    lower = lane < LANES // 2
    first = info[1] & 1
    for head in range(heads):
        own, near = slots[0, head].astype(F32), slots[1, head].astype(F32)
        low = jnp.where(lower, own, pltpu.roll(near, LANES // 2, 1))
        high = jnp.where(lower, pltpu.roll(own, LANES // 2, 1), near)
        bias[head] = jnp.where(first == 0, low, high).astype(BF)
        rest[head, :, :LANES] = jnp.where(first == 0, high, low).astype(BF)


def attend_heads(queries, biases, keys, values, previous, keep):
    count, wide = queries.shape
    heads = biases[0].shape[0]
    size = wide // heads
    scale = 1.0 / math.sqrt(size)
    span = keys.shape[0] // LANES
    lane = lax.broadcasted_iota(jnp.int32, (count, LANES), 1)
    out = [None] * (wide // LANES)
    together = 8
    for start in range(0, heads, together):
        members = []
        for head in range(start, start + together):
            first, last = head * size, (head + 1) * size
            low, high = first // LANES, -(-last // LANES)
            chunk = slice(low * LANES, high * LANES)
            chunk_lane = lax.broadcasted_iota(jnp.int32, (count, (high - low) * LANES), 1) + low * LANES
            inside = (chunk_lane >= first) & (chunk_lane < last)
            query = jnp.where(inside, queries[:, chunk].astype(F32), 0.0).astype(BF)
            members.append((head, first, low, high, dot_nt(query, keys[:, chunk])))
        raised = []
        for head, first, low, high, score in members:
            tile = jnp.concatenate([bias[head] for bias in biases], axis=1)
            score = score * scale + tile.astype(F32)
            top = jnp.broadcast_to(jnp.max(score, axis=-1, keepdims=True), (count, LANES))
            if previous is not None:
                former = previous[1][head]
                top = jnp.maximum(top, former)
            weights = jnp.exp(score - jnp.concatenate([top] * span, axis=1))
            total = jnp.broadcast_to(jnp.sum(weights, axis=-1, keepdims=True), (count, LANES))
            fade = None
            if previous is not None:
                fade = jnp.exp(former - top)
                total = total + fade * previous[2][head]
            keep(head, top, total)
            raised.append((weights.astype(BF), fade, total))
        for (head, first, low, high, _), (weights, fade, total) in zip(members, raised):
            mixed = dot(weights, values[:, low * LANES : high * LANES])
            if previous is not None:
                inverse = 1.0 / total
            for block in range(low, high):
                piece = mixed[:, (block - low) * LANES : (block - low + 1) * LANES]
                if previous is not None:
                    piece = (piece + fade * previous[0][:, block * LANES : (block + 1) * LANES]) * inverse
                if out[block] is not None:
                    piece = jnp.where(lane + block * LANES >= first, piece, out[block])
                out[block] = piece
    return out


def attend_first(info, weight_far, gain, own_act, own_far, near_far, *refs, others, steps, solo):
    rows_count = len(steps)
    other_acts, refs = refs[:others], refs[others:]
    own, near, refs = refs[:rows_count], refs[rows_count : 2 * rows_count], refs[2 * rows_count :]
    act, queries, gates, key_weight, value_weight, pair_bias, rest_bias, mixed, tops, totals = refs[:10]
    query_weight, gate_weight, tokens, keys, values, bias, slots, sems = refs[10:]
    share, wide = own[0].shape
    weights = fetches(
        [weight_far.at[:, pl.ds(part * wide, wide)] for part in range(4)],
        [query_weight, key_weight, value_weight, gate_weight],
        sems,
    )
    targets = (slots.at[0], slots.at[1]) if solo else [bias.at[:, :, pl.ds(at, LANES)] for at in (0, LANES)]
    tiles = fetches(*bias_pieces(info, (own_far, near_far), 0, targets, share), sems, 4)
    later = []
    for block in range(rest_bias.shape[2] // (2 * LANES)):
        targets = [rest_bias.at[:, :, pl.ds((2 * block + half) * LANES, LANES)] for half in range(2)]
        sources, places = bias_pieces(info, (own_far, near_far), block + 1, targets, share)
        later += fetches(sources, places, sems, 4 + len(tiles) + len(later))
    for copy in weights[:3] + tiles + weights[3:] + later:
        copy.start()
    pairs = others + 1
    place = info[2]
    act[pl.ds(pl.multiple_of(place * share, share), share), :] = own_act[...]
    for step in range(1, pairs):
        at = lax.rem(place - step + pairs, pairs) * share
        act[pl.ds(pl.multiple_of(at, share), share), :] = other_acts[step - 1][...]
    normed = norm_rows(act[...].astype(F32), gain[...]).astype(BF)
    place_keys(info, own, near, tokens, steps, solo)
    weights[0].wait()
    queries[...] = dot(normed, query_weight[...]).astype(BF)
    weights[1].wait()
    keys[...] = dot(tokens[...], key_weight[...]).astype(BF)
    weights[2].wait()
    values[...] = dot(tokens[...], value_weight[...]).astype(BF)
    for copy in tiles:
        copy.wait()
    if solo:
        split_bias(info, slots, bias, pair_bias)
    else:
        pair_bias[...] = jnp.zeros(pair_bias.shape, BF)

    def keep(head, top, total):
        tops[head] = top
        totals[head] = total

    out = attend_heads(queries, [bias], keys, values, None, keep)
    for block, piece in enumerate(out):
        mixed[:, block * LANES : (block + 1) * LANES] = piece
    weights[3].wait()
    gates[...] = jax.nn.sigmoid(dot(normed, gate_weight[...]).astype(BF).astype(F32))
    for copy in later:
        copy.wait()


def attend_rest(
    info, queries, key_weight, value_weight, pair_bias, rest_bias, former, former_top, former_total, *refs,
    steps, solo, part, parts
):
    if part == 0:
        rows_count = len(steps)
        own, near = refs[:rows_count], refs[rows_count : 2 * rows_count]
        packed, tokens, keys, values = refs[2 * rows_count :]
        place_keys(info, own, near, tokens, steps, solo)
    else:
        tokens, packed, keys, values = refs
    heads = rest_bias.shape[0] // parts
    count = queries.shape[0]
    wide = keys.shape[1]
    some_heads = pl.ds(part * heads, heads)
    some = pl.ds(part * wide, wide)
    keys[...] = dot(tokens[...], key_weight[:, some]).astype(BF)
    values[...] = dot(tokens[...], value_weight[:, some]).astype(BF)
    lane = lax.broadcasted_iota(jnp.int32, (count, LANES), 1)
    ends = [jnp.zeros((count, LANES), F32), jnp.ones((count, LANES), F32)]

    def keep(head, top, total):
        ends[0] = jnp.where(lane == head, top, ends[0])
        ends[1] = jnp.where(lane == head, total, ends[1])

    biases = [ref.at[some_heads] for ref in ((pair_bias, rest_bias) if solo else (rest_bias,))]
    previous = (former.at[:, some], former_top.at[some_heads], former_total.at[some_heads])
    out = attend_heads(queries.at[:, some], biases, keys, values, previous, keep)
    for block, piece in enumerate(out):
        packed[:, block * LANES : (block + 1) * LANES] = piece.astype(BF)
    logs = ends[0] + jnp.log(ends[1])
    first = logs.astype(BF).astype(F32)
    rest = logs - first
    second = rest.astype(BF).astype(F32)
    rest = rest - second
    packed[:, wide:] = (first + pltpu.roll(second, heads, 1) + pltpu.roll(rest, 2 * heads, 1)).astype(BF)


def finish_part(so_far, gates, token_out, *refs, heads, size, part):
    parts, refs = refs[:-2], refs[-2:]
    count = so_far.shape[0]
    some = heads * size
    head = lax.broadcasted_iota(jnp.int32, (LANES, some), 0)
    feature = lax.broadcasted_iota(jnp.int32, (LANES, some), 1)
    expand = jnp.where((feature >= head * size) & (feature < (head + 1) * size), 1.0, 0.0).astype(BF)
    logs = []
    for piece in parts:
        packed = piece[:, some:].astype(F32)
        logs.append(packed + pltpu.roll(packed, LANES - heads, 1) + pltpu.roll(packed, LANES - 2 * heads, 1))
    top = functools.reduce(jnp.maximum, logs)
    weights = [jnp.exp(log - top) for log in logs]
    total = functools.reduce(jnp.add, weights)
    mixed = jnp.zeros((count, some), F32)
    for piece, weight in zip(parts, weights):
        factor = weight / total
        coarse = factor.astype(BF)
        fine = (factor - coarse.astype(F32)).astype(BF)
        mixed = mixed + (dot(coarse, expand) + dot(fine, expand)) * piece[:, :some].astype(F32)
    place = slice(part * some, (part + 1) * some)
    gated = (mixed * gates[:, place]).astype(BF)
    result = so_far[...].astype(F32) + dot(gated, token_out[place, :])
    down, out = refs
    if part == 0:
        out[...] = result
    else:
        out[...] = dot(result.astype(BF), down[...]).astype(BF)


def second_inner(
    info, offsets, ids, atoms1, own_back, near_back, gain, qkv, bias,
    atoms2, mixed, edge_q, edge_k, edge_v, q, k, v, *, share
):
    tokens = 2 * own_back.shape[0]
    table = jnp.concatenate([own_back[...], near_back[...]], axis=0)
    table_ids = (token_of(tokens, share, info[0], 1) + info[1] * tokens).astype(F32)
    step = 256
    for at in range(0, atoms1.shape[0], step):
        members = []
        for first in range(at, at + step, LANES):
            atom_ids = jnp.broadcast_to(ids[:, first : first + LANES].astype(F32), (LANES, LANES)).T
            members.append(
                jnp.concatenate(
                    [one_hot(table_ids[:, t : t + LANES], atom_ids) for t in range(0, tokens, LANES)], axis=1
                )
            )
        member = jnp.concatenate(members, axis=0)
        atoms2[at : at + step, :] = (atoms1[at : at + step, :].astype(F32) + dot(member, table)).astype(BF)
    for at in range(0, atoms1.shape[0], step):
        project(atoms2[at : at + step, :], gain[...], qkv[...], q, k, v, at)
    inner_windows(starts_from(offsets, info[4]), bias, q, k, v, mixed, edge_q, edge_k, edge_v)


def second_edge(
    info, offsets, atoms2, near, far, own_back, near_back, far_back, gain, qkv, out_weight, bias,
    mixed, edge_q, edge_k, edge_v, result, k, v, edge_mixed, ends, *, share, columns
):
    side, column = info[0], info[3]
    ends[:, :RIM, :] = bias[:, :RIM, :]
    ends[:, RIM:, :] = bias[:, bias.shape[1] - RIM :, :]
    tokens = 2 * own_back.shape[0]
    table = jnp.concatenate([own_back[...], near_back[...]], axis=0)
    table_ids = token_of(tokens, share, side)
    first_token = (info[1] * tokens).astype(F32)

    def rim_ids(message):
        packed = message[RIM:, :].astype(F32)
        return (packed[0:1, :RIM] * 64.0 + packed[0:1, RIM:] - first_token).astype(jnp.int32)

    near_rows = near[:RIM, :].astype(F32) + dot_tn(one_hot(table_ids, rim_ids(near)), table)
    far_token = rim_ids(far)
    beyond = lax.broadcasted_iota(jnp.int32, (RIM, 1), 0) + jnp.where(
        column == 0, -RIM, jnp.where(column == columns - 1, tokens, 4 * tokens)
    )
    far_rows = (
        far[:RIM, :].astype(F32)
        + dot_tn(one_hot(table_ids, far_token), table)
        + dot_tn(one_hot(beyond, far_token), far_back[...])
    )
    edges = edge_windows(
        starts_from(offsets, info[4] - RIM), ends, gain[...], qkv[...], near_rows.astype(BF).astype(F32), far_rows.astype(BF).astype(F32), side,
        edge_q, edge_k, edge_v, k, v, edge_mixed,
    )
    parts = 4
    for part in range(parts):
        next(edges)
        close_inner(atoms2, mixed, out_weight, result, part, parts)
    for _ in edges:
        pass
    close_edge(atoms2, edge_mixed, out_weight, result)


def stay(x):
    return pltpu.with_memory_space_constraint(x, pltpu.HBM)


def call(kernel, outs, scratch, specs, flops, limit=20):
    return pl.pallas_call(
        kernel,
        out_shape=outs,
        in_specs=specs,
        out_specs=jax.tree.map(lambda _: VMEM, outs),
        scratch_shapes=scratch,
        compiler_params=pltpu.CompilerParams(vmem_limit_bytes=limit * 1024 * 1024),
        cost_estimate=pl.CostEstimate(flops=flops, bytes_accessed=1_000, transcendentals=1_000),
    )


def body(
    atom_acts, first_gain, first_qkv, first_out, second_gain, second_qkv, second_out, atom_bias, window_start,
    atom_token, up_weight, token_gain, token_weight, token_out, down_weight, pair_bias,
):
    rows, channels = atom_acts.shape
    heads, tok_rows, slots = pair_bias.shape
    wide = token_weight.shape[0]
    row_count, col_count = lax.axis_size("row"), lax.axis_size("col")
    pairs = col_count // 2
    share = tok_rows // col_count
    half = tok_rows // 2
    row, col = lax.axis_index("row"), lax.axis_index("col")
    side, pair = col % 2, col // 2
    info = jnp.stack([side, row, pair, col, (row * col_count + col) * rows]).astype(jnp.int32)
    devices = row_count * col_count
    group_count = lax.axis_size("group")

    def to_near(x):
        return lax.ppermute(x, "col", [(i, i ^ 1) for i in range(col_count)])

    def swapped(x, swap):
        pairs_list = []
        for i in range(group_count * devices):
            group_at, at = divmod(i, devices)
            if at in swap:
                target = group_at * devices + swap[at]
            else:
                target = (group_at ^ 1) * devices + at if group_count % 2 == 0 else i
            pairs_list.append((i, target))
        return lax.ppermute(x, ("group", "row", "col"), pairs_list)

    def to_far(x):
        return swapped(x, {i: i + 1 if i % 2 else i - 1 for i in range(1, devices - 1)})

    def to_beyond(x):
        swap = {}
        for i in range(1, row_count):
            first, last = i * col_count, i * col_count - 1
            for one, other in ((first, first - col_count + 1), (last, last + col_count - 1)):
                swap[one], swap[other] = other, one
        if col_count > 4:
            for i in range(devices):
                if 2 <= i % col_count < col_count - 2:
                    swap[i] = i ^ 1
        return swapped(x, swap)

    def along_pairs(x, step):
        return lax.ppermute(
            x, "col", [(2 * i + k, 2 * ((i + step) % pairs) + k) for i in range(pairs) for k in range(2)]
        )

    def along_rows(x, step):
        return lax.ppermute(x, "row", [(i, i ^ step) for i in range(row_count)])

    def rim_of(x, last):
        return lax.dynamic_slice_in_dim(x, jnp.where(last, rows - RIM, 0), RIM, axis=0)

    near_acts = to_near(rim_of(atom_acts, side == 0))
    far_acts = to_far(rim_of(atom_acts, side == 1))

    ids = atom_token.reshape(1, rows)
    inner_scratch = [
        pltpu.VMEM((rows, channels), BF),
        pltpu.VMEM((rows, channels), F32),
        pltpu.VMEM((rows, channels), F32),
    ]
    edge_scratch = [
        pltpu.VMEM((6 * RIM, channels), F32),
        pltpu.VMEM((6 * RIM, channels), F32),
        pltpu.VMEM((2 * RIM, channels), BF),
    ]
    atom_shape = jax.ShapeDtypeStruct((rows, channels), BF)
    edge_shapes = [
        jax.ShapeDtypeStruct((2 * RIM, channels), BF),
        jax.ShapeDtypeStruct((4 * RIM, channels), F32),
        jax.ShapeDtypeStruct((4 * RIM, channels), F32),
    ]
    packed_shape = jax.ShapeDtypeStruct((half, wide + LANES), BF)
    first_gain, second_gain = first_gain.reshape(1, -1), second_gain.reshape(1, -1)
    pieces = 2
    windows = window_start.shape[0]
    edge = RIM * windows // rows
    groups = (windows - 2 * edge) // window_group(windows, edge)
    first_args = [atom_acts, first_gain, first_qkv]
    mixed1 = call(
        functools.partial(first_inner, pieces=pieces),
        [atom_shape] + edge_shapes + [jax.ShapeDtypeStruct((atom_bias.shape[0], 2 * RIM, atom_bias.shape[2]), BF)],
        inner_scratch
        + [pltpu.VMEM(x.shape, x.dtype) for x in first_args]
        + [pltpu.SMEM(window_start.shape, jnp.int32), pltpu.VMEM(atom_bias.shape, BF)]
        + [pltpu.SemaphoreType.DMA((5 + pieces,)), pltpu.SemaphoreType.DMA((groups,))],
        [SMEM] + [HBM] * 5,
        1_500_000_000,
        16,
    )(info, *map(stay, first_args), stay(window_start), stay(atom_bias))
    message_shape = jax.ShapeDtypeStruct((RIM + 16, channels), BF)
    atoms1, send, keep, near_message, far_message = call(
        functools.partial(first_edge, share=share),
        [atom_shape, packed_shape, packed_shape, message_shape, message_shape],
        edge_scratch,
        [SMEM, SMEM] + [VMEM] * 13,
        2_000_000_000,
        16,
    )(
        info, window_start, ids, atom_acts, near_acts, far_acts, first_gain, first_qkv, first_out,
        up_weight, *mixed1,
    )

    chip_sum = (keep.astype(F32) + to_near(send).astype(F32)).astype(BF)
    chip_sum, near_bias, near_message, far_message = lax.optimization_barrier(
        (chip_sum, pair_bias, near_message, far_message)
    )
    bias_near = to_near(near_bias)
    sums = [lax.dynamic_slice_in_dim(chip_sum, pair * share, share, axis=0)]
    for step in range(1, pairs):
        piece = lax.dynamic_slice_in_dim(chip_sum, (pair + step) % pairs * share, share, axis=0)
        sums.append(along_pairs(piece, step))
    near_message, far_message = to_near(near_message), to_far(far_message)
    sums, bias_near, near_message, far_message = lax.optimization_barrier(
        (sums, bias_near, near_message, far_message)
    )
    share_shape = jax.ShapeDtypeStruct((share, wide), BF)
    gain_row = token_gain.reshape(1, -1)
    act, normed = call(
        functools.partial(mean_tokens, count=len(sums)), [share_shape] * 2, [], [VMEM] * (len(sums) + 1), 1_000_000
    )(*sums, gain_row)

    group = LANES // share
    solo = group == 2
    split = 1 if solo else group
    own_keys = [normed] + [along_rows(normed, step) for step in range(1, row_count)]
    near_keys = [to_near(x) for x in own_keys[:split]]
    other_acts = [along_pairs(act, step) for step in range(1, pairs)]
    half_shape = jax.ShapeDtypeStruct((half, wide), BF)
    wide_shape = jax.ShapeDtypeStruct((half, wide), F32)
    rest = row_count - split

    def key_scratch(count):
        return [pltpu.VMEM((2 * count * share, wide), BF)] * 3

    head_shape = jax.ShapeDtypeStruct((heads, half, LANES), F32)
    weight_shape = jax.ShapeDtypeStruct((wide, wide), BF)
    tile_count = 2 * pairs
    blocks = row_count // group - 1
    act_rows, queries, gates, *held, mixed, tops, totals = call(
        functools.partial(attend_first, others=len(other_acts), steps=list(range(split)), solo=solo),
        [half_shape, half_shape, wide_shape, weight_shape, weight_shape]
        + [jax.ShapeDtypeStruct((heads, half, LANES), BF), jax.ShapeDtypeStruct((heads, half, 2 * LANES * blocks), BF)]
        + [wide_shape, head_shape, head_shape],
        [pltpu.VMEM((wide, wide), BF)] * 2
        + key_scratch(split)
        + [pltpu.VMEM((heads, half, 2 * split * share), BF), pltpu.VMEM((2, heads, half, LANES), BF)]
        + [pltpu.SemaphoreType.DMA((4 + tile_count * (blocks + 1),))],
        [SMEM, HBM, VMEM, VMEM, HBM, HBM] + [VMEM] * (len(other_acts) + 2 * split),
        1_000,
        24,
    )(
        info, stay(token_weight), gain_row, act, stay(pair_bias), stay(bias_near), *other_acts,
        *own_keys[:split], *near_keys,
    )
    rest_steps = sorted(range(split, row_count), key=lambda step: (step < group, step))
    rest_keys, mixed = lax.optimization_barrier(([own_keys[step] for step in rest_steps], mixed))
    rest_near = [to_near(x) for x in rest_keys]
    halves = 2
    some = wide // halves
    key_rows = jax.ShapeDtypeStruct((2 * rest * share, wide), BF)
    rest_scratch = [pltpu.VMEM((2 * rest * share, some), BF)] * 2
    part_shape = jax.ShapeDtypeStruct((half, some + LANES), BF)
    rest_args = [info, queries, *held, mixed, tops, totals]
    early_part, key_rows = call(
        functools.partial(attend_rest, steps=rest_steps, solo=solo, part=0, parts=halves),
        [part_shape, key_rows],
        rest_scratch,
        [SMEM] + [VMEM] * (8 + 2 * rest),
        2_000_000_000,
    )(*rest_args, *rest_keys, *rest_near)
    late_part = call(
        functools.partial(attend_rest, steps=rest_steps, solo=solo, part=1, parts=halves),
        part_shape,
        rest_scratch,
        [SMEM] + [VMEM] * 9,
        2_000_000_000,
    )(*rest_args, key_rows)
    early_parts = [along_pairs(early_part, step) for step in range(1, pairs)]
    late_parts = [along_pairs(late_part, step) for step in range(1, pairs)]
    def finish(so_far, part, pieces, out):
        return call(
            functools.partial(finish_part, heads=heads // halves, size=wide // heads, part=part),
            out,
            [],
            [VMEM] * (4 + pairs),
            200_000_000,
        )(so_far, gates, token_out, *pieces, down_weight)

    result = finish(act_rows, 0, [early_part] + early_parts, wide_shape)
    own_back = finish(result, 1, [late_part] + late_parts, jax.ShapeDtypeStruct((half, channels), BF))

    near_back = to_near(own_back)
    if share >= RIM:
        last_rows = own_back[half - RIM :]
        first_rows = own_back[:RIM]
    else:
        both = jnp.where(side == 0, jnp.stack([own_back, near_back]), jnp.stack([near_back, own_back]))
        both = both.reshape(2, pairs, share, channels).transpose(1, 0, 2, 3).reshape(tok_rows, channels)
        last_rows = both[tok_rows - RIM :]
        first_rows = both[:RIM]
    far_back = to_beyond(jnp.where(side == 1, last_rows, first_rows))

    atoms2, *mixed2 = call(
        functools.partial(second_inner, share=share),
        [atom_shape, atom_shape] + edge_shapes,
        inner_scratch,
        [SMEM, SMEM] + [VMEM] * 7,
        1_500_000_000,
        16,
    )(info, window_start, ids, atoms1, own_back, near_back, second_gain, second_qkv, atom_bias)
    return call(
        functools.partial(second_edge, share=share, columns=col_count),
        atom_shape,
        edge_scratch + [pltpu.VMEM((atom_bias.shape[0], 2 * RIM, atom_bias.shape[2]), BF)],
        [SMEM, SMEM] + [VMEM] * 14,
        300_000_000,
        16,
    )(
        info, window_start, atoms2, near_message, far_message, own_back, near_back, far_back,
        second_gain, second_qkv, second_out, atom_bias, *mixed2,
    )


def solution(mesh):
    atoms = P(("group", "row", "col"))
    in_specs = (
        P(("group", "row", "col"), None),
        P(), P(), P(), P(), P(), P(),
        P(None, ("group", "row", "col"), None),
        atoms,
        atoms,
        P(), P(), P(), P(), P(),
        P(None, ("group", "row"), "col"),
    )
    out_specs = P(("group", "row", "col"), None)
    return jax.shard_map(body, mesh=mesh, in_specs=in_specs, out_specs=out_specs, check_vma=False)
```
